32 devices in a mesh: req: 4 (over x, core), exp: 8 (over z, y).
Axes of the slice: x: 2, y: 2, z: 4, core: 2. Of those that a mesh axis runs over, the one named last changes fastest.
Arguments:
- queries: bfloat16 [4096, 2048], P('req', 'exp'), may hold values from -6 to 6
- keys: bfloat16 [4096, 2048], P('req', 'exp'), may hold values from -15 to 15
- values: bfloat16 [4096, 2048], P('req', 'exp'), may hold values from -6 to 6
- prefix_keys: bfloat16 [4, 4096, 2048], P(None, 'req', 'exp'), may hold values from -15 to 15
- prefix_values: bfloat16 [4, 4096, 2048], P(None, 'req', 'exp'), may hold values from -6 to 6
- lengths: int32 [4, 8], P('req'), may hold values from 1 to 512, 1024 in all within a row
- groups: int32 [4, 8], P('req'), may hold values from 0 to 3
- residual: bfloat16 [4096, 2048], P(('req', 'exp')), may hold values from -6 to 6
- out_proj: bfloat16 [2048, 2048], P('exp'), may hold values from -0.125 to 0.125
- norm_gain: bfloat16 [2048], replicated, may hold values from 0.099609375 to 1.8984375
- expert_ids: int32 [4096, 4], P(('req', 'exp')), may hold values from 0 to 31, all different within a row; in each aligned block of 128 rows (0 to 127, 128 to 255, ...) at most 32 rows name the same one
- expert_gates: bfloat16 [4096, 4], P(('req', 'exp')), may hold values from 0.049804688 to 0.5
- w_gate: bfloat16 [32, 2048, 704], P('exp'), may hold values from -0.125 to 0.125
- w_up: bfloat16 [32, 2048, 704], P('exp'), may hold values from -0.125 to 0.125
- w_down: bfloat16 [32, 704, 2048], P('exp'), may hold values from -0.21875 to 0.21875
Outputs:
- layer_out: bfloat16 [4096, 2048], P(('req', 'exp'))
The draws below stay inside these ranges and needn't reach their ends.
Inputs may be any that keep to these rules, and one draw needn't show every extreme that they name: The 8 lengths of a row sum to 1024; the longest request of each row has half of 1024 tokens. `expert_ids`: each row names 4 different experts. Among the 128 tokens of one device, no expert is named more than 32 times; on some device some expert is named exactly 32 times.
All inputs are finite; a program needn't handle non-finite values.
Results may differ from the reference program's by a relative error of at most 0.02.
Values may be sent and summed in bfloat16 or wider, within the bound.
No kernel may reach another device: no remote copies, remote signals or barrier semaphores. Data moves between devices by JAX's collectives and lax.ppermute only.
A program may use at most 256 MiB of HBM per device.

```python
import math
import jax
import jax.numpy as jnp
import numpy as np
from jax import lax

D = 2048
HEADS = 16
HEAD = 128
TOPK = 4
EXPERTS = 32
FE = 704
G = 4
RQ = 8
PREF = 4096
ROW_TOK = 1024
TOKENS = 4096
TOK_DEV = 128
CAP = 32
N_REQ = 4


def draw_queries(key, part):
    drawn = jnp.clip(jax.random.normal(jax.random.fold_in(key, 11), (TOKENS, D), jnp.float32), -5.5, 5.5)
    return drawn.astype(jnp.bfloat16)


def draw_prefix_keys(key, part):
    drawn = jnp.clip(2.5 * jax.random.normal(jax.random.fold_in(key, 23), (G, PREF, D), jnp.float32), -15.0, 15.0)
    return drawn.astype(jnp.bfloat16)


def set_ends(result, own_key, smallest, largest):
    longest = result.shape.index(max(result.shape))
    spots = []
    for shift in (0, 1):
        where = [jax.random.randint(jax.random.fold_in(own_key, axis), (), 0, length) for axis, length in enumerate(result.shape)]
        where[longest] = (where[longest] + shift) % result.shape[longest]
        spots.append(tuple(where))
    return result.at[spots[0]].set(smallest).at[spots[1]].set(largest)


def shard_levels(key, dims, pieces, smallest, high):
    factor_of, own = 1.0, jax.random.fold_in(key, 6)
    for dim, blocks in pieces:
        steps = jnp.exp(jax.random.uniform(jax.random.fold_in(own, dim), (blocks,), jnp.float32, smallest / len(pieces), high / len(pieces)))
        factor_of = factor_of * jnp.repeat(steps, dims[dim] // blocks).reshape([-1 if axis == dim else 1 for axis in range(len(dims))])
    return factor_of


def split_up(amount, total, reach, skew):
    weights = [(1 << 20) // math.isqrt(standing ** skew) + 1 for standing in range(2, amount + 1)]
    rest, given = total - reach - (amount - 1), [1] * (amount - 1)
    while rest > 0:
        candidates = [i for i in range(amount - 1) if given[i] < reach]
        pool, budget = sum([weights[i] for i in candidates]), rest
        for i in candidates:
            extra = min(reach - given[i], max(1, budget * weights[i] // pool), rest)
            given[i] = given[i] + extra
            rest = rest - extra
    return np.array([reach] + given)


def ragged_sizes(rng, amount, total, bound, lean):
    if amount == 2:
        one = jax.random.randint(rng, (), max(1, total - bound), min(bound, total - 1) + 1)
        return jnp.stack([one, total - one])
    tallies = jnp.asarray(split_up(amount, total, bound, lean), jnp.int32)
    couples = (amount - 1) // 2
    giver, taker = tallies[1:1 + 2 * couples:2], tallies[2:2 + 2 * couples:2]
    slack = jnp.minimum(giver - 1, bound - taker)
    shifted = jax.random.randint(jax.random.fold_in(rng, 1), (couples,), 0, 1 << 20) % (slack + 1)
    tallies = tallies.at[1:1 + 2 * couples:2].set(giver - shifted).at[2:2 + 2 * couples:2].set(taker + shifted)
    return tallies[jax.random.permutation(jax.random.fold_in(rng, 2), amount)]


def shared_out(rng, own, number, rows, number_of, top, limit, slope):
    order = jax.random.permutation(rng, number_of)
    heavy_load, usual = load_shares(number_of, rows * top, limit, slope, True), load_shares(number_of, rows * top, limit, slope, False)
    places = jnp.arange(number_of)

    def named(sizes, rotation):
        used = int((sizes > 0).sum())
        fixed = max(1, used // 4)
        moved = fixed + (places - fixed + rotation * (used - fixed)) % max(1, number_of - fixed)
        return jnp.zeros((number_of,), jnp.int32).at[order[jnp.where(places < fixed, places, moved)]].set(jnp.asarray(sizes, jnp.int32))

    sizes = jnp.where(number % 4 == 0, named(heavy_load, number // 4), named(usual, number - number // 4 - 1))
    mixed = jax.random.permutation(jax.random.fold_in(own, 3), number_of)
    donor, taker = mixed[0:number_of // 2 * 2:2], mixed[1:number_of // 2 * 2:2]
    margin = jnp.minimum(sizes[donor] - 1, limit - sizes[taker]) // 2
    margin = jnp.where((donor == order[0]) | (taker == order[0]) | (sizes[taker] == 0), 0, jnp.maximum(margin, 0))
    moved = jax.random.randint(jax.random.fold_in(own, 4), (number_of // 2,), 0, 1 << 20) % (margin + 1)
    sizes = sizes.at[donor].add(-moved).at[taker].add(moved)
    members = jnp.searchsorted(jnp.cumsum(sizes), jnp.arange(rows * top), side="right").astype(jnp.int32)
    table = members.reshape(top, rows).T
    table = table[jax.random.permutation(jax.random.fold_in(own, 1), rows)]
    rotation = jax.random.randint(jax.random.fold_in(own, 2), (rows, 1), 0, top)
    return jnp.take_along_axis(table, (jnp.arange(top)[None, :] + rotation) % top, axis=1)


def load_shares(number_of, total, bound, slope, full):
    portions = [(1 << 20) // math.isqrt(grade ** slope) + 1 for grade in range(1, number_of + 1)]
    largest = bound if full else min(bound, max(-(-total // number_of), total * portions[0] // sum(portions)))
    least = 1 if total - largest >= number_of - 1 else 0
    holding, spare = [largest] + [least] * (number_of - 1), total - largest - least * (number_of - 1)
    while spare > 0:
        movable = [i for i in range(1, number_of) if holding[i] < largest] or [i for i in range(1, number_of) if holding[i] < bound]
        whole, left = sum([portions[i] for i in movable]), spare
        for i in movable:
            more = min(bound - holding[i], max(1, left * portions[i] // whole), spare)
            holding[i] = holding[i] + more
            spare = spare - more
    return np.array(holding)


def noise(stream_key, dims, spread, reach, cuts=(), kind=jnp.bfloat16):
    loudness = shard_levels(stream_key, dims, cuts, -0.22, 0.18) if cuts else 1.0
    values = jax.random.normal(stream_key, dims, jnp.float32) * spread * loudness
    return jnp.minimum(jnp.maximum(values, -reach), reach).astype(kind)


def setup_inputs(seed: int = 0) -> dict:
    key_list = jax.random.split(jax.random.key(seed), 16)
    queries = draw_queries(jax.random.fold_in(key_list[15], 71), 0)
    keys = noise(key_list[1], (TOKENS, D), 2.5, 15.0, ((0, 4), (1, 8)))
    values = noise(key_list[2], (TOKENS, D), 1.0, 6.0, ((0, 4), (1, 8)))
    prefix_keys = draw_prefix_keys(jax.random.fold_in(key_list[15], 71), 0)
    prefix_values = noise(key_list[4], (G, PREF, D), 1.0, 6.0, ((1, 4), (2, 8)))
    lengths = jax.vmap(lambda own: ragged_sizes(own, RQ, ROW_TOK, ROW_TOK // 2, 2))(jax.random.split(key_list[5], N_REQ)).reshape((N_REQ, RQ)).astype(jnp.int32)
    groups = set_ends(jax.random.randint(key_list[6], (N_REQ, RQ), 0, G), jax.random.fold_in(key_list[6], 1), 0, G - 1).astype(jnp.int32)
    residual = noise(key_list[7], (TOKENS, D), 1.0, 6.0, ((0, 32),))
    out_proj = noise(key_list[8], (D, D), D ** -0.5, 0.125, ((0, 8),))
    norm_gain = jnp.clip(1.0 + 0.18 * jax.random.normal(key_list[9], (D,), jnp.float32), 0.099609375, 1.8984375).astype(jnp.bfloat16)
    expert_ids_keys = jax.random.split(jax.random.fold_in(key_list[10], 1), TOKENS // TOK_DEV)
    expert_ids_turns = jax.random.permutation(jax.random.fold_in(key_list[10], 3), TOKENS // TOK_DEV)
    expert_ids = jax.vmap(lambda own, number: shared_out(jax.random.fold_in(key_list[10], 2), own, number, TOK_DEV, EXPERTS, TOPK, CAP, 2))(expert_ids_keys, expert_ids_turns).reshape((TOKENS, TOPK))
    expert_gates = jnp.clip(0.049804688 + 0.4501953 * jax.random.uniform(key_list[11], (TOKENS, TOPK), jnp.float32) ** shard_levels(key_list[11], (TOKENS, TOPK), ((0, 32),), -0.2, 0.2), 0.049804688, 0.5).astype(jnp.bfloat16)
    w_gate = noise(key_list[12], (EXPERTS, D, FE), D ** -0.5, 0.125, ((0, 8),))
    w_up = noise(key_list[13], (EXPERTS, D, FE), D ** -0.5, 0.125, ((0, 8),))
    w_down = noise(key_list[14], (EXPERTS, FE, D), FE ** -0.5, 0.21875, ((0, 8),))
    return dict(queries=queries, keys=keys, values=values, prefix_keys=prefix_keys, prefix_values=prefix_values, lengths=lengths, groups=groups, residual=residual, out_proj=out_proj, norm_gain=norm_gain, expert_ids=expert_ids, expert_gates=expert_gates, w_gate=w_gate, w_up=w_up, w_down=w_down)


NEG = -1e+30

def token_layout(lengths, groups):
    req_ends = jnp.cumsum(lengths, axis=-1)
    starts = req_ends - lengths
    position = jnp.arange(ROW_TOK, dtype=jnp.int32)
    request = lax.optimization_barrier(jnp.sum((position[None, :, None] >= req_ends[:, None, :]).astype(jnp.int32), axis=-1))
    onehot = request[:, :, None] == jnp.arange(RQ, dtype=jnp.int32)[None, None, :]
    first_tok = lax.optimization_barrier(jnp.sum(jnp.where(onehot, starts[:, None, :], 0), axis=-1))
    tok_group = lax.optimization_barrier(jnp.sum(jnp.where(onehot, groups[:, None, :], 0), axis=-1))
    return (request, position[None, :] - first_tok, tok_group)

def reference(queries, keys, values, prefix_keys, prefix_values, lengths, groups, residual, out_proj, norm_gain, expert_ids, expert_gates, w_gate, w_up, w_down):
    request, position, tok_group = token_layout(lengths, groups)
    scaling = 1.0 / math.sqrt(HEAD)
    block_len = min(128, ROW_TOK)
    per_row = ROW_TOK // block_len
    key_grid = prefix_keys.astype(jnp.float32).reshape(G, PREF, HEADS, HEAD)
    val_grid = prefix_values.astype(jnp.float32).reshape(G, PREF, HEADS, HEAD)

    def per_block(block_id):
        row_id = block_id // per_row
        offset = block_id % per_row * block_len
        query_grid = lax.dynamic_slice_in_dim(queries, block_id * block_len, block_len, 0).astype(jnp.float32).reshape(block_len, HEADS, HEAD)
        row_keys = lax.dynamic_slice_in_dim(keys, row_id * ROW_TOK, ROW_TOK, 0).astype(jnp.float32).reshape(ROW_TOK, HEADS, HEAD)
        row_vals = lax.dynamic_slice_in_dim(values, row_id * ROW_TOK, ROW_TOK, 0).astype(jnp.float32).reshape(ROW_TOK, HEADS, HEAD)
        row_req = lax.dynamic_index_in_dim(request, row_id, 0, keepdims=False)
        row_pos = lax.dynamic_index_in_dim(position, row_id, 0, keepdims=False)
        row_grp = lax.dynamic_index_in_dim(tok_group, row_id, 0, keepdims=False)
        query_req = lax.dynamic_slice_in_dim(row_req, offset, block_len, 0)
        query_pos = lax.dynamic_slice_in_dim(row_pos, offset, block_len, 0)
        query_grp = lax.dynamic_slice_in_dim(row_grp, offset, block_len, 0)
        pre_scores = jnp.einsum('qhd,gkhd->qhgk', query_grid, key_grid) * scaling
        member = query_grp[:, None] == jnp.arange(G, dtype=jnp.int32)[None, :]
        pre_scores = jnp.where(member[:, None, :, None], pre_scores, NEG)
        suf_scores = jnp.einsum('qhd,khd->qhk', query_grid, row_keys) * scaling
        allowed = (row_req[None, :] == query_req[:, None]) & (row_pos[None, :] <= query_pos[:, None])
        suf_scores = jnp.where(allowed[:, None, :], suf_scores, NEG)
        maxima = jnp.maximum(lax.optimization_barrier(jnp.max(pre_scores, axis=(2, 3))), lax.optimization_barrier(jnp.max(suf_scores, axis=2)))
        pre_exp = jnp.exp(pre_scores - maxima[:, :, None, None])
        suf_exp = jnp.exp(suf_scores - maxima[:, :, None])
        totals = lax.optimization_barrier(jnp.sum(pre_exp, axis=(2, 3))) + lax.optimization_barrier(jnp.sum(suf_exp, axis=2))
        pre_probs = lax.optimization_barrier(pre_exp.astype(jnp.bfloat16)).astype(jnp.float32)
        suf_probs = lax.optimization_barrier(suf_exp.astype(jnp.bfloat16)).astype(jnp.float32)
        weighted = jnp.einsum('qhgk,gkhd->qhd', pre_probs, val_grid) + jnp.einsum('qhk,khd->qhd', suf_probs, row_vals)
        return (weighted / totals[:, :, None]).astype(jnp.bfloat16).reshape(block_len, D)
    attended = lax.map(per_block, jnp.arange(TOKENS // block_len, dtype=jnp.int32)).reshape(TOKENS, D)
    stream = residual.astype(jnp.float32) + jnp.dot(attended, out_proj, preferred_element_type=jnp.float32)
    meansq = lax.optimization_barrier(jnp.mean(stream * stream, axis=-1, keepdims=True))
    normed = (stream * lax.rsqrt(meansq + 1e-06) * norm_gain.astype(jnp.float32)).astype(jnp.bfloat16)
    flat_ids = expert_ids.reshape(-1)
    flat_gate = expert_gates.reshape(-1).astype(jnp.float32)
    most_rows = TOKENS // TOK_DEV * CAP

    def per_expert(summed, expert):
        chosen = flat_ids == expert
        where_rows = jnp.nonzero(chosen, size=most_rows, fill_value=0)[0]
        is_live = jnp.arange(most_rows) < jnp.sum(chosen.astype(jnp.int32))
        tok_rows = where_rows // TOPK
        inputs = normed[tok_rows]
        gate_h = jnp.dot(inputs, w_gate[expert], preferred_element_type=jnp.float32)
        up_h = jnp.dot(inputs, w_up[expert], preferred_element_type=jnp.float32)
        hidden = (jax.nn.silu(gate_h) * up_h).astype(jnp.bfloat16)
        expert_out = jnp.dot(hidden, w_down[expert], preferred_element_type=jnp.float32)
        weight = jnp.where(is_live, flat_gate[where_rows], 0.0)
        return (summed.at[tok_rows].add(expert_out * weight[:, None]), None)
    summed, unused = lax.scan(per_expert, jnp.zeros((TOKENS, D), jnp.float32), jnp.arange(EXPERTS, dtype=jnp.int32))
    return (stream + summed).astype(jnp.bfloat16)
```

```python
import math

import jax
import jax.numpy as jnp
from jax import lax
from jax.experimental import pallas as pl
from jax.experimental.pallas import tpu as pltpu
from jax.sharding import PartitionSpec as P

HEAD = 128
TOPK = 4
EXPERTS = 32
G = 4
RQ = 8
ROW_TOK = 1024


NEG = -1e30


def token_layout(lengths, groups):
    req_ends = jnp.cumsum(lengths, axis=-1)
    starts = req_ends - lengths
    position = jnp.arange(ROW_TOK, dtype=jnp.int32)
    request = jnp.sum((position[None, :, None] >= req_ends[:, None, :]).astype(jnp.int32), axis=-1)
    onehot = request[:, :, None] == jnp.arange(RQ, dtype=jnp.int32)[None, None, :]
    first_tok = jnp.sum(jnp.where(onehot, starts[:, None, :], 0), axis=-1)
    tok_group = jnp.sum(jnp.where(onehot, groups[:, None, :], 0), axis=-1)
    return (request, position[None, :] - first_tok, tok_group)


def split_blocks(row_count):
    if row_count % 1024 == 0 and row_count > 1024:
        return row_count // 1024
    return 1


def pack_parts(parts):
    return jnp.concatenate([parts[0], parts[1], parts[2]], axis=1)


def unpack_parts(packed, head_count):
    columns = head_count * HEAD
    return (
        packed[:, :columns],
        packed[:, columns : columns + head_count],
        packed[:, columns + head_count :],
    )


def attend_prefix(query_rows, query_group, prefix_k, prefix_v):
    row_count, columns = query_rows.shape
    head_count = columns // HEAD
    span = prefix_k.shape[1]
    key_grid = prefix_k.reshape(G, span, head_count, HEAD)
    val_grid = prefix_v.reshape(G, span, head_count, HEAD)
    blocks = split_blocks(row_count)
    block_len = row_count // blocks
    scaling = 1.0 / math.sqrt(HEAD)

    def per_block(pieces):
        block_q, block_g = pieces
        query_grid = block_q.reshape(block_len, head_count, HEAD)
        scores = (
            jnp.einsum("qhd,gkhd->hqgk", query_grid, key_grid, preferred_element_type=jnp.float32)
            * scaling
        )
        member = block_g[:, None] == jnp.arange(G, dtype=jnp.int32)[None, :]
        scores = jnp.where(member[None, :, :, None], scores, NEG)
        maxima = jnp.max(scores, axis=(2, 3))
        exp_terms = jnp.exp(scores - maxima[:, :, None, None])
        totals = jnp.sum(exp_terms, axis=(2, 3))
        weighted = jnp.einsum(
            "hqgk,gkhd->qhd",
            exp_terms.astype(jnp.bfloat16),
            val_grid,
            preferred_element_type=jnp.float32,
        )
        return (weighted.reshape(block_len, columns), maxima.T, totals.T)

    weighted, maxima, totals = lax.map(
        per_block,
        (query_rows.reshape(blocks, block_len, columns), query_group.reshape(blocks, block_len)),
    )
    return (
        weighted.reshape(row_count, columns),
        maxima.reshape(row_count, head_count),
        totals.reshape(row_count, head_count),
    )


def attend_suffix(queries, keys, values, request, position):
    row_count, columns = queries.shape
    head_count = columns // HEAD
    blocks = split_blocks(row_count)
    block_len = row_count // blocks
    scaling = 1.0 / math.sqrt(HEAD)
    key_grid = keys.reshape(row_count, head_count, HEAD)
    val_grid = values.reshape(row_count, head_count, HEAD)

    def per_block(pieces):
        block_q, block_req, block_pos = pieces
        query_grid = block_q.reshape(block_len, head_count, HEAD)
        scores = (
            jnp.einsum("qhd,khd->hqk", query_grid, key_grid, preferred_element_type=jnp.float32)
            * scaling
        )
        allowed = (request[None, :] == block_req[:, None]) & (
            position[None, :] <= block_pos[:, None]
        )
        scores = jnp.where(allowed[None, :, :], scores, NEG)
        maxima = jnp.max(scores, axis=2)
        exp_terms = jnp.exp(scores - maxima[:, :, None])
        totals = jnp.sum(exp_terms, axis=2)
        weighted = jnp.einsum(
            "hqk,khd->qhd",
            exp_terms.astype(jnp.bfloat16),
            val_grid,
            preferred_element_type=jnp.float32,
        )
        return (weighted.reshape(block_len, columns), maxima.T, totals.T)

    weighted, maxima, totals = lax.map(
        per_block,
        (
            queries.reshape(blocks, block_len, columns),
            request.reshape(blocks, block_len),
            position.reshape(blocks, block_len),
        ),
    )
    return (
        weighted.reshape(row_count, columns),
        maxima.reshape(row_count, head_count),
        totals.reshape(row_count, head_count),
    )


def combine(former, latter):
    weighted_a, maxima_a, totals_a = former
    weighted_b, maxima_b, totals_b = latter
    row_count, head_count = maxima_a.shape
    maxima = jnp.maximum(maxima_a, maxima_b)
    factor_a = jnp.exp(maxima_a - maxima)
    factor_b = jnp.exp(maxima_b - maxima)
    weighted = (
        weighted_a.reshape(row_count, head_count, HEAD) * factor_a[:, :, None]
        + weighted_b.reshape(row_count, head_count, HEAD) * factor_b[:, :, None]
    )
    return (
        weighted.reshape(row_count, head_count * HEAD),
        maxima,
        totals_a * factor_a + totals_b * factor_b,
    )


def general_device(
    queries,
    keys,
    values,
    prefix_keys,
    prefix_values,
    lengths,
    groups,
    residual,
    out_proj,
    norm_gain,
    expert_ids,
    expert_gates,
    w_gate,
    w_up,
    w_down,
):
    row_tok, columns = queries.shape
    head_count = columns // HEAD
    tok_dev = residual.shape[0]
    request, position, tok_group = token_layout(lengths, groups)
    request, position, tok_group = (request[0], position[0], tok_group[0])
    all_groups = lax.all_gather(tok_group, "req", axis=0, tiled=True)
    partial_value = pack_parts(
        attend_prefix(
            lax.all_gather(queries, "req", axis=0, tiled=True),
            all_groups,
            prefix_keys,
            prefix_values,
        )
    )
    returned = lax.all_to_all(partial_value, "req", split_axis=0, concat_axis=0, tiled=True)
    owners = returned.shape[0] // row_tok
    back_w, back_m, back_t = unpack_parts(returned, head_count)
    all_weighted = back_w.reshape(owners, row_tok, head_count, HEAD)
    all_maxima = back_m.reshape(owners, row_tok, head_count)
    all_totals = back_t.reshape(owners, row_tok, head_count)
    maxima = jnp.max(all_maxima, axis=0)
    factor = jnp.exp(all_maxima - maxima[None])
    weighted = jnp.sum(all_weighted * factor[..., None], axis=0).reshape(row_tok, columns)
    prefix_part = (weighted, maxima, jnp.sum(all_totals * factor, axis=0))
    suffix_part = attend_suffix(queries, keys, values, request, position)
    weighted, maxima, totals = combine(prefix_part, suffix_part)
    attended = (
        (weighted.reshape(row_tok, head_count, HEAD) / totals[:, :, None])
        .reshape(row_tok, columns)
        .astype(jnp.bfloat16)
    )
    projected = lax.psum_scatter(
        jnp.dot(attended, out_proj, preferred_element_type=jnp.float32),
        "exp",
        scatter_dimension=0,
        tiled=True,
    )
    stream = residual.astype(jnp.float32) + projected
    meansq = jnp.mean(stream * stream, axis=-1, keepdims=True)
    normed = (stream * lax.rsqrt(meansq + 1e-06) * norm_gain.astype(jnp.float32)).astype(
        jnp.bfloat16
    )
    capacity = max(2, tok_dev // 4)
    flat_ids = expert_ids.reshape(-1)
    onehot = (flat_ids[:, None] == jnp.arange(EXPERTS, dtype=jnp.int32)[None, :]).astype(jnp.int32)
    slot_of = jnp.sum(onehot * (jnp.cumsum(onehot, axis=0) - 1), axis=1)
    source_rows = jnp.arange(tok_dev * TOPK, dtype=jnp.int32) // TOPK
    buffer = (
        jnp.zeros((EXPERTS, capacity, normed.shape[1]), jnp.bfloat16)
        .at[flat_ids, slot_of]
        .set(normed[source_rows])
    )
    exp_count = lax.axis_size("exp")
    exp_dev = w_gate.shape[0]
    received = lax.all_to_all(buffer, "exp", split_axis=0, concat_axis=0, tiled=True)
    slots = received.shape[1]
    grid_in = received.reshape(exp_count, exp_dev, slots, received.shape[2])
    gate_h = jnp.einsum("secd,edf->secf", grid_in, w_gate, preferred_element_type=jnp.float32)
    up_h = jnp.einsum("secd,edf->secf", grid_in, w_up, preferred_element_type=jnp.float32)
    hidden = (jax.nn.silu(gate_h) * up_h).astype(jnp.bfloat16)
    expert_out = jnp.einsum("secf,efd->secd", hidden, w_down, preferred_element_type=jnp.float32)
    returned = lax.all_to_all(
        expert_out.reshape(EXPERTS, slots, received.shape[2]),
        "exp",
        split_axis=0,
        concat_axis=0,
        tiled=True,
    )
    gathered = returned[flat_ids, slot_of] * expert_gates.reshape(-1).astype(jnp.float32)[:, None]
    mixture = jnp.sum(gathered.reshape(tok_dev, TOPK, gathered.shape[1]), axis=1)
    return (stream + mixture).astype(jnp.bfloat16)


BLK = 128
LOG2E = 1.4426950408889634
SCORE_SCALE = LOG2E / math.sqrt(HEAD)
VMEM_BIG = 56 * 1024 * 1024


def core_swap(array):
    return lax.ppermute(array, "req", [(i, i ^ 1) for i in range(4)])


def x_swap(array):
    return lax.ppermute(array, "req", [(i, i ^ 2) for i in range(4)])


def y_swap(array):
    return lax.ppermute(array, "exp", [(i, i ^ 1) for i in range(8)])


def z_up(array, sources=3):
    return lax.ppermute(array, "exp", [(i, i + 2) for i in range(2 * sources)])


def z_down(array, sources=3):
    return lax.ppermute(array, "exp", [(i, i - 2) for i in range(8 - 2 * sources, 8)])


def row_meta(lengths, groups):
    ends = jnp.cumsum(lengths, axis=-1)
    starts = ends - lengths
    blocks = jnp.arange(ROW_TOK // BLK, dtype=jnp.int32)[None, :, None] * BLK
    overlap = (starts[:, None, :] < blocks + BLK) & (ends[:, None, :] > blocks)
    bits = jnp.zeros(overlap.shape[:2], jnp.int32)
    for g in range(G):
        present = jnp.any(overlap & (groups[:, None, :] == g), axis=-1)
        bits = bits + (present.astype(jnp.int32) << g)
    return jnp.concatenate([starts, groups, bits], axis=1)


def send_halves_kernel(sc_ref, q, k, v, pk, pv, out_qkv, out_pk, out_pv):
    out_qkv[0] = q[...]
    out_qkv[1] = k[...]
    out_qkv[2] = v[...]
    out_pk[...] = pk[...]
    out_pv[...] = pv[...]


def send_halves(core, q, k, v, pk, pv):
    rows, span = q.shape[0], pk.shape[1]
    part = rows // G
    token_in = pl.BlockSpec((part, HEAD), lambda i, s: (i, 1 - s[0]))
    prefix_in = pl.BlockSpec((1, span, HEAD), lambda i, s: (i, 0, 1 - s[0]))
    prefix_out = pl.BlockSpec((1, span, HEAD), lambda i, s: (i, 0, 0))
    return pl.pallas_call(
        send_halves_kernel,
        grid_spec=pltpu.PrefetchScalarGridSpec(
            num_scalar_prefetch=1,
            grid=(G,),
            in_specs=[token_in] * 3 + [prefix_in] * 2,
            out_specs=[
                pl.BlockSpec((3, part, HEAD), lambda i, s: (0, i, 0)),
                prefix_out,
                prefix_out,
            ],
        ),
        out_shape=(
            jax.ShapeDtypeStruct((3, rows, HEAD), q.dtype),
            jax.ShapeDtypeStruct((G, span, HEAD), q.dtype),
            jax.ShapeDtypeStruct((G, span, HEAD), q.dtype),
        ),
        name="send_halves",
    )(core, q, k, v, pk, pv)


def token_columns(meta_ref, row, first_token, count):
    token = first_token + lax.broadcasted_iota(jnp.int32, (count, 1), 0)
    group = jnp.full((count, 1), meta_ref[row, RQ], jnp.int32)
    first = jnp.zeros((count, 1), jnp.int32)
    for j in range(1, RQ):
        start = meta_ref[row, j]
        later = token >= start
        group = jnp.where(later, meta_ref[row, RQ + j], group)
        first = jnp.where(later, start, first)
    return token, group, first


def as_row(column):
    return jnp.transpose(jnp.broadcast_to(column, (BLK, BLK)))[0:1, :]


def prefix_kernel(meta_ref, sc_ref, q_ref, ka, kb, va, vb, o_ref, lse_ref):
    row, block = pl.program_id(0), pl.program_id(1)
    token, group, unused = token_columns(meta_ref, row, block * BLK, BLK)
    bits = meta_ref[row, 2 * RQ + block]
    contract = (((1,), (1,)), ((), ()))

    def attend(g, carry):
        @pl.when((bits >> g) & 1 == 1)
        def held():
            q = q_ref[0]
            sa = lax.dot_general(q, ka[g], contract, preferred_element_type=jnp.float32)
            sb = lax.dot_general(q, kb[g], contract, preferred_element_type=jnp.float32)
            top = jnp.maximum(
                jnp.max(sa, axis=1, keepdims=True), jnp.max(sb, axis=1, keepdims=True)
            )
            pa = jnp.exp2((sa - top) * SCORE_SCALE)
            pb = jnp.exp2((sb - top) * SCORE_SCALE)
            total = jnp.sum(pa, axis=1, keepdims=True) + jnp.sum(pb, axis=1, keepdims=True)
            out = jnp.dot(
                pa.astype(jnp.bfloat16), va[g], preferred_element_type=jnp.float32
            ) + jnp.dot(pb.astype(jnp.bfloat16), vb[g], preferred_element_type=jnp.float32)
            mine = group == g
            o_ref[0] = jnp.where(mine, out / total, o_ref[0].astype(jnp.float32)).astype(o_ref.dtype)
            lse = as_row(top * SCORE_SCALE + jnp.log2(total))
            mine_row = as_row(mine.astype(jnp.float32)) > 0.5
            here = pl.ds(block, 1)
            lse_ref[0, here, :] = jnp.where(mine_row, lse, lse_ref[0, here, :])

        return carry

    lax.fori_loop(0, G, attend, 0)


def prefix_attend(meta, core, q, pk, pk_other, pv, pv_other, out_dtype):
    rows, tokens, unused = q.shape
    span = pk.shape[1]
    own = pl.BlockSpec((G, span, HEAD), lambda r, b, m, s: (0, 0, s[0]))
    other = pl.BlockSpec((G, span, HEAD), lambda r, b, m, s: (0, 0, 0))
    blocks = tokens // BLK
    return pl.pallas_call(
        prefix_kernel,
        grid_spec=pltpu.PrefetchScalarGridSpec(
            num_scalar_prefetch=2,
            grid=(rows, blocks),
            in_specs=[
                pl.BlockSpec((1, BLK, HEAD), lambda r, b, m, s: (r, b, 0)),
                own,
                other,
                own,
                other,
            ],
            out_specs=[
                pl.BlockSpec((1, BLK, HEAD), lambda r, b, m, s: (r, b, 0)),
                pl.BlockSpec((1, blocks, BLK), lambda r, b, m, s: (r, 0, 0)),
            ],
        ),
        out_shape=(
            jax.ShapeDtypeStruct((rows, tokens, HEAD), out_dtype),
            jax.ShapeDtypeStruct((rows, blocks, BLK), jnp.float32),
        ),
        compiler_params=pltpu.CompilerParams(vmem_limit_bytes=VMEM_BIG),
        cost_estimate=pl.CostEstimate(
            flops=rows * tokens * span * HEAD * 8 * 4,
            bytes_accessed=4 * G * span * HEAD * 2,
            transcendentals=0,
        ),
        name="prefix_attend",
    )(meta, core, q, pk, pk_other, pv, pv_other)


SUF = 256


def suffix_kernel(meta_ref, q_ref, k_ref, v_ref, o_ref, lse_ref):
    row, block = pl.program_id(0), pl.program_id(1)
    for i in range(ROW_TOK // SUF):

        @pl.when(block == i)
        def held():
            width = (i + 1) * SUF
            token, unused, first = token_columns(meta_ref, row, i * SUF, SUF)
            s = lax.dot_general(
                q_ref[0],
                k_ref[0, :width, :],
                (((1,), (1,)), ((), ())),
                preferred_element_type=jnp.float32,
            )
            other = lax.broadcasted_iota(jnp.int32, (SUF, width), 1)
            s = jnp.where((other >= first) & (other <= token), s, NEG)
            top = jnp.max(s, axis=1, keepdims=True)
            p = jnp.exp2((s - top) * SCORE_SCALE)
            total = jnp.sum(p, axis=1, keepdims=True)
            out = jnp.dot(
                p.astype(jnp.bfloat16), v_ref[0, :width, :], preferred_element_type=jnp.float32
            )
            o_ref[0] = out / total
            lse = top * SCORE_SCALE + jnp.log2(total)
            for part in range(SUF // BLK):
                place = i * (SUF // BLK) + part
                lse_ref[0, place : place + 1, :] = as_row(lse[part * BLK : (part + 1) * BLK])


def suffix_attend(meta, q, k, v):
    rows, tokens, unused = q.shape
    whole = pl.BlockSpec((1, tokens, HEAD), lambda r, b, m: (r, 0, 0))
    blocks = tokens // BLK
    return pl.pallas_call(
        suffix_kernel,
        grid_spec=pltpu.PrefetchScalarGridSpec(
            num_scalar_prefetch=1,
            grid=(rows, tokens // SUF),
            in_specs=[pl.BlockSpec((1, SUF, HEAD), lambda r, b, m: (r, b, 0)), whole, whole],
            out_specs=[
                pl.BlockSpec((1, SUF, HEAD), lambda r, b, m: (r, b, 0)),
                pl.BlockSpec((1, blocks, BLK), lambda r, b, m: (r, 0, 0)),
            ],
        ),
        out_shape=(
            jax.ShapeDtypeStruct((rows, tokens, HEAD), jnp.float32),
            jax.ShapeDtypeStruct((rows, blocks, BLK), jnp.float32),
        ),
        compiler_params=pltpu.CompilerParams(vmem_limit_bytes=VMEM_BIG),
        cost_estimate=pl.CostEstimate(
            flops=rows * tokens * tokens * HEAD * 4 * 4, bytes_accessed=1 << 20, transcendentals=0
        ),
        name="suffix_attend",
    )(meta, q, k, v)


def merge_kernel(*refs):
    parts, out_ref = refs[:-1], refs[-1]
    block = pl.program_id(0)
    half = len(parts) // 2
    for row in range(2):
        sources = parts[row * half : (row + 1) * half]
        lses = [
            jnp.transpose(jnp.broadcast_to(lse[0, pl.ds(block, 1), :], (BLK, BLK)))
            for lse in sources[1::2]
        ]
        top = lses[0]
        for lse in lses[1:]:
            top = jnp.maximum(top, lse)
        weights = [jnp.exp2(lse - top) for lse in lses]
        total = weights[0]
        summed = weights[0] * sources[0][0].astype(jnp.float32)
        for weight, o in zip(weights[1:], sources[2::2]):
            total = total + weight
            summed = summed + weight * o[0].astype(jnp.float32)
        out_ref[0, row * BLK : (row + 1) * BLK, :] = (summed / total).astype(out_ref.dtype)


def merge_parts(parts):
    blocks = parts[0][0][0].shape[1] // BLK
    specs, operands = [], []
    for row in parts:
        for o, lse, index in row:
            operands += [o, lse]
            specs += [
                pl.BlockSpec((1, BLK, HEAD), lambda b, index=index: (index, b, 0)),
                pl.BlockSpec((1, blocks, BLK), lambda b, index=index: (index, 0, 0)),
            ]
    return pl.pallas_call(
        merge_kernel,
        grid=(blocks,),
        in_specs=specs,
        out_specs=pl.BlockSpec((1, 2 * BLK, HEAD), lambda b: (b, 0, 0)),
        out_shape=jax.ShapeDtypeStruct((blocks, 2 * BLK, HEAD), jnp.bfloat16),
        name="merge_parts",
    )(*operands)


def project_kernel(a_ref, w_ref, keep_ref, send_ref, lhs):
    @pl.when(pl.program_id(0) == 0)
    def first():
        for h in range(a_ref.shape[0]):
            lhs[:, h * HEAD : (h + 1) * HEAD] = a_ref[h]

    out = jnp.dot(lhs[...], w_ref[...], preferred_element_type=jnp.float32)
    rows = keep_ref.shape[0]
    keep_ref[...] = out[:rows]
    send_ref[...] = out[rows:].astype(send_ref.dtype)


def project(attended, weights):
    heads, tokens, unused = attended.shape
    depth, width = weights.shape
    rows, tile = tokens // 2, 512
    out_spec = pl.BlockSpec((rows, tile), lambda i: (0, i))
    return pl.pallas_call(
        project_kernel,
        grid=(width // tile,),
        in_specs=[
            pl.BlockSpec((heads, tokens, HEAD), lambda i: (0, 0, 0)),
            pl.BlockSpec((depth, tile), lambda i: (0, i)),
        ],
        out_specs=[out_spec, out_spec],
        out_shape=(
            jax.ShapeDtypeStruct((rows, width), jnp.float32),
            jax.ShapeDtypeStruct((rows, width), jnp.bfloat16),
        ),
        scratch_shapes=[pltpu.VMEM((tokens, depth), jnp.bfloat16)],
        name="project",
    )(attended, weights)


def norm_kernel(keep, got, residual, gain, stream_ref, normed_ref):
    stream = residual[...].astype(jnp.float32) + (keep[...] + got[...].astype(jnp.float32))
    meansq = jnp.mean(stream * stream, axis=-1, keepdims=True)
    stream_ref[...] = stream
    normed = stream * lax.rsqrt(meansq + 1e-06) * gain[...].astype(jnp.float32)
    normed_ref[...] = normed.astype(normed_ref.dtype)


def norm_rows(keep, got, residual, gain):
    return pl.pallas_call(
        norm_kernel,
        out_shape=(
            jax.ShapeDtypeStruct(keep.shape, jnp.float32),
            jax.ShapeDtypeStruct(keep.shape, jnp.bfloat16),
        ),
        name="norm_rows",
    )(keep, got, residual, gain.reshape(1, -1))


EXP_DEV = 4
CAP_ROWS = 256


def route_kernel(sc_ref, tab_ref, row_ref, col_ref, scr):
    for slot in range(8):
        tab = tab_ref[sc_ref[slot]].astype(jnp.float32)
        ids, gates = tab[:TOPK], tab[TOPK:]
        here = slice(slot * BLK, (slot + 1) * BLK)
        for j in range(EXP_DEV):
            chosen = ids == (sc_ref[8] + j).astype(jnp.float32)
            scr[j : j + 1, here] = jnp.sum(chosen.astype(jnp.float32), axis=0, keepdims=True)
            scr[EXP_DEV + j : EXP_DEV + j + 1, here] = jnp.sum(
                jnp.where(chosen, gates, 0.0), axis=0, keepdims=True
            )
    held = scr[...]
    count = held.shape[1]
    before = (
        lax.broadcasted_iota(jnp.int32, (count, count), 0)
        < lax.broadcasted_iota(jnp.int32, (count, count), 1)
    ).astype(jnp.bfloat16)
    places = jnp.dot(held.astype(jnp.bfloat16), before, preferred_element_type=jnp.float32)
    place_row = lax.broadcasted_iota(jnp.int32, held.shape, 0) < EXP_DEV
    chosen = jnp.concatenate([held[:EXP_DEV], held[:EXP_DEV]], axis=0) > 0.5
    table = jnp.where(place_row, jnp.where(chosen, places, -1.0), held)
    row_ref[...] = table
    for slot in range(8):
        here = slice(slot * BLK, (slot + 1) * BLK)
        tall = jnp.concatenate([table[:, here], jnp.zeros((BLK - 8, BLK), jnp.float32)], axis=0)
        col_ref[here, :] = jnp.transpose(tall)


def route(scalars, tab):
    tokens = tab.shape[0] * BLK
    return pl.pallas_call(
        route_kernel,
        in_specs=[
            pl.BlockSpec(memory_space=pltpu.SMEM),
            pl.BlockSpec(memory_space=pltpu.VMEM),
        ],
        out_shape=(
            jax.ShapeDtypeStruct((8, tokens), jnp.float32),
            jax.ShapeDtypeStruct((tokens, BLK), jnp.float32),
        ),
        scratch_shapes=[pltpu.VMEM((8, tokens), jnp.float32)],
        name="route",
    )(scalars, tab)


def experts_kernel(*refs):
    chunks = refs[:8]
    row_ref, col_ref, wg, wu, wd, out_ref, rows_in, rows_out, sems = refs[8:]
    expert = pl.program_id(0)
    tokens = rows_in.shape[0]

    @pl.when(expert == 0)
    def first():
        copies = [
            pltpu.make_async_copy(
                chunk, rows_in.at[i * BLK : (i + 1) * BLK, :], sems.at[i]
            )
            for i, chunk in enumerate(chunks)
        ]
        for copy in copies:
            copy.start()
        for copy in copies:
            copy.wait()

    places = row_ref[pl.ds(expert, 1), :]
    slots = lax.broadcasted_iota(jnp.int32, (CAP_ROWS, tokens), 0).astype(jnp.float32)
    pick = (slots == places).astype(jnp.bfloat16)
    picked = jnp.dot(pick, rows_in[...], preferred_element_type=jnp.float32).astype(jnp.bfloat16)
    contract = (((1,), (1,)), ((), ()))
    gate_h = lax.dot_general(picked, wg[0], contract, preferred_element_type=jnp.float32)
    up_h = lax.dot_general(picked, wu[0], contract, preferred_element_type=jnp.float32)
    hidden = (gate_h / (1.0 + jnp.exp(-gate_h)) * up_h).astype(jnp.bfloat16)
    out = jnp.dot(hidden, wd[0], preferred_element_type=jnp.float32)
    rows_out[pl.ds(pl.multiple_of(expert * CAP_ROWS, CAP_ROWS), CAP_ROWS), :] = out.astype(
        jnp.bfloat16
    )

    @pl.when(expert == EXP_DEV - 1)
    def last():
        def give(i, carry):
            here = pl.ds(pl.multiple_of(i * BLK, BLK), BLK)
            cols = col_ref[here, :]
            slot = lax.broadcasted_iota(jnp.int32, (BLK, CAP_ROWS), 1).astype(jnp.float32)
            weights = jnp.concatenate(
                [
                    jnp.where(
                        slot == cols[:, j : j + 1], cols[:, EXP_DEV + j : EXP_DEV + j + 1], 0.0
                    ).astype(jnp.bfloat16)
                    for j in range(EXP_DEV)
                ],
                axis=1,
            )
            out_ref[i] = jnp.dot(
                weights, rows_out[...], preferred_element_type=jnp.float32
            ).astype(out_ref.dtype)
            return carry

        lax.fori_loop(0, tokens // BLK, give, 0)


def run_experts(chunks, row_tab, col_tab, w_gate, w_up, w_down):
    width = chunks[0].shape[1]
    hidden = w_down.shape[1]
    tokens = len(chunks) * BLK
    once = pl.Buffered(1)
    return pl.pallas_call(
        experts_kernel,
        grid=(EXP_DEV,),
        in_specs=[pl.BlockSpec(memory_space=pl.ANY)] * 8
        + [
            pl.BlockSpec((8, tokens), lambda j: (0, 0)),
            pl.BlockSpec((tokens, BLK), lambda j: (0, 0)),
            pl.BlockSpec((1, hidden, width), lambda j: (j, 0, 0)),
            pl.BlockSpec((1, hidden, width), lambda j: (j, 0, 0)),
            pl.BlockSpec((1, hidden, width), lambda j: (j, 0, 0)),
        ],
        out_specs=pl.BlockSpec((8, BLK, width), lambda j: (0, 0, 0), pipeline_mode=once),
        out_shape=jax.ShapeDtypeStruct((8, BLK, width), jnp.bfloat16),
        scratch_shapes=[
            pltpu.VMEM((tokens, width), jnp.bfloat16),
            pltpu.VMEM((EXP_DEV * CAP_ROWS, width), jnp.bfloat16),
            pltpu.SemaphoreType.DMA((8,)),
        ],
        compiler_params=pltpu.CompilerParams(vmem_limit_bytes=VMEM_BIG),
        name="experts",
    )(*chunks, row_tab, col_tab, w_gate.transpose(0, 2, 1), w_up.transpose(0, 2, 1), w_down)


def pick_by_z(z, *choices):
    picked = choices[-1]
    for i in range(len(choices) - 2, -1, -1):
        if choices[i] is not picked:
            picked = jnp.where(z == i, choices[i], picked)
    return picked


SLOT_Z = ((0, 1, 2, 3), (1, 0, 2, 3), (2, 1, 3, 0), (3, 2, 1, 0))


def gather_rows(z, own):
    up, down = z_up(own), z_down(own)
    there = [y_swap(own)]
    first = pick_by_z(z, down, up, up, up)
    up2, down2 = z_up(up), z_down(down)
    there.append(y_swap(first))
    second = pick_by_z(z, down2, down, down, up2)
    up3, down3 = z_up(up2), z_down(down2)
    there.append(y_swap(second))
    third = pick_by_z(z, down3, down2, up2, up3)
    there.append(y_swap(third))
    return [own, first, second, third] + there


def scatter_sums(z, sums):
    def plus(a, b):
        return (a.astype(jnp.float32) + b.astype(jnp.float32)).astype(jnp.bfloat16)

    s3 = plus(sums[3], y_swap(sums[7]))
    up, down = z_up(s3, 1), z_down(s3, 1)
    s2 = plus(sums[2], y_swap(sums[6]))
    up = z_up(pick_by_z(z, s2, plus(s3, up), s2, s2), 2)
    down = z_down(pick_by_z(z, s2, s2, plus(s3, down), s2), 2)
    s1 = plus(sums[1], y_swap(sums[5]))
    up = z_up(pick_by_z(z, s1, plus(s2, up), plus(s2, up), s1), 3)
    down = z_down(pick_by_z(z, s1, plus(s1, down), plus(s1, down), s1), 3)
    s0 = (sums[0], y_swap(sums[4]))
    return [part.astype(jnp.float32) for part in (*s0, up, down)]


def tabled(values, index):
    return jnp.asarray(values, jnp.int32)[index]


def block_device(
    queries,
    keys,
    values,
    prefix_keys,
    prefix_values,
    lengths,
    groups,
    residual,
    out_proj,
    norm_gain,
    expert_ids,
    expert_gates,
    w_gate,
    w_up,
    w_down,
):
    row_tok = queries.shape[0]
    core = lax.rem(lax.axis_index("req"), 2)
    place = lax.axis_index("exp")
    z = place // 2
    core_arg = core.astype(jnp.int32).reshape(1)

    proj_rows = lax.dynamic_slice_in_dim(out_proj, core * HEAD, HEAD, 0)
    proj_rows = lax.all_gather(proj_rows, "exp", axis=0, tiled=True)

    shape = jnp.concatenate([lengths, groups], axis=1)
    shapes = jnp.concatenate([shape, core_swap(shape)], axis=0)
    shapes = jnp.concatenate([shapes, x_swap(shapes)], axis=0)
    meta = row_meta(shapes[:, :RQ], shapes[:, RQ:])

    qkv_theirs, pk_theirs, pv_theirs = send_halves(
        core_arg, queries, keys, values, prefix_keys, prefix_values
    )
    qkv_other = core_swap(qkv_theirs)
    pk_other, pv_other = core_swap(pk_theirs), core_swap(pv_theirs)

    def mine(array):
        return jnp.where(core == 0, array[:, :HEAD], array[:, HEAD:])

    q_two = jnp.stack([mine(queries), qkv_other[0]])
    k_two = jnp.stack([mine(keys), qkv_other[1]])
    v_two = jnp.stack([mine(values), qkv_other[2]])
    q_far = x_swap(q_two)

    tab = jnp.concatenate([expert_ids.T.astype(jnp.bfloat16), expert_gates.T], axis=0)[None]
    for step in (1, 2, 4):
        tab = jnp.concatenate(
            [tab, lax.ppermute(tab, "exp", [(i, i ^ step) for i in range(8)])], axis=0
        )
    slot_z = tabled(SLOT_Z, z)
    slot_place = jnp.concatenate(
        [slot_z * 2 + lax.rem(place, 2), slot_z * 2 + 1 - lax.rem(place, 2)]
    )
    scalars = jnp.concatenate([slot_place ^ place, (place * EXP_DEV).reshape(1)])
    row_tab, col_tab = route(scalars.astype(jnp.int32), tab)

    def prefix(q, rows, dtype):
        return prefix_attend(
            meta[rows], core_arg, q, prefix_keys, pk_other, prefix_values, pv_other, dtype
        )

    suffix = suffix_attend(meta[:2], q_two, k_two, v_two)
    near = prefix(q_two, slice(0, 2), jnp.float32)
    far = prefix(q_far, slice(2, 4), jnp.bfloat16)
    back = (x_swap(far[0]), x_swap(far[1]))
    attended = merge_parts(
        [[(*part, row) for part in (suffix, near, back)] for row in range(2)]
    )
    heads = lax.all_to_all(attended, "exp", split_axis=0, concat_axis=0, tiled=True)
    keep, send = project(heads, proj_rows)
    stream, normed = norm_rows(keep, core_swap(send), residual, norm_gain)
    rows = gather_rows(z, normed)
    sums = run_experts(rows, row_tab, col_tab, w_gate, w_up, w_down)
    parts = scatter_sums(z, sums)
    return (stream + sum(parts[1:], parts[0])).astype(jnp.bfloat16)


def solution(mesh):
    in_specs = (
        P("req", "exp"),
        P("req", "exp"),
        P("req", "exp"),
        P(None, "req", "exp"),
        P(None, "req", "exp"),
        P("req", None),
        P("req", None),
        P(("req", "exp"), None),
        P("exp", None),
        P(),
        P(("req", "exp"), None),
        P(("req", "exp"), None),
        P("exp", None, None),
        P("exp", None, None),
        P("exp", None, None),
    )
    out_specs = P(("req", "exp"), None)
    blocked = mesh.shape["req"] == 4 and mesh.shape["exp"] == 8
    return jax.shard_map(
        block_device if blocked else general_device,
        mesh=mesh, in_specs=in_specs, out_specs=out_specs, check_vma=False
    )
```

```python
import math

import jax
import jax.numpy as jnp
from jax import lax
from jax.experimental import pallas as pl
from jax.experimental.pallas import tpu as pltpu
from jax.sharding import PartitionSpec as P

HEAD = 128
TOPK = 4
EXPERTS = 32
G = 4
RQ = 8
ROW_TOK = 1024


NEG = -1e30


def token_layout(lengths, groups):
    req_ends = jnp.cumsum(lengths, axis=-1)
    starts = req_ends - lengths
    position = jnp.arange(ROW_TOK, dtype=jnp.int32)
    request = jnp.sum((position[None, :, None] >= req_ends[:, None, :]).astype(jnp.int32), axis=-1)
    onehot = request[:, :, None] == jnp.arange(RQ, dtype=jnp.int32)[None, None, :]
    first_tok = jnp.sum(jnp.where(onehot, starts[:, None, :], 0), axis=-1)
    tok_group = jnp.sum(jnp.where(onehot, groups[:, None, :], 0), axis=-1)
    return (request, position[None, :] - first_tok, tok_group)


def split_blocks(row_count):
    if row_count % 1024 == 0 and row_count > 1024:
        return row_count // 1024
    return 1


def pack_parts(parts):
    return jnp.concatenate([parts[0], parts[1], parts[2]], axis=1)


def unpack_parts(packed, head_count):
    columns = head_count * HEAD
    return (
        packed[:, :columns],
        packed[:, columns : columns + head_count],
        packed[:, columns + head_count :],
    )


def attend_prefix(query_rows, query_group, prefix_k, prefix_v):
    row_count, columns = query_rows.shape
    head_count = columns // HEAD
    span = prefix_k.shape[1]
    key_grid = prefix_k.reshape(G, span, head_count, HEAD)
    val_grid = prefix_v.reshape(G, span, head_count, HEAD)
    blocks = split_blocks(row_count)
    block_len = row_count // blocks
    scaling = 1.0 / math.sqrt(HEAD)

    def per_block(pieces):
        block_q, block_g = pieces
        query_grid = block_q.reshape(block_len, head_count, HEAD)
        scores = (
            jnp.einsum("qhd,gkhd->hqgk", query_grid, key_grid, preferred_element_type=jnp.float32)
            * scaling
        )
        member = block_g[:, None] == jnp.arange(G, dtype=jnp.int32)[None, :]
        scores = jnp.where(member[None, :, :, None], scores, NEG)
        maxima = jnp.max(scores, axis=(2, 3))
        exp_terms = jnp.exp(scores - maxima[:, :, None, None])
        totals = jnp.sum(exp_terms, axis=(2, 3))
        weighted = jnp.einsum(
            "hqgk,gkhd->qhd",
            exp_terms.astype(jnp.bfloat16),
            val_grid,
            preferred_element_type=jnp.float32,
        )
        return (weighted.reshape(block_len, columns), maxima.T, totals.T)

    weighted, maxima, totals = lax.map(
        per_block,
        (query_rows.reshape(blocks, block_len, columns), query_group.reshape(blocks, block_len)),
    )
    return (
        weighted.reshape(row_count, columns),
        maxima.reshape(row_count, head_count),
        totals.reshape(row_count, head_count),
    )


def attend_suffix(queries, keys, values, request, position):
    row_count, columns = queries.shape
    head_count = columns // HEAD
    blocks = split_blocks(row_count)
    block_len = row_count // blocks
    scaling = 1.0 / math.sqrt(HEAD)
    key_grid = keys.reshape(row_count, head_count, HEAD)
    val_grid = values.reshape(row_count, head_count, HEAD)

    def per_block(pieces):
        block_q, block_req, block_pos = pieces
        query_grid = block_q.reshape(block_len, head_count, HEAD)
        scores = (
            jnp.einsum("qhd,khd->hqk", query_grid, key_grid, preferred_element_type=jnp.float32)
            * scaling
        )
        allowed = (request[None, :] == block_req[:, None]) & (
            position[None, :] <= block_pos[:, None]
        )
        scores = jnp.where(allowed[None, :, :], scores, NEG)
        maxima = jnp.max(scores, axis=2)
        exp_terms = jnp.exp(scores - maxima[:, :, None])
        totals = jnp.sum(exp_terms, axis=2)
        weighted = jnp.einsum(
            "hqk,khd->qhd",
            exp_terms.astype(jnp.bfloat16),
            val_grid,
            preferred_element_type=jnp.float32,
        )
        return (weighted.reshape(block_len, columns), maxima.T, totals.T)

    weighted, maxima, totals = lax.map(
        per_block,
        (
            queries.reshape(blocks, block_len, columns),
            request.reshape(blocks, block_len),
            position.reshape(blocks, block_len),
        ),
    )
    return (
        weighted.reshape(row_count, columns),
        maxima.reshape(row_count, head_count),
        totals.reshape(row_count, head_count),
    )


def combine(former, latter):
    weighted_a, maxima_a, totals_a = former
    weighted_b, maxima_b, totals_b = latter
    row_count, head_count = maxima_a.shape
    maxima = jnp.maximum(maxima_a, maxima_b)
    factor_a = jnp.exp(maxima_a - maxima)
    factor_b = jnp.exp(maxima_b - maxima)
    weighted = (
        weighted_a.reshape(row_count, head_count, HEAD) * factor_a[:, :, None]
        + weighted_b.reshape(row_count, head_count, HEAD) * factor_b[:, :, None]
    )
    return (
        weighted.reshape(row_count, head_count * HEAD),
        maxima,
        totals_a * factor_a + totals_b * factor_b,
    )


def general_device(
    queries,
    keys,
    values,
    prefix_keys,
    prefix_values,
    lengths,
    groups,
    residual,
    out_proj,
    norm_gain,
    expert_ids,
    expert_gates,
    w_gate,
    w_up,
    w_down,
):
    row_tok, columns = queries.shape
    head_count = columns // HEAD
    tok_dev = residual.shape[0]
    request, position, tok_group = token_layout(lengths, groups)
    request, position, tok_group = (request[0], position[0], tok_group[0])
    all_groups = lax.all_gather(tok_group, "req", axis=0, tiled=True)
    partial_value = pack_parts(
        attend_prefix(
            lax.all_gather(queries, "req", axis=0, tiled=True),
            all_groups,
            prefix_keys,
            prefix_values,
        )
    )
    returned = lax.all_to_all(partial_value, "req", split_axis=0, concat_axis=0, tiled=True)
    owners = returned.shape[0] // row_tok
    back_w, back_m, back_t = unpack_parts(returned, head_count)
    all_weighted = back_w.reshape(owners, row_tok, head_count, HEAD)
    all_maxima = back_m.reshape(owners, row_tok, head_count)
    all_totals = back_t.reshape(owners, row_tok, head_count)
    maxima = jnp.max(all_maxima, axis=0)
    factor = jnp.exp(all_maxima - maxima[None])
    weighted = jnp.sum(all_weighted * factor[..., None], axis=0).reshape(row_tok, columns)
    prefix_part = (weighted, maxima, jnp.sum(all_totals * factor, axis=0))
    suffix_part = attend_suffix(queries, keys, values, request, position)
    weighted, maxima, totals = combine(prefix_part, suffix_part)
    attended = (
        (weighted.reshape(row_tok, head_count, HEAD) / totals[:, :, None])
        .reshape(row_tok, columns)
        .astype(jnp.bfloat16)
    )
    projected = lax.psum_scatter(
        jnp.dot(attended, out_proj, preferred_element_type=jnp.float32),
        "exp",
        scatter_dimension=0,
        tiled=True,
    )
    stream = residual.astype(jnp.float32) + projected
    meansq = jnp.mean(stream * stream, axis=-1, keepdims=True)
    normed = (stream * lax.rsqrt(meansq + 1e-06) * norm_gain.astype(jnp.float32)).astype(
        jnp.bfloat16
    )
    capacity = max(2, tok_dev // 4)
    flat_ids = expert_ids.reshape(-1)
    onehot = (flat_ids[:, None] == jnp.arange(EXPERTS, dtype=jnp.int32)[None, :]).astype(jnp.int32)
    slot_of = jnp.sum(onehot * (jnp.cumsum(onehot, axis=0) - 1), axis=1)
    source_rows = jnp.arange(tok_dev * TOPK, dtype=jnp.int32) // TOPK
    buffer = (
        jnp.zeros((EXPERTS, capacity, normed.shape[1]), jnp.bfloat16)
        .at[flat_ids, slot_of]
        .set(normed[source_rows])
    )
    exp_count = lax.axis_size("exp")
    exp_dev = w_gate.shape[0]
    received = lax.all_to_all(buffer, "exp", split_axis=0, concat_axis=0, tiled=True)
    slots = received.shape[1]
    grid_in = received.reshape(exp_count, exp_dev, slots, received.shape[2])
    gate_h = jnp.einsum("secd,edf->secf", grid_in, w_gate, preferred_element_type=jnp.float32)
    up_h = jnp.einsum("secd,edf->secf", grid_in, w_up, preferred_element_type=jnp.float32)
    hidden = (jax.nn.silu(gate_h) * up_h).astype(jnp.bfloat16)
    expert_out = jnp.einsum("secf,efd->secd", hidden, w_down, preferred_element_type=jnp.float32)
    returned = lax.all_to_all(
        expert_out.reshape(EXPERTS, slots, received.shape[2]),
        "exp",
        split_axis=0,
        concat_axis=0,
        tiled=True,
    )
    gathered = returned[flat_ids, slot_of] * expert_gates.reshape(-1).astype(jnp.float32)[:, None]
    mixture = jnp.sum(gathered.reshape(tok_dev, TOPK, gathered.shape[1]), axis=1)
    return (stream + mixture).astype(jnp.bfloat16)


BLK = 128
LOG2E = 1.4426950408889634
SCORE_SCALE = LOG2E / math.sqrt(HEAD)
VMEM_BIG = 56 * 1024 * 1024


def core_swap(array):
    return lax.ppermute(array, "req", [(i, i ^ 1) for i in range(4)])


def x_swap(array):
    return lax.ppermute(array, "req", [(i, i ^ 2) for i in range(4)])


def y_swap(array):
    return lax.ppermute(array, "exp", [(i, i ^ 1) for i in range(8)])


def z_up(array, sources=3):
    return lax.ppermute(array, "exp", [(i, i + 2) for i in range(2 * sources)])


def z_down(array, sources=3):
    return lax.ppermute(array, "exp", [(i, i - 2) for i in range(8 - 2 * sources, 8)])


def send_halves_kernel(sc_ref, q, k, v, pk, pv, out_qkv, out_pk, out_pv):
    out_qkv[0] = q[...]
    out_qkv[1] = k[...]
    out_qkv[2] = v[...]
    out_pk[...] = pk[...]
    out_pv[...] = pv[...]


def send_halves(core, q, k, v, pk, pv):
    rows, span = q.shape[0], pk.shape[1]
    part = rows // G
    token_in = pl.BlockSpec((part, HEAD), lambda i, s: (i, 1 - s[0]))
    prefix_in = pl.BlockSpec((1, span, HEAD), lambda i, s: (i, 0, 1 - s[0]))
    prefix_out = pl.BlockSpec((1, span, HEAD), lambda i, s: (i, 0, 0))
    return pl.pallas_call(
        send_halves_kernel,
        grid_spec=pltpu.PrefetchScalarGridSpec(
            num_scalar_prefetch=1,
            grid=(G,),
            in_specs=[token_in] * 3 + [prefix_in] * 2,
            out_specs=[
                pl.BlockSpec((3, part, HEAD), lambda i, s: (0, i, 0)),
                prefix_out,
                prefix_out,
            ],
        ),
        out_shape=(
            jax.ShapeDtypeStruct((3, rows, HEAD), q.dtype),
            jax.ShapeDtypeStruct((G, span, HEAD), q.dtype),
            jax.ShapeDtypeStruct((G, span, HEAD), q.dtype),
        ),
        name="send_halves",
    )(core, q, k, v, pk, pv)


def as_row(column):
    return jnp.transpose(jnp.broadcast_to(column, (BLK, BLK)))[0:1, :]


SUF = 256
SUB = 32
PER_ITEM = 8
ITEMS = 16


def prefix_work(lengths, groups):
    rows = lengths.shape[0]
    ends = jnp.cumsum(lengths, axis=-1)
    starts = ends - lengths
    blocks = rows * ROW_TOK // SUB
    at = (jnp.arange(ROW_TOK // SUB, dtype=jnp.int32) * SUB)[None, :, None]
    overlap = (starts[:, None, :] < at + SUB) & (ends[:, None, :] > at)
    of_group = groups[None, :, None, :] == jnp.arange(G, dtype=jnp.int32)[:, None, None, None]
    present = jnp.any(overlap[None] & of_group, axis=-1).reshape(G, blocks).astype(jnp.int32)
    items = (jnp.sum(present, axis=1) + PER_ITEM - 1) // PER_ITEM
    base = (jnp.cumsum(items) - items) * PER_ITEM
    slot = jnp.where(present > 0, base[:, None] + jnp.cumsum(present, axis=1) - 1, -1)
    value = jnp.arange(G * blocks, dtype=jnp.int32) + 1
    hit = slot.reshape(1, -1) == jnp.arange(ITEMS * PER_ITEM, dtype=jnp.int32)[:, None]
    held = jnp.sum(jnp.where(hit, value[None, :], 0), axis=1).reshape(ITEMS, PER_ITEM)
    held = jnp.where(held > 0, held, held[:, :1])
    held = (jnp.where(held > 0, held, held[:1, :1]) - 1).reshape(-1)
    return jnp.concatenate(
        [starts.reshape(-1), groups.reshape(-1), jnp.sum(items).reshape(1), held // blocks, held % blocks]
    )


def prefix_kernel(work_ref, q_ref, ka, kb, va, vb, o_ref, lse_ref, grp, lse, sa, sb, ta, tb):
    tokens = q_ref.shape[0]
    rows = tokens // ROW_TOK
    span = va.shape[1]
    head = 2 * rows * RQ
    for r in range(rows):
        token = lax.broadcasted_iota(jnp.int32, (ROW_TOK, HEAD), 0)
        group = jnp.full((ROW_TOK, HEAD), work_ref[(rows + r) * RQ], jnp.int32)
        for j in range(1, RQ):
            group = jnp.where(
                token >= work_ref[r * RQ + j], work_ref[(rows + r) * RQ + j], group
            )
        grp[r * ROW_TOK : (r + 1) * ROW_TOK, :] = group
    step = 512

    def places(item):
        at = head + 1 + ITEMS * PER_ITEM + item * PER_ITEM
        return [
            pl.ds(pl.multiple_of(work_ref[at + i] * SUB, SUB), SUB) for i in range(PER_ITEM)
        ]

    def group_of(item):
        return work_ref[head + 1 + item * PER_ITEM]

    def lanes(x, op):
        parts = [x[:, c : c + HEAD] for c in range(0, x.shape[1], HEAD)]
        while len(parts) > 1:
            parts = [op(a, b) for a, b in zip(parts[::2], parts[1::2])]
        return parts[0]

    def score(item, s, tops):
        g = group_of(item)
        q = jnp.concatenate([q_ref[place, :] for place in places(item)], axis=0)
        for half, k in enumerate((ka, kb)):
            for c in range(0, span, step):
                x = lax.dot_general(
                    q,
                    k[g, c : c + step, :],
                    (((1,), (1,)), ((), ())),
                    preferred_element_type=jnp.float32,
                )
                s[:, half * span + c : half * span + c + step] = x
                top = lanes(x, jnp.maximum)
                tops[...] = top if half == 0 and c == 0 else jnp.maximum(tops[...], top)

    def weigh(item, s, tops):
        g = group_of(item)
        where = places(item)
        for part in range(2):
            here = slice(part * BLK, (part + 1) * BLK)
            top = jnp.max(tops[here, :], axis=1, keepdims=True)
            out = jnp.zeros((BLK, HEAD), jnp.float32)
            total = jnp.zeros((BLK, HEAD), jnp.float32)
            for half, v in enumerate((va, vb)):
                for c in range(0, span, step):
                    x = s[here, half * span + c : half * span + c + step]
                    p = jnp.exp2((x - top) * SCORE_SCALE)
                    total = total + lanes(p, jnp.add)
                    out = out + jnp.dot(
                        p.astype(jnp.bfloat16),
                        v[g, c : c + step, :],
                        preferred_element_type=jnp.float32,
                    )
            total = jnp.sum(total, axis=1, keepdims=True)
            out = out * (1.0 / total)
            here_lse = jnp.broadcast_to(top * SCORE_SCALE + jnp.log2(total), (BLK, HEAD))
            for i in range(BLK // SUB):
                place = where[part * (BLK // SUB) + i]
                sub = slice(i * SUB, (i + 1) * SUB)
                mine = grp[place, :] == g
                o_ref[place, :] = jnp.where(
                    mine, out[sub], o_ref[place, :].astype(jnp.float32)
                ).astype(o_ref.dtype)
                lse[place, :] = jnp.where(mine, here_lse[sub], lse[place, :])

    count = work_ref[head]
    score(0, sa, ta)

    def pair(i, carry):
        second = jnp.minimum(2 * i + 1, ITEMS - 1)
        third = jnp.minimum(2 * i + 2, ITEMS - 1)
        score(second, sb, tb)
        weigh(2 * i, sa, ta)
        score(third, sa, ta)
        weigh(second, sb, tb)
        return carry

    lax.fori_loop(0, (count + 1) // 2, pair, 0)
    for b in range(tokens // BLK):
        lse_ref[b : b + 1, :] = jnp.transpose(lse[b * BLK : (b + 1) * BLK, :])[0:1, :]


def prefix_attend(work, core, q, pk, pk_other, pv, pv_other, out_dtype):
    tokens, unused = q.shape
    span = pv.shape[1]
    own = pl.BlockSpec((G, span, HEAD), lambda i, s: (0, 0, s[0]))
    whole = pl.BlockSpec((G, span, HEAD), lambda i, s: (0, 0, 0))
    blocks = tokens // BLK

    def body(core_ref, *refs):
        prefix_kernel(*refs)

    return pl.pallas_call(
        body,
        grid_spec=pltpu.PrefetchScalarGridSpec(
            num_scalar_prefetch=1,
            grid=(1,),
            in_specs=[
                pl.BlockSpec(memory_space=pltpu.SMEM),
                pl.BlockSpec((tokens, HEAD), lambda i, s: (0, 0)),
                own,
                whole,
                own,
                whole,
            ],
            out_specs=[
                pl.BlockSpec((tokens, HEAD), lambda i, s: (0, 0)),
                pl.BlockSpec((blocks, BLK), lambda i, s: (0, 0)),
            ],
            scratch_shapes=[
                pltpu.VMEM((tokens, HEAD), jnp.int32),
                pltpu.VMEM((tokens, HEAD), jnp.float32),
                pltpu.VMEM((PER_ITEM * SUB, 2 * span), jnp.float32),
                pltpu.VMEM((PER_ITEM * SUB, 2 * span), jnp.float32),
                pltpu.VMEM((PER_ITEM * SUB, HEAD), jnp.float32),
                pltpu.VMEM((PER_ITEM * SUB, HEAD), jnp.float32),
            ],
        ),
        out_shape=(
            jax.ShapeDtypeStruct((tokens, HEAD), out_dtype),
            jax.ShapeDtypeStruct((blocks, BLK), jnp.float32),
        ),
        compiler_params=pltpu.CompilerParams(vmem_limit_bytes=VMEM_BIG),
        cost_estimate=pl.CostEstimate(
            flops=tokens * span * HEAD * 8 * 4,
            bytes_accessed=4 * G * span * HEAD * 2,
            transcendentals=0,
        ),
        name="prefix_attend",
    )(core, work, q, pk, pk_other, pv, pv_other)


def suffix_kernel(meta_ref, q_ref, k_ref, v_ref, o_ref, lse_ref):
    row = pl.program_id(0)
    token = lax.broadcasted_iota(jnp.int32, (ROW_TOK, 1), 0)
    first = jnp.zeros((ROW_TOK, 1), jnp.int32)
    for j in range(1, RQ):
        start = meta_ref[row, j]
        first = jnp.where(token >= start, start, first)

    def score(i):
        low = max(0, i * SUF - ROW_TOK // 2)
        here, seen = slice(i * SUF, (i + 1) * SUF), slice(low, (i + 1) * SUF)
        s = lax.dot_general(
            q_ref[0, here, :],
            k_ref[0, seen, :],
            (((1,), (1,)), ((), ())),
            preferred_element_type=jnp.float32,
        )
        other = low + lax.broadcasted_iota(jnp.int32, s.shape, 1)
        return jnp.where((other >= first[here]) & (other <= token[here]), s, NEG)

    def weigh(i, s):
        low = max(0, i * SUF - ROW_TOK // 2)
        here, seen = slice(i * SUF, (i + 1) * SUF), slice(low, (i + 1) * SUF)
        top = jnp.max(s, axis=1, keepdims=True)
        p = jnp.exp2((s - top) * SCORE_SCALE)
        total = jnp.sum(p, axis=1, keepdims=True)
        out = jnp.dot(
            p.astype(jnp.bfloat16), v_ref[0, seen, :], preferred_element_type=jnp.float32
        )
        o_ref[0, here, :] = out * (1.0 / total)
        lse = top * SCORE_SCALE + jnp.log2(total)
        for part in range(SUF // BLK):
            at = i * (SUF // BLK) + part
            lse_ref[0, at : at + 1, :] = as_row(lse[part * BLK : (part + 1) * BLK])

    count = ROW_TOK // SUF
    held = score(0)
    for i in range(count):
        later = score(i + 1) if i + 1 < count else None
        weigh(i, held)
        held = later


def suffix_attend(starts, q, k, v):
    rows, tokens, unused = q.shape
    whole = pl.BlockSpec((1, tokens, HEAD), lambda r, b: (r, 0, 0))
    blocks = tokens // BLK
    return pl.pallas_call(
        suffix_kernel,
        grid_spec=pltpu.PrefetchScalarGridSpec(
            num_scalar_prefetch=1,
            grid=(rows,),
            in_specs=[whole] * 3,
            out_specs=[whole, pl.BlockSpec((1, blocks, BLK), lambda r, b: (r, 0, 0))],
        ),
        out_shape=(
            jax.ShapeDtypeStruct((rows, tokens, HEAD), jnp.float32),
            jax.ShapeDtypeStruct((rows, blocks, BLK), jnp.float32),
        ),
        compiler_params=pltpu.CompilerParams(vmem_limit_bytes=VMEM_BIG),
        cost_estimate=pl.CostEstimate(
            flops=rows * tokens * tokens * HEAD * 4 * 4, bytes_accessed=1 << 20, transcendentals=0
        ),
        name="suffix_attend",
    )(starts, q, k, v)


MERGE_BLOCKS = 4


def merge_kernel(*refs):
    parts, out_ref = refs[:-1], refs[-1]
    step = pl.program_id(0)
    half = len(parts) // 2
    for row in range(2):
        sources = parts[row * half : (row + 1) * half]
        for block in range(MERGE_BLOCKS):
            here = slice(block * BLK, (block + 1) * BLK)
            at = pl.ds(step * MERGE_BLOCKS + block, 1)
            lses = [
                jnp.transpose(jnp.broadcast_to(lse[0, at, :], (BLK, BLK))) for lse in sources[1::2]
            ]
            top = lses[0]
            for lse in lses[1:]:
                top = jnp.maximum(top, lse)
            total, summed = 0.0, 0.0
            for lse, o in zip(lses, sources[0::2]):
                weight = jnp.exp2(lse - top)
                total = total + weight
                summed = summed + weight * o[0, here, :].astype(jnp.float32)
            out_ref[block, row * BLK : (row + 1) * BLK, :] = (summed / total).astype(out_ref.dtype)


def merge_parts(parts):
    blocks = parts[0][0][0].shape[1] // BLK
    specs, operands = [], []
    for row in parts:
        for o, lse, index in row:
            operands += [o, lse]
            specs += [
                pl.BlockSpec((1, MERGE_BLOCKS * BLK, HEAD), lambda b, index=index: (index, b, 0)),
                pl.BlockSpec((1, blocks, BLK), lambda b, index=index: (index, 0, 0)),
            ]
    return pl.pallas_call(
        merge_kernel,
        grid=(blocks // MERGE_BLOCKS,),
        in_specs=specs,
        out_specs=pl.BlockSpec((MERGE_BLOCKS, 2 * BLK, HEAD), lambda b: (b, 0, 0)),
        out_shape=jax.ShapeDtypeStruct((blocks, 2 * BLK, HEAD), jnp.bfloat16),
        name="merge_parts",
    )(*operands)


def project_kernel(a_ref, w_ref, keep_ref, send_ref, lhs):
    @pl.when(pl.program_id(0) == 0)
    def first():
        for h in range(a_ref.shape[0]):
            lhs[:, h * HEAD : (h + 1) * HEAD] = a_ref[h]

    out = jnp.dot(lhs[...], w_ref[...], preferred_element_type=jnp.float32)
    rows = keep_ref.shape[0]
    keep_ref[...] = out[:rows]
    send_ref[...] = out[rows:].astype(send_ref.dtype)


def project(attended, weights):
    heads, tokens, unused = attended.shape
    depth, width = weights.shape
    rows, tile = tokens // 2, 512
    out_spec = pl.BlockSpec((rows, tile), lambda i: (0, i))
    return pl.pallas_call(
        project_kernel,
        grid=(width // tile,),
        in_specs=[
            pl.BlockSpec((heads, tokens, HEAD), lambda i: (0, 0, 0)),
            pl.BlockSpec((depth, tile), lambda i: (0, i)),
        ],
        out_specs=[out_spec, out_spec],
        out_shape=(
            jax.ShapeDtypeStruct((rows, width), jnp.float32),
            jax.ShapeDtypeStruct((rows, width), jnp.bfloat16),
        ),
        scratch_shapes=[pltpu.VMEM((tokens, depth), jnp.bfloat16)],
        name="project",
    )(attended, weights)


def norm_kernel(keep, got, residual, gain, stream_ref, normed_ref):
    stream = residual[...].astype(jnp.float32) + (keep[...] + got[...].astype(jnp.float32))
    meansq = jnp.mean(stream * stream, axis=-1, keepdims=True)
    stream_ref[...] = stream
    normed = stream * lax.rsqrt(meansq + 1e-06) * gain[...].astype(jnp.float32)
    normed_ref[...] = normed.astype(normed_ref.dtype)


def norm_rows(keep, got, residual, gain):
    return pl.pallas_call(
        norm_kernel,
        out_shape=(
            jax.ShapeDtypeStruct(keep.shape, jnp.float32),
            jax.ShapeDtypeStruct(keep.shape, jnp.bfloat16),
        ),
        name="norm_rows",
    )(keep, got, residual, gain.reshape(1, -1))


EXP_DEV = 4
SLOTS = 32


def route_kernel(sc_ref, tab_ref, pick_ref, give_ref):
    before = (
        lax.broadcasted_iota(jnp.int32, (BLK, BLK), 0)
        < lax.broadcasted_iota(jnp.int32, (BLK, BLK), 1)
    ).astype(jnp.bfloat16)
    place = lax.broadcasted_iota(jnp.int32, (SLOTS, BLK), 0).astype(jnp.float32)
    for slot in range(8):
        tab = tab_ref[sc_ref[slot]].astype(jnp.float32)
        ids, gates = tab[:TOPK], tab[TOPK:]
        chosen, weights = [], []
        for j in range(EXP_DEV):
            match = ids == (sc_ref[8] + j).astype(jnp.float32)
            chosen.append(jnp.sum(match.astype(jnp.float32), axis=0, keepdims=True))
            weights.append(jnp.sum(jnp.where(match, gates, 0.0), axis=0, keepdims=True))
        held = jnp.concatenate(chosen + chosen, axis=0)
        places = jnp.dot(held.astype(jnp.bfloat16), before, preferred_element_type=jnp.float32)
        places = jnp.where(held > 0.5, places, -1.0)
        hits = [place == places[j : j + 1] for j in range(EXP_DEV)]
        pick_ref[slot] = jnp.concatenate(
            [hit.astype(jnp.float32) for hit in hits], axis=0
        ).astype(jnp.bfloat16)
        spread = jnp.concatenate(
            [jnp.where(hit, weight, 0.0) for hit, weight in zip(hits, weights)], axis=0
        )
        give_ref[slot] = jnp.transpose(spread).astype(jnp.bfloat16)


def route(scalars, tab):
    shape = jax.ShapeDtypeStruct((8, BLK, EXP_DEV * SLOTS), jnp.bfloat16)
    return pl.pallas_call(
        route_kernel,
        in_specs=[
            pl.BlockSpec(memory_space=pltpu.SMEM),
            pl.BlockSpec(memory_space=pltpu.VMEM),
        ],
        out_shape=(shape, shape),
        name="route",
    )(scalars, tab)


def experts_kernel(*refs):
    picked = refs[:8]
    give_ref, wg, wu, wd, out_ref, rows_out = refs[8:]
    expert = pl.program_id(0)
    rows = jnp.concatenate([part[...] for part in picked], axis=0)
    contract = (((1,), (1,)), ((), ()))
    gate_h = lax.dot_general(rows, wg[0], contract, preferred_element_type=jnp.float32)
    up_h = lax.dot_general(rows, wu[0], contract, preferred_element_type=jnp.float32)
    hidden = (gate_h / (1.0 + jnp.exp(-gate_h)) * up_h).astype(jnp.bfloat16)
    out = jnp.dot(hidden, wd[0], preferred_element_type=jnp.float32).astype(jnp.bfloat16)
    here = pl.ds(pl.multiple_of(expert * SLOTS, SLOTS), SLOTS)
    for slot in range(8):
        rows_out[slot, here, :] = out[slot * SLOTS : (slot + 1) * SLOTS]

    @pl.when(expert == EXP_DEV - 1)
    def last():
        for slot in range(8):
            out_ref[slot] = jnp.dot(
                give_ref[slot], rows_out[slot], preferred_element_type=jnp.float32
            ).astype(out_ref.dtype)


def run_experts(picked, give, w_gate, w_up, w_down):
    width = picked[0].shape[1]
    hidden = w_down.shape[1]
    once = pl.Buffered(1)
    return pl.pallas_call(
        experts_kernel,
        grid=(EXP_DEV,),
        in_specs=[pl.BlockSpec((SLOTS, width), lambda j: (j, 0))] * 8
        + [pl.BlockSpec((8, BLK, BLK), lambda j: (0, 0, 0))]
        + [pl.BlockSpec((1, hidden, width), lambda j: (j, 0, 0))] * 3,
        out_specs=pl.BlockSpec((8, BLK, width), lambda j: (0, 0, 0), pipeline_mode=once),
        out_shape=jax.ShapeDtypeStruct((8, BLK, width), jnp.bfloat16),
        scratch_shapes=[pltpu.VMEM((8, EXP_DEV * SLOTS, width), jnp.bfloat16)],
        compiler_params=pltpu.CompilerParams(vmem_limit_bytes=VMEM_BIG),
        name="experts",
    )(*picked, give, w_gate.transpose(0, 2, 1), w_up.transpose(0, 2, 1), w_down)


def pick_by_z(z, *choices):
    picked = choices[-1]
    for i in range(len(choices) - 2, -1, -1):
        if choices[i] is not picked:
            picked = jnp.where(z == i, choices[i], picked)
    return picked


SLOT_Z = ((0, 1, 2, 3), (1, 0, 2, 3), (2, 1, 3, 0), (3, 2, 1, 0))


def together(*arrays):
    return lax.optimization_barrier(arrays)


def gather_rows(z, own):
    up, down, there0 = together(z_up(own), z_down(own), y_swap(own))
    first = pick_by_z(z, down, up, up, up)
    up2, down2, there1 = together(z_up(up), z_down(down), y_swap(first))
    second = pick_by_z(z, down2, down, down, up2)
    up3, down3, there2 = together(z_up(up2), z_down(down2), y_swap(second))
    third = pick_by_z(z, down3, down2, up2, up3)
    return [own, first, second, third, there0, there1, there2, y_swap(third)]


def scatter_sums(z, sums):
    def plus(a, b):
        return (a.astype(jnp.float32) + b.astype(jnp.float32)).astype(jnp.bfloat16)

    s3 = plus(sums[3], y_swap(sums[7]))
    up, down = z_up(s3, 1), z_down(s3, 1)
    s2 = plus(sums[2], y_swap(sums[6]))
    up = z_up(pick_by_z(z, s2, plus(s3, up), s2, s2), 2)
    down = z_down(pick_by_z(z, s2, s2, plus(s3, down), s2), 2)
    s1 = plus(sums[1], y_swap(sums[5]))
    up = z_up(pick_by_z(z, s1, plus(s2, up), plus(s2, up), s1), 3)
    down = z_down(pick_by_z(z, s1, plus(s1, down), plus(s1, down), s1), 3)
    s0 = (sums[0], y_swap(sums[4]))
    return [part.astype(jnp.float32) for part in (*s0, up, down)]


def tabled(values, index):
    return jnp.asarray(values, jnp.int32)[index]


def block_device(
    queries,
    keys,
    values,
    prefix_keys,
    prefix_values,
    lengths,
    groups,
    residual,
    out_proj,
    norm_gain,
    expert_ids,
    expert_gates,
    w_gate,
    w_up,
    w_down,
):
    row_tok = queries.shape[0]
    core = lax.rem(lax.axis_index("req"), 2)
    place = lax.axis_index("exp")
    z = place // 2
    core_arg = core.astype(jnp.int32).reshape(1)

    proj_rows = lax.dynamic_slice_in_dim(out_proj, core * HEAD, HEAD, 0)
    proj_rows = lax.all_gather(proj_rows, "exp", axis=0, tiled=True)

    shape = jnp.concatenate([lengths, groups], axis=1)
    shapes = jnp.concatenate([shape, core_swap(shape)], axis=0)
    shapes = jnp.concatenate([shapes, x_swap(shapes)], axis=0)

    qkv_theirs, pk_theirs, pv_theirs = send_halves(
        core_arg, queries, keys, values, prefix_keys, prefix_values
    )
    qkv_other = core_swap(qkv_theirs)
    pk_other, pv_other = core_swap(pk_theirs), core_swap(pv_theirs)

    def mine(array):
        return jnp.where(core == 0, array[:, :HEAD], array[:, HEAD:])

    q_two = jnp.stack([mine(queries), qkv_other[0]])
    k_two = jnp.stack([mine(keys), qkv_other[1]])
    v_two = jnp.stack([mine(values), qkv_other[2]])
    q_far = x_swap(q_two)

    tab = jnp.concatenate([expert_ids.T.astype(jnp.bfloat16), expert_gates.T], axis=0)[None]
    for step in (1, 2, 4):
        tab = jnp.concatenate(
            [tab, lax.ppermute(tab, "exp", [(i, i ^ step) for i in range(8)])], axis=0
        )
    slot_z = tabled(SLOT_Z, z)
    slot_place = jnp.concatenate(
        [slot_z * 2 + lax.rem(place, 2), slot_z * 2 + 1 - lax.rem(place, 2)]
    )
    scalars = jnp.concatenate([slot_place ^ place, (place * EXP_DEV).reshape(1)])
    pick, give = route(scalars.astype(jnp.int32), tab)

    def prefix(q, rows, dtype):
        count = q.shape[0]
        work = prefix_work(shapes[rows, :RQ], shapes[rows, RQ:])
        o, lse = prefix_attend(
            work,
            core_arg,
            q.reshape(count * row_tok, HEAD),
            prefix_keys,
            pk_other,
            prefix_values,
            pv_other,
            dtype,
        )
        return o.reshape(q.shape), lse.reshape(count, row_tok // BLK, BLK)

    near_lengths = shapes[:2, :RQ]
    suffix = suffix_attend(jnp.cumsum(near_lengths, axis=1) - near_lengths, q_two, k_two, v_two)
    far = prefix(q_far, slice(2, 4), jnp.bfloat16)
    back = (x_swap(far[0]), x_swap(far[1]))
    near = prefix(q_two, slice(0, 2), jnp.float32)
    attended = merge_parts(
        [[(*part, row) for part in (suffix, near, back)] for row in range(2)]
    )
    heads = lax.all_to_all(attended, "exp", split_axis=0, concat_axis=0, tiled=True)
    keep, send = project(heads, proj_rows)
    stream, normed = norm_rows(keep, core_swap(send), residual, norm_gain)
    rows = gather_rows(z, normed)
    picked = [
        jnp.dot(pick[i], part, preferred_element_type=jnp.float32).astype(jnp.bfloat16)
        for i, part in enumerate(rows)
    ]
    sums = run_experts(picked, give, w_gate, w_up, w_down)
    parts = scatter_sums(z, sums)
    return (stream + sum(parts[1:], parts[0])).astype(jnp.bfloat16)


def solution(mesh):
    in_specs = (
        P("req", "exp"),
        P("req", "exp"),
        P("req", "exp"),
        P(None, "req", "exp"),
        P(None, "req", "exp"),
        P("req", None),
        P("req", None),
        P(("req", "exp"), None),
        P("exp", None),
        P(),
        P(("req", "exp"), None),
        P(("req", "exp"), None),
        P("exp", None, None),
        P("exp", None, None),
        P("exp", None, None),
    )
    out_specs = P(("req", "exp"), None)
    blocked = mesh.shape["req"] == 4 and mesh.shape["exp"] == 8
    return jax.shard_map(
        block_device if blocked else general_device,
        mesh=mesh,
        in_specs=in_specs,
        out_specs=out_specs,
        check_vma=False,
    )
```

```python
import math

import jax
import jax.numpy as jnp
from jax import lax
from jax.experimental import pallas as pl
from jax.experimental.pallas import tpu as pltpu
from jax.sharding import PartitionSpec as P

HEAD = 128
TOPK = 4
EXPERTS = 32
G = 4
RQ = 8
ROW_TOK = 1024


NEG = -1e30


def token_layout(lengths, groups):
    req_ends = jnp.cumsum(lengths, axis=-1)
    starts = req_ends - lengths
    position = jnp.arange(ROW_TOK, dtype=jnp.int32)
    request = jnp.sum((position[None, :, None] >= req_ends[:, None, :]).astype(jnp.int32), axis=-1)
    onehot = request[:, :, None] == jnp.arange(RQ, dtype=jnp.int32)[None, None, :]
    first_tok = jnp.sum(jnp.where(onehot, starts[:, None, :], 0), axis=-1)
    tok_group = jnp.sum(jnp.where(onehot, groups[:, None, :], 0), axis=-1)
    return (request, position[None, :] - first_tok, tok_group)


def split_blocks(row_count):
    if row_count % 1024 == 0 and row_count > 1024:
        return row_count // 1024
    return 1


def pack_parts(parts):
    return jnp.concatenate([parts[0], parts[1], parts[2]], axis=1)


def unpack_parts(packed, head_count):
    columns = head_count * HEAD
    return (
        packed[:, :columns],
        packed[:, columns : columns + head_count],
        packed[:, columns + head_count :],
    )


def attend_prefix(query_rows, query_group, prefix_k, prefix_v):
    row_count, columns = query_rows.shape
    head_count = columns // HEAD
    span = prefix_k.shape[1]
    key_grid = prefix_k.reshape(G, span, head_count, HEAD)
    val_grid = prefix_v.reshape(G, span, head_count, HEAD)
    blocks = split_blocks(row_count)
    block_len = row_count // blocks
    scaling = 1.0 / math.sqrt(HEAD)

    def per_block(pieces):
        block_q, block_g = pieces
        query_grid = block_q.reshape(block_len, head_count, HEAD)
        scores = (
            jnp.einsum("qhd,gkhd->hqgk", query_grid, key_grid, preferred_element_type=jnp.float32)
            * scaling
        )
        member = block_g[:, None] == jnp.arange(G, dtype=jnp.int32)[None, :]
        scores = jnp.where(member[None, :, :, None], scores, NEG)
        maxima = jnp.max(scores, axis=(2, 3))
        exp_terms = jnp.exp(scores - maxima[:, :, None, None])
        totals = jnp.sum(exp_terms, axis=(2, 3))
        weighted = jnp.einsum(
            "hqgk,gkhd->qhd",
            exp_terms.astype(jnp.bfloat16),
            val_grid,
            preferred_element_type=jnp.float32,
        )
        return (weighted.reshape(block_len, columns), maxima.T, totals.T)

    weighted, maxima, totals = lax.map(
        per_block,
        (query_rows.reshape(blocks, block_len, columns), query_group.reshape(blocks, block_len)),
    )
    return (
        weighted.reshape(row_count, columns),
        maxima.reshape(row_count, head_count),
        totals.reshape(row_count, head_count),
    )


def attend_suffix(queries, keys, values, request, position):
    row_count, columns = queries.shape
    head_count = columns // HEAD
    blocks = split_blocks(row_count)
    block_len = row_count // blocks
    scaling = 1.0 / math.sqrt(HEAD)
    key_grid = keys.reshape(row_count, head_count, HEAD)
    val_grid = values.reshape(row_count, head_count, HEAD)

    def per_block(pieces):
        block_q, block_req, block_pos = pieces
        query_grid = block_q.reshape(block_len, head_count, HEAD)
        scores = (
            jnp.einsum("qhd,khd->hqk", query_grid, key_grid, preferred_element_type=jnp.float32)
            * scaling
        )
        allowed = (request[None, :] == block_req[:, None]) & (
            position[None, :] <= block_pos[:, None]
        )
        scores = jnp.where(allowed[None, :, :], scores, NEG)
        maxima = jnp.max(scores, axis=2)
        exp_terms = jnp.exp(scores - maxima[:, :, None])
        totals = jnp.sum(exp_terms, axis=2)
        weighted = jnp.einsum(
            "hqk,khd->qhd",
            exp_terms.astype(jnp.bfloat16),
            val_grid,
            preferred_element_type=jnp.float32,
        )
        return (weighted.reshape(block_len, columns), maxima.T, totals.T)

    weighted, maxima, totals = lax.map(
        per_block,
        (
            queries.reshape(blocks, block_len, columns),
            request.reshape(blocks, block_len),
            position.reshape(blocks, block_len),
        ),
    )
    return (
        weighted.reshape(row_count, columns),
        maxima.reshape(row_count, head_count),
        totals.reshape(row_count, head_count),
    )


def combine(former, latter):
    weighted_a, maxima_a, totals_a = former
    weighted_b, maxima_b, totals_b = latter
    row_count, head_count = maxima_a.shape
    maxima = jnp.maximum(maxima_a, maxima_b)
    factor_a = jnp.exp(maxima_a - maxima)
    factor_b = jnp.exp(maxima_b - maxima)
    weighted = (
        weighted_a.reshape(row_count, head_count, HEAD) * factor_a[:, :, None]
        + weighted_b.reshape(row_count, head_count, HEAD) * factor_b[:, :, None]
    )
    return (
        weighted.reshape(row_count, head_count * HEAD),
        maxima,
        totals_a * factor_a + totals_b * factor_b,
    )


def general_device(
    queries,
    keys,
    values,
    prefix_keys,
    prefix_values,
    lengths,
    groups,
    residual,
    out_proj,
    norm_gain,
    expert_ids,
    expert_gates,
    w_gate,
    w_up,
    w_down,
):
    row_tok, columns = queries.shape
    head_count = columns // HEAD
    tok_dev = residual.shape[0]
    request, position, tok_group = token_layout(lengths, groups)
    request, position, tok_group = (request[0], position[0], tok_group[0])
    all_groups = lax.all_gather(tok_group, "req", axis=0, tiled=True)
    partial_value = pack_parts(
        attend_prefix(
            lax.all_gather(queries, "req", axis=0, tiled=True),
            all_groups,
            prefix_keys,
            prefix_values,
        )
    )
    returned = lax.all_to_all(partial_value, "req", split_axis=0, concat_axis=0, tiled=True)
    owners = returned.shape[0] // row_tok
    back_w, back_m, back_t = unpack_parts(returned, head_count)
    all_weighted = back_w.reshape(owners, row_tok, head_count, HEAD)
    all_maxima = back_m.reshape(owners, row_tok, head_count)
    all_totals = back_t.reshape(owners, row_tok, head_count)
    maxima = jnp.max(all_maxima, axis=0)
    factor = jnp.exp(all_maxima - maxima[None])
    weighted = jnp.sum(all_weighted * factor[..., None], axis=0).reshape(row_tok, columns)
    prefix_part = (weighted, maxima, jnp.sum(all_totals * factor, axis=0))
    suffix_part = attend_suffix(queries, keys, values, request, position)
    weighted, maxima, totals = combine(prefix_part, suffix_part)
    attended = (
        (weighted.reshape(row_tok, head_count, HEAD) / totals[:, :, None])
        .reshape(row_tok, columns)
        .astype(jnp.bfloat16)
    )
    projected = lax.psum_scatter(
        jnp.dot(attended, out_proj, preferred_element_type=jnp.float32),
        "exp",
        scatter_dimension=0,
        tiled=True,
    )
    stream = residual.astype(jnp.float32) + projected
    meansq = jnp.mean(stream * stream, axis=-1, keepdims=True)
    normed = (stream * lax.rsqrt(meansq + 1e-06) * norm_gain.astype(jnp.float32)).astype(
        jnp.bfloat16
    )
    capacity = max(2, tok_dev // 4)
    flat_ids = expert_ids.reshape(-1)
    onehot = (flat_ids[:, None] == jnp.arange(EXPERTS, dtype=jnp.int32)[None, :]).astype(jnp.int32)
    slot_of = jnp.sum(onehot * (jnp.cumsum(onehot, axis=0) - 1), axis=1)
    source_rows = jnp.arange(tok_dev * TOPK, dtype=jnp.int32) // TOPK
    buffer = (
        jnp.zeros((EXPERTS, capacity, normed.shape[1]), jnp.bfloat16)
        .at[flat_ids, slot_of]
        .set(normed[source_rows])
    )
    exp_count = lax.axis_size("exp")
    exp_dev = w_gate.shape[0]
    received = lax.all_to_all(buffer, "exp", split_axis=0, concat_axis=0, tiled=True)
    slots = received.shape[1]
    grid_in = received.reshape(exp_count, exp_dev, slots, received.shape[2])
    gate_h = jnp.einsum("secd,edf->secf", grid_in, w_gate, preferred_element_type=jnp.float32)
    up_h = jnp.einsum("secd,edf->secf", grid_in, w_up, preferred_element_type=jnp.float32)
    hidden = (jax.nn.silu(gate_h) * up_h).astype(jnp.bfloat16)
    expert_out = jnp.einsum("secf,efd->secd", hidden, w_down, preferred_element_type=jnp.float32)
    returned = lax.all_to_all(
        expert_out.reshape(EXPERTS, slots, received.shape[2]),
        "exp",
        split_axis=0,
        concat_axis=0,
        tiled=True,
    )
    gathered = returned[flat_ids, slot_of] * expert_gates.reshape(-1).astype(jnp.float32)[:, None]
    mixture = jnp.sum(gathered.reshape(tok_dev, TOPK, gathered.shape[1]), axis=1)
    return (stream + mixture).astype(jnp.bfloat16)


BLK = 128
LOG2E = 1.4426950408889634
SCORE_SCALE = LOG2E / math.sqrt(HEAD)
VMEM_BIG = 56 * 1024 * 1024


def core_swap(array):
    return lax.ppermute(array, "req", [(i, i ^ 1) for i in range(4)])


def x_swap(array):
    return lax.ppermute(array, "req", [(i, i ^ 2) for i in range(4)])


def y_swap(array):
    return lax.ppermute(array, "exp", [(i, i ^ 1) for i in range(8)])


def z_up(array, first=0, last=2):
    return lax.ppermute(array, "exp", [(i, i + 2) for i in range(2 * first, 2 * last + 2)])


def z_down(array, first=3, last=1):
    return lax.ppermute(array, "exp", [(i, i - 2) for i in range(2 * last, 2 * first + 2)])


def split_tokens_kernel(sc_ref, *refs):
    for i in range(3):
        refs[6][i] = refs[i][...]
        refs[7][i] = refs[3 + i][...]


def split_tokens(core, q, k, v):
    rows = q.shape[0]
    part = rows // 2
    mine = pl.BlockSpec((part, HEAD), lambda i, s: (i, s[0]))
    theirs = pl.BlockSpec((part, HEAD), lambda i, s: (i, 1 - s[0]))
    out = pl.BlockSpec((3, part, HEAD), lambda i, s: (0, i, 0))
    shape = jax.ShapeDtypeStruct((3, rows, HEAD), q.dtype)
    return pl.pallas_call(
        split_tokens_kernel,
        grid_spec=pltpu.PrefetchScalarGridSpec(
            num_scalar_prefetch=1,
            grid=(2,),
            in_specs=[mine] * 3 + [theirs] * 3,
            out_specs=[out, out],
        ),
        out_shape=(shape, shape),
        name="split_tokens",
    )(core, q, k, v, q, k, v)


def split_prefix_kernel(sc_ref, pk, pv, out_pk, out_pv):
    out_pk[...] = pk[...]
    out_pv[...] = pv[...]


def split_prefix(core, pk, pv):
    span = pk.shape[1]
    theirs = pl.BlockSpec((1, span, HEAD), lambda i, s: (i, 0, 1 - s[0]))
    out = pl.BlockSpec((1, span, HEAD), lambda i, s: (i, 0, 0))
    shape = jax.ShapeDtypeStruct((G, span, HEAD), pk.dtype)
    return pl.pallas_call(
        split_prefix_kernel,
        grid_spec=pltpu.PrefetchScalarGridSpec(
            num_scalar_prefetch=1, grid=(G,), in_specs=[theirs] * 2, out_specs=[out] * 2
        ),
        out_shape=(shape, shape),
        name="split_prefix",
    )(core, pk, pv)


def as_row(column):
    return jnp.transpose(jnp.broadcast_to(column, (BLK, BLK)))[0:1, :]


SUF = 256
SUB = 32
PER_ITEM = 8
ITEMS = 16


def build_work(shape_ref, rows, item_group, item_block):
    per_row = ROW_TOK // SUB
    spans = []
    for r in range(rows):
        start = 0
        for j in range(RQ):
            end = start + shape_ref[r, j]
            first, last = r * per_row + start // SUB, r * per_row + (end - 1) // SUB
            spans.append((first, last, shape_ref[r, RQ + j]))
            start = end

    def of_group(g, begin):
        at, done = begin, jnp.int32(-1)
        for first, last, group in spans:
            first = jnp.maximum(first, done + 1)
            match = group == g
            count = jnp.where(match, last - first + 1, 0)

            def put(i, carry, at=at, first=first):
                item_block[at + i] = first + i
                return carry

            lax.fori_loop(0, count, put, 0)
            at = at + count
            done = jnp.where(match, last, done)
        stop = (at + PER_ITEM - 1) // PER_ITEM * PER_ITEM

        def fill(i, carry):
            item_block[i] = item_block[begin]
            return carry

        def name(i, carry):
            item_group[i] = g
            return carry

        lax.fori_loop(at, stop, fill, 0)
        lax.fori_loop(begin // PER_ITEM, stop // PER_ITEM, name, 0)
        return stop

    return lax.fori_loop(0, G, of_group, jnp.int32(0)) // PER_ITEM


def prefix_kernel(
    core_ref, shape_ref, q0, q1, pk, pk_other, pv, pv_other, o_ref, lse_ref,
    q_ref, ka, kb, va, vb, grp, lse, sa, sb, ta, tb, item_group, item_block, sems,
):
    tokens = q_ref.shape[0]
    rows = tokens // ROW_TOK
    span = ka.shape[1]
    mine_cols = pl.ds(pl.multiple_of(core_ref[0] * HEAD, HEAD), HEAD)
    copies = [
        pltpu.make_async_copy(q0, q_ref.at[:ROW_TOK, :], sems.at[0]),
        pltpu.make_async_copy(q1, q_ref.at[ROW_TOK:, :], sems.at[1]),
        pltpu.make_async_copy(pk.at[:, :, mine_cols], ka, sems.at[2]),
        pltpu.make_async_copy(pk_other, kb, sems.at[3]),
        pltpu.make_async_copy(pv.at[:, :, mine_cols], va, sems.at[4]),
        pltpu.make_async_copy(pv_other, vb, sems.at[5]),
    ]
    for copy in copies:
        copy.start()
    for r in range(rows):
        token = lax.broadcasted_iota(jnp.int32, (ROW_TOK, HEAD), 0)
        group = jnp.full((ROW_TOK, HEAD), shape_ref[r, RQ], jnp.int32)
        start = 0
        for j in range(1, RQ):
            start = start + shape_ref[r, j - 1]
            group = jnp.where(token >= start, shape_ref[r, RQ + j], group)
        grp[r * ROW_TOK : (r + 1) * ROW_TOK, :] = group
    count = build_work(shape_ref, rows, item_group, item_block)
    for copy in copies:
        copy.wait()
    step = 512

    def held(item):
        return jnp.where(item < count, item, 0)

    def places(item):
        at = held(item) * PER_ITEM
        return [
            pl.ds(pl.multiple_of(item_block[at + i] * SUB, SUB), SUB) for i in range(PER_ITEM)
        ]

    def group_of(item):
        return item_group[held(item)]

    def lanes(x, op):
        parts = [x[:, c : c + HEAD] for c in range(0, x.shape[1], HEAD)]
        while len(parts) > 1:
            parts = [op(a, b) for a, b in zip(parts[::2], parts[1::2])]
        return parts[0]

    def score(item, s, tops):
        g = group_of(item)
        q = jnp.concatenate([q_ref[place, :] for place in places(item)], axis=0)
        for half, k in enumerate((ka, kb)):
            for c in range(0, span, step):
                x = lax.dot_general(
                    q,
                    k[g, c : c + step, :],
                    (((1,), (1,)), ((), ())),
                    preferred_element_type=jnp.float32,
                )
                s[:, half * span + c : half * span + c + step] = x
                top = lanes(x, jnp.maximum)
                tops[...] = top if half == 0 and c == 0 else jnp.maximum(tops[...], top)

    def weigh(item, s, tops):
        g = group_of(item)
        where = places(item)
        for part in range(2):
            here = slice(part * BLK, (part + 1) * BLK)
            top = jnp.max(tops[here, :], axis=1, keepdims=True)
            out = jnp.zeros((BLK, HEAD), jnp.float32)
            total = jnp.zeros((BLK, HEAD), jnp.float32)
            for half, v in enumerate((va, vb)):
                for c in range(0, span, step):
                    x = s[here, half * span + c : half * span + c + step]
                    p = jnp.exp2((x - top) * SCORE_SCALE)
                    total = total + lanes(p, jnp.add)
                    out = out + jnp.dot(
                        p.astype(jnp.bfloat16),
                        v[g, c : c + step, :],
                        preferred_element_type=jnp.float32,
                    )
            total = jnp.sum(total, axis=1, keepdims=True)
            out = out * (1.0 / total)
            here_lse = jnp.broadcast_to(top * SCORE_SCALE + jnp.log2(total), (BLK, HEAD))
            for i in range(BLK // SUB):
                place = where[part * (BLK // SUB) + i]
                sub = slice(i * SUB, (i + 1) * SUB)
                mine = grp[place, :] == g
                o_ref[place, :] = jnp.where(
                    mine, out[sub], o_ref[place, :].astype(jnp.float32)
                ).astype(o_ref.dtype)
                lse[place, :] = jnp.where(mine, here_lse[sub], lse[place, :])

    score(0, sa, ta)

    def pair(i, carry):
        score(2 * i + 1, sb, tb)
        weigh(2 * i, sa, ta)
        score(2 * i + 2, sa, ta)
        weigh(2 * i + 1, sb, tb)
        return carry

    lax.fori_loop(0, (count + 1) // 2, pair, 0)
    for b in range(tokens // BLK):
        lse_ref[b // 8, b % 8 : b % 8 + 1, :] = jnp.transpose(lse[b * BLK : (b + 1) * BLK, :])[
            0:1, :
        ]


def prefix_attend(core, shape, q0, q1, pk, pk_other, pv, pv_other, out_dtype):
    rows = shape.shape[0]
    tokens = rows * ROW_TOK
    span = pk.shape[1]
    blocks = ROW_TOK // BLK
    smem = pl.BlockSpec(memory_space=pltpu.SMEM)
    vmem = pl.BlockSpec(memory_space=pltpu.VMEM)
    anywhere = pl.BlockSpec(memory_space=pl.ANY)
    prefix_buffer = pltpu.VMEM((G, span, HEAD), pk.dtype)
    per_token = pltpu.VMEM((tokens, HEAD), jnp.float32)
    scores = pltpu.VMEM((PER_ITEM * SUB, 2 * span), jnp.float32)
    tops = pltpu.VMEM((PER_ITEM * SUB, HEAD), jnp.float32)
    return pl.pallas_call(
        prefix_kernel,
        in_specs=[smem, smem] + [anywhere] * 6,
        out_specs=(vmem, vmem),
        out_shape=(
            jax.ShapeDtypeStruct((tokens, HEAD), out_dtype),
            jax.ShapeDtypeStruct((rows, blocks, BLK), jnp.float32),
        ),
        scratch_shapes=[
            pltpu.VMEM((tokens, HEAD), q0.dtype),
            prefix_buffer,
            prefix_buffer,
            prefix_buffer,
            prefix_buffer,
            pltpu.VMEM((tokens, HEAD), jnp.int32),
            per_token,
            scores,
            scores,
            tops,
            tops,
            pltpu.SMEM((ITEMS,), jnp.int32),
            pltpu.SMEM((ITEMS * PER_ITEM,), jnp.int32),
            pltpu.SemaphoreType.DMA((6,)),
        ],
        compiler_params=pltpu.CompilerParams(vmem_limit_bytes=VMEM_BIG),
        cost_estimate=pl.CostEstimate(
            flops=tokens * span * HEAD * 8 * 4,
            bytes_accessed=4 * G * span * HEAD * 2,
            transcendentals=0,
        ),
        name="prefix_attend",
    )(core, shape, q0, q1, pk, pk_other, pv, pv_other)


def suffix_kernel(shape_ref, row0, row1, o_ref, lse_ref):
    count = ROW_TOK // SUF
    for row, qkv in enumerate((row0, row1)):
        token = lax.broadcasted_iota(jnp.int32, (ROW_TOK, 1), 0)
        first = jnp.zeros((ROW_TOK, 1), jnp.int32)
        start = 0
        for j in range(1, RQ):
            start = start + shape_ref[row, j - 1]
            first = jnp.where(token >= start, start, first)

        def bounds(i):
            low = max(0, i * SUF - ROW_TOK // 2)
            return low, slice(i * SUF, (i + 1) * SUF), slice(low, (i + 1) * SUF)

        def score(i, qkv=qkv, first=first, token=token):
            low, here, seen = bounds(i)
            s = lax.dot_general(
                qkv[0, here, :],
                qkv[1, seen, :],
                (((1,), (1,)), ((), ())),
                preferred_element_type=jnp.float32,
            )
            other = low + lax.broadcasted_iota(jnp.int32, s.shape, 1)
            return jnp.where((other >= first[here]) & (other <= token[here]), s, NEG)

        def weigh(i, s, row=row, qkv=qkv):
            unused, here, seen = bounds(i)
            top = jnp.max(s, axis=1, keepdims=True)
            p = jnp.exp2((s - top) * SCORE_SCALE)
            total = jnp.sum(p, axis=1, keepdims=True)
            out = jnp.dot(
                p.astype(jnp.bfloat16), qkv[2, seen, :], preferred_element_type=jnp.float32
            )
            o_ref[row * ROW_TOK + i * SUF : row * ROW_TOK + (i + 1) * SUF, :] = out * (1.0 / total)
            lse = top * SCORE_SCALE + jnp.log2(total)
            for part in range(SUF // BLK):
                at = i * (SUF // BLK) + part
                lse_ref[row, at : at + 1, :] = as_row(lse[part * BLK : (part + 1) * BLK])

        held = score(0)
        for i in range(count):
            later = score(i + 1) if i + 1 < count else None
            weigh(i, held)
            held = later


def suffix_attend(shape, row0, row1):
    rows, tokens = shape.shape[0], row0.shape[1]
    smem = pl.BlockSpec(memory_space=pltpu.SMEM)
    vmem = pl.BlockSpec(memory_space=pltpu.VMEM)
    return pl.pallas_call(
        suffix_kernel,
        in_specs=[smem, vmem, vmem],
        out_specs=(vmem, vmem),
        out_shape=(
            jax.ShapeDtypeStruct((rows * tokens, HEAD), jnp.float32),
            jax.ShapeDtypeStruct((rows, tokens // BLK, BLK), jnp.float32),
        ),
        compiler_params=pltpu.CompilerParams(vmem_limit_bytes=VMEM_BIG),
        cost_estimate=pl.CostEstimate(
            flops=rows * tokens * tokens * HEAD * 4 * 4, bytes_accessed=1 << 20, transcendentals=0
        ),
        name="suffix_attend",
    )(shape, row0, row1)


MERGE_BLOCKS = 4


def merge_kernel(*refs):
    parts, out_ref = refs[:-1], refs[-1]
    step = pl.program_id(0)
    half = len(parts) // 2
    for row in range(2):
        sources = parts[row * half : (row + 1) * half]
        for block in range(MERGE_BLOCKS):
            here = slice(block * BLK, (block + 1) * BLK)
            at = pl.ds(step * MERGE_BLOCKS + block, 1)
            lses = [
                jnp.transpose(jnp.broadcast_to(lse[0, at, :], (BLK, BLK))) for lse in sources[1::2]
            ]
            top = lses[0]
            for lse in lses[1:]:
                top = jnp.maximum(top, lse)
            total, summed = 0.0, 0.0
            for lse, o in zip(lses, sources[0::2]):
                weight = jnp.exp2(lse - top)
                total = total + weight
                summed = summed + weight * o[here, :].astype(jnp.float32)
            out_ref[block, row * BLK : (row + 1) * BLK, :] = (summed / total).astype(out_ref.dtype)


def merge_parts(parts):
    blocks = ROW_TOK // BLK
    steps = blocks // MERGE_BLOCKS
    specs, operands = [], []
    for row in range(2):
        for o, lse in parts:
            operands += [o, lse]
            specs += [
                pl.BlockSpec((MERGE_BLOCKS * BLK, HEAD), lambda b, row=row: (row * steps + b, 0)),
                pl.BlockSpec((1, blocks, BLK), lambda b, row=row: (row, 0, 0)),
            ]
    return pl.pallas_call(
        merge_kernel,
        grid=(steps,),
        in_specs=specs,
        out_specs=pl.BlockSpec((MERGE_BLOCKS, 2 * BLK, HEAD), lambda b: (b, 0, 0)),
        out_shape=jax.ShapeDtypeStruct((blocks, 2 * BLK, HEAD), jnp.bfloat16),
        name="merge_parts",
    )(*operands)


def project_kernel(a_ref, w_ref, keep_ref, send_ref, lhs):
    @pl.when(pl.program_id(0) == 0)
    def first():
        for h in range(a_ref.shape[0]):
            lhs[:, h * HEAD : (h + 1) * HEAD] = a_ref[h]

    out = jnp.dot(lhs[...], w_ref[...], preferred_element_type=jnp.float32)
    rows = keep_ref.shape[0]
    keep_ref[...] = out[:rows]
    send_ref[...] = out[rows:].astype(send_ref.dtype)


def project(attended, weights):
    heads, tokens, unused = attended.shape
    depth, width = weights.shape
    rows, tile = tokens // 2, 1024
    out_spec = pl.BlockSpec((rows, tile), lambda i: (0, i))
    return pl.pallas_call(
        project_kernel,
        grid=(width // tile,),
        in_specs=[
            pl.BlockSpec((heads, tokens, HEAD), lambda i: (0, 0, 0)),
            pl.BlockSpec((depth, tile), lambda i: (0, i)),
        ],
        out_specs=[out_spec, out_spec],
        out_shape=(
            jax.ShapeDtypeStruct((rows, width), jnp.float32),
            jax.ShapeDtypeStruct((rows, width), jnp.bfloat16),
        ),
        scratch_shapes=[pltpu.VMEM((tokens, depth), jnp.bfloat16)],
        compiler_params=pltpu.CompilerParams(vmem_limit_bytes=VMEM_BIG),
        name="project",
    )(attended, weights)


def norm_kernel(keep, got, residual, gain, stream_ref, normed_ref):
    stream = residual[...].astype(jnp.float32) + (keep[...] + got[...].astype(jnp.float32))
    meansq = jnp.mean(stream * stream, axis=-1, keepdims=True)
    stream_ref[...] = stream
    normed = stream * lax.rsqrt(meansq + 1e-06) * gain[...].astype(jnp.float32)
    normed_ref[...] = normed.astype(normed_ref.dtype)


def norm_rows(keep, got, residual, gain):
    return pl.pallas_call(
        norm_kernel,
        out_shape=(
            jax.ShapeDtypeStruct(keep.shape, jnp.float32),
            jax.ShapeDtypeStruct(keep.shape, jnp.bfloat16),
        ),
        name="norm_rows",
    )(keep, got, residual, gain)


EXP_DEV = 4
SLOTS = 32


def route_kernel(sc_ref, tab_ref, pick_ref, give_ref):
    before = (
        lax.broadcasted_iota(jnp.int32, (BLK, BLK), 0)
        < lax.broadcasted_iota(jnp.int32, (BLK, BLK), 1)
    ).astype(jnp.bfloat16)
    place = lax.broadcasted_iota(jnp.int32, (SLOTS, BLK), 0).astype(jnp.float32)
    for slot in range(8):
        tab = tab_ref[sc_ref[slot]].astype(jnp.float32)
        ids, gates = tab[:TOPK], tab[TOPK:]
        chosen, weights = [], []
        for j in range(EXP_DEV):
            match = ids == (sc_ref[8] + j).astype(jnp.float32)
            chosen.append(jnp.sum(match.astype(jnp.float32), axis=0, keepdims=True))
            weights.append(jnp.sum(jnp.where(match, gates, 0.0), axis=0, keepdims=True))
        held = jnp.concatenate(chosen + chosen, axis=0)
        places = jnp.dot(held.astype(jnp.bfloat16), before, preferred_element_type=jnp.float32)
        places = jnp.where(held > 0.5, places, -1.0)
        hits = [place == places[j : j + 1] for j in range(EXP_DEV)]
        pick_ref[slot] = jnp.concatenate(
            [hit.astype(jnp.float32) for hit in hits], axis=0
        ).astype(jnp.bfloat16)
        spread = jnp.concatenate(
            [jnp.where(hit, weight, 0.0) for hit, weight in zip(hits, weights)], axis=0
        )
        give_ref[slot] = jnp.transpose(spread).astype(jnp.bfloat16)


def route(scalars, tab):
    shape = jax.ShapeDtypeStruct((8, BLK, EXP_DEV * SLOTS), jnp.bfloat16)
    return pl.pallas_call(
        route_kernel,
        in_specs=[
            pl.BlockSpec(memory_space=pltpu.SMEM),
            pl.BlockSpec(memory_space=pltpu.VMEM),
        ],
        out_shape=(shape, shape),
        name="route",
    )(scalars, tab)


def experts_kernel(*refs):
    picked = refs[:8]
    give_ref, wg, wu, wd = refs[8:12]
    outs, rows_out = refs[12:21], refs[21]
    expert = pl.program_id(0)
    rows = jnp.concatenate([part[...] for part in picked], axis=0)
    contract = (((1,), (1,)), ((), ()))
    gate_h = lax.dot_general(rows, wg[0], contract, preferred_element_type=jnp.float32)
    up_h = lax.dot_general(rows, wu[0], contract, preferred_element_type=jnp.float32)
    hidden = (gate_h / (1.0 + jnp.exp(-gate_h)) * up_h).astype(jnp.bfloat16)
    out = jnp.dot(hidden, wd[0], preferred_element_type=jnp.float32).astype(jnp.bfloat16)
    here = pl.ds(pl.multiple_of(expert * SLOTS, SLOTS), SLOTS)
    for slot in range(8):
        rows_out[slot, here, :] = out[slot * SLOTS : (slot + 1) * SLOTS]

    @pl.when(expert == EXP_DEV - 1)
    def last():
        for slot in range(8):
            out = jnp.dot(give_ref[slot], rows_out[slot], preferred_element_type=jnp.float32)
            out = out.astype(jnp.bfloat16)
            if slot < 7:
                outs[slot][...] = out
            else:
                outs[7][...] = out[: BLK // 2]
                outs[8][...] = out[BLK // 2 :]


def run_experts(picked, give, w_gate, w_up, w_down):
    width = picked[0].shape[1]
    hidden = w_down.shape[1]
    once = pl.Buffered(1)
    heights = [BLK] * 7 + [BLK // 2] * 2
    return pl.pallas_call(
        experts_kernel,
        grid=(EXP_DEV,),
        in_specs=[pl.BlockSpec((SLOTS, width), lambda j: (j, 0))] * 8
        + [pl.BlockSpec((8, BLK, BLK), lambda j: (0, 0, 0))]
        + [pl.BlockSpec((1, hidden, width), lambda j: (j, 0, 0))] * 3,
        out_specs=[pl.BlockSpec((n, width), lambda j: (0, 0), pipeline_mode=once) for n in heights],
        out_shape=[jax.ShapeDtypeStruct((n, width), jnp.bfloat16) for n in heights],
        scratch_shapes=[pltpu.VMEM((8, EXP_DEV * SLOTS, width), jnp.bfloat16)],
        compiler_params=pltpu.CompilerParams(vmem_limit_bytes=VMEM_BIG),
        name="experts",
    )(*picked, give, w_gate.transpose(0, 2, 1), w_up.transpose(0, 2, 1), w_down)


def pick_by_z(z, *choices):
    picked = choices[-1]
    for i in range(len(choices) - 2, -1, -1):
        if choices[i] is not picked:
            picked = jnp.where(z == i, choices[i], picked)
    return picked


SLOT_Z = ((0, 1, 2, 3), (1, 0, 3, 2), (2, 3, 0, 1), (3, 2, 1, 0))


def together(*arrays):
    return lax.optimization_barrier(arrays)


def gather_rows(z, own):
    half = own.shape[0] // 2
    up, down, there0 = together(z_up(own), z_down(own), y_swap(own))
    first = pick_by_z(z, down, up, down, up)
    up2, down2, there1 = together(z_up(up), z_down(down), y_swap(first))
    second = pick_by_z(z, down2, down2, up2, up2)
    up3, down3, there2 = together(z_up(up2), z_down(down2), y_swap(second))
    third = pick_by_z(z, down3, down, up, up3)
    late_up = z_up(pick_by_z(z, there0, there0, there2, there2)[half:], 1, 2)
    late_down = z_down(pick_by_z(z, there2, there2, there0, there0)[half:], 2, 1)
    late, late_up, late_down = together(y_swap(third[:half]), late_up, late_down)
    there3 = jnp.concatenate([late, pick_by_z(z, late_down, late_down, late_up, late_up)], axis=0)
    return [own, first, second, third, there0, there1, there2, there3]


def plus(*parts):
    return sum([part.astype(jnp.float32) for part in parts[1:]], parts[0].astype(jnp.float32))


def plus16(*parts):
    return plus(*parts).astype(jnp.bfloat16)


def scatter_sums(z, sums):
    half = sums[7].shape[0]
    got, late_up, late_down = together(
        y_swap(sums[7]), z_up(sums[8], 0, 1), z_down(sums[8], 3, 2)
    )
    s3 = jnp.concatenate([plus16(sums[3][:half], got), sums[3][half:]], axis=0)
    fourth = plus16(sums[4][half:], pick_by_z(z, late_down, late_down, late_up, late_up))
    sixth = plus16(sums[6][half:], pick_by_z(z, late_up, late_up, late_down, late_down))
    fourth = jnp.concatenate([sums[4][:half], fourth], axis=0)
    sixth = jnp.concatenate([sums[6][:half], sixth], axis=0)
    got, up, down = together(y_swap(sixth), z_up(s3, 0, 0), z_down(s3, 3, 3))
    s2 = plus16(sums[2], got)
    got, up, down = together(
        y_swap(sums[5]),
        z_up(pick_by_z(z, s2, plus16(s2, up), s2, s2), 0, 1),
        z_down(pick_by_z(z, s2, s2, plus16(s2, down), s2), 3, 2),
    )
    s1 = plus16(sums[1], got)
    got, up, down = together(
        y_swap(fourth),
        z_up(pick_by_z(z, s1, plus16(s3, up), plus16(s1, up), s1)),
        z_down(pick_by_z(z, s1, plus16(s1, down), plus16(s3, down), s1)),
    )
    return plus(sums[0], got, up, down)


def tabled(values, index):
    return jnp.asarray(values, jnp.int32)[index]


def block_device(
    queries,
    keys,
    values,
    prefix_keys,
    prefix_values,
    lengths,
    groups,
    residual,
    out_proj,
    norm_gain,
    expert_ids,
    expert_gates,
    w_gate,
    w_up,
    w_down,
):
    row_tok = queries.shape[0]
    core = lax.rem(lax.axis_index("req"), 2)
    place = lax.axis_index("exp")
    z = place // 2
    core_arg = core.astype(jnp.int32).reshape(1)

    mine, theirs = split_tokens(core_arg, queries, keys, values)
    q_far0 = x_swap(mine[0])
    other = core_swap(theirs)

    shape = jnp.concatenate([lengths, groups], axis=1)
    near_shape = jnp.concatenate([shape, core_swap(shape)], axis=0)
    far_shape = x_swap(near_shape)

    pk_theirs, pv_theirs = split_prefix(core_arg, prefix_keys, prefix_values)
    pk_other, pv_other = core_swap(pk_theirs), core_swap(pv_theirs)
    q_far1 = x_swap(other[0])

    proj_rows = lax.dynamic_slice_in_dim(out_proj, core * HEAD, HEAD, 0)
    proj_rows = lax.all_gather(proj_rows, "exp", axis=0, tiled=True)

    tab = jnp.concatenate([expert_ids.T.astype(jnp.bfloat16), expert_gates.T], axis=0)[None]
    for step in (1, 2, 4):
        tab = jnp.concatenate(
            [tab, lax.ppermute(tab, "exp", [(i, i ^ step) for i in range(8)])], axis=0
        )
    slot_z = tabled(SLOT_Z, z)
    slot_place = jnp.concatenate(
        [slot_z * 2 + lax.rem(place, 2), slot_z * 2 + 1 - lax.rem(place, 2)]
    )
    scalars = jnp.concatenate([slot_place ^ place, (place * EXP_DEV).reshape(1)])
    pick, give = route(scalars.astype(jnp.int32), tab)

    def prefix(shape, q0, q1, dtype):
        return prefix_attend(
            core_arg, shape, q0, q1, prefix_keys, pk_other, prefix_values, pv_other, dtype
        )

    suffix = suffix_attend(near_shape, mine, other)
    far = prefix(far_shape, q_far0, q_far1, jnp.bfloat16)
    back = (x_swap(far[0]), x_swap(far[1]))
    near = prefix(near_shape, mine[0], other[0], jnp.float32)
    near_o, pick, give, gain = together(near[0], pick, give, norm_gain.reshape(1, -1))
    attended = merge_parts([suffix, (near_o, near[1]), back])
    heads = lax.all_to_all(attended, "exp", split_axis=0, concat_axis=0, tiled=True)
    keep, send = project(heads, proj_rows)
    stream, normed = norm_rows(keep, core_swap(send), residual, gain)
    rows = gather_rows(z, normed)
    picked = [
        jnp.dot(pick[i], part, preferred_element_type=jnp.float32).astype(jnp.bfloat16)
        for i, part in enumerate(rows)
    ]
    sums = run_experts(picked, give, w_gate, w_up, w_down)
    return (stream + scatter_sums(z, sums)).astype(jnp.bfloat16)


def solution(mesh):
    in_specs = (
        P("req", "exp"),
        P("req", "exp"),
        P("req", "exp"),
        P(None, "req", "exp"),
        P(None, "req", "exp"),
        P("req", None),
        P("req", None),
        P(("req", "exp"), None),
        P("exp", None),
        P(),
        P(("req", "exp"), None),
        P(("req", "exp"), None),
        P("exp", None, None),
        P("exp", None, None),
        P("exp", None, None),
    )
    out_specs = P(("req", "exp"), None)
    blocked = mesh.shape["req"] == 4 and mesh.shape["exp"] == 8
    return jax.shard_map(
        block_device if blocked else general_device,
        mesh=mesh,
        in_specs=in_specs,
        out_specs=out_specs,
        check_vma=False,
    )
```

```python
import functools
import math

import jax
import jax.numpy as jnp
from jax import lax
from jax.experimental import pallas as pl
from jax.experimental.pallas import tpu as pltpu
from jax.sharding import PartitionSpec as P

HEAD = 128
TOPK = 4
EXPERTS = 32
G = 4
RQ = 8
ROW_TOK = 1024


NEG = -1e30


def token_layout(lengths, groups):
    req_ends = jnp.cumsum(lengths, axis=-1)
    starts = req_ends - lengths
    position = jnp.arange(ROW_TOK, dtype=jnp.int32)
    request = jnp.sum((position[None, :, None] >= req_ends[:, None, :]).astype(jnp.int32), axis=-1)
    onehot = request[:, :, None] == jnp.arange(RQ, dtype=jnp.int32)[None, None, :]
    first_tok = jnp.sum(jnp.where(onehot, starts[:, None, :], 0), axis=-1)
    tok_group = jnp.sum(jnp.where(onehot, groups[:, None, :], 0), axis=-1)
    return (request, position[None, :] - first_tok, tok_group)


def split_blocks(row_count):
    if row_count % 1024 == 0 and row_count > 1024:
        return row_count // 1024
    return 1


def pack_parts(parts):
    return jnp.concatenate([parts[0], parts[1], parts[2]], axis=1)


def unpack_parts(packed, head_count):
    columns = head_count * HEAD
    return (
        packed[:, :columns],
        packed[:, columns : columns + head_count],
        packed[:, columns + head_count :],
    )


def attend_prefix(query_rows, query_group, prefix_k, prefix_v):
    row_count, columns = query_rows.shape
    head_count = columns // HEAD
    span = prefix_k.shape[1]
    key_grid = prefix_k.reshape(G, span, head_count, HEAD)
    val_grid = prefix_v.reshape(G, span, head_count, HEAD)
    blocks = split_blocks(row_count)
    block_len = row_count // blocks
    scaling = 1.0 / math.sqrt(HEAD)

    def per_block(pieces):
        block_q, block_g = pieces
        query_grid = block_q.reshape(block_len, head_count, HEAD)
        scores = (
            jnp.einsum("qhd,gkhd->hqgk", query_grid, key_grid, preferred_element_type=jnp.float32)
            * scaling
        )
        member = block_g[:, None] == jnp.arange(G, dtype=jnp.int32)[None, :]
        scores = jnp.where(member[None, :, :, None], scores, NEG)
        maxima = jnp.max(scores, axis=(2, 3))
        exp_terms = jnp.exp(scores - maxima[:, :, None, None])
        totals = jnp.sum(exp_terms, axis=(2, 3))
        weighted = jnp.einsum(
            "hqgk,gkhd->qhd",
            exp_terms.astype(jnp.bfloat16),
            val_grid,
            preferred_element_type=jnp.float32,
        )
        return (weighted.reshape(block_len, columns), maxima.T, totals.T)

    weighted, maxima, totals = lax.map(
        per_block,
        (query_rows.reshape(blocks, block_len, columns), query_group.reshape(blocks, block_len)),
    )
    return (
        weighted.reshape(row_count, columns),
        maxima.reshape(row_count, head_count),
        totals.reshape(row_count, head_count),
    )


def attend_suffix(queries, keys, values, request, position):
    row_count, columns = queries.shape
    head_count = columns // HEAD
    blocks = split_blocks(row_count)
    block_len = row_count // blocks
    scaling = 1.0 / math.sqrt(HEAD)
    key_grid = keys.reshape(row_count, head_count, HEAD)
    val_grid = values.reshape(row_count, head_count, HEAD)

    def per_block(pieces):
        block_q, block_req, block_pos = pieces
        query_grid = block_q.reshape(block_len, head_count, HEAD)
        scores = (
            jnp.einsum("qhd,khd->hqk", query_grid, key_grid, preferred_element_type=jnp.float32)
            * scaling
        )
        allowed = (request[None, :] == block_req[:, None]) & (
            position[None, :] <= block_pos[:, None]
        )
        scores = jnp.where(allowed[None, :, :], scores, NEG)
        maxima = jnp.max(scores, axis=2)
        exp_terms = jnp.exp(scores - maxima[:, :, None])
        totals = jnp.sum(exp_terms, axis=2)
        weighted = jnp.einsum(
            "hqk,khd->qhd",
            exp_terms.astype(jnp.bfloat16),
            val_grid,
            preferred_element_type=jnp.float32,
        )
        return (weighted.reshape(block_len, columns), maxima.T, totals.T)

    weighted, maxima, totals = lax.map(
        per_block,
        (
            queries.reshape(blocks, block_len, columns),
            request.reshape(blocks, block_len),
            position.reshape(blocks, block_len),
        ),
    )
    return (
        weighted.reshape(row_count, columns),
        maxima.reshape(row_count, head_count),
        totals.reshape(row_count, head_count),
    )


def combine(former, latter):
    weighted_a, maxima_a, totals_a = former
    weighted_b, maxima_b, totals_b = latter
    row_count, head_count = maxima_a.shape
    maxima = jnp.maximum(maxima_a, maxima_b)
    factor_a = jnp.exp(maxima_a - maxima)
    factor_b = jnp.exp(maxima_b - maxima)
    weighted = (
        weighted_a.reshape(row_count, head_count, HEAD) * factor_a[:, :, None]
        + weighted_b.reshape(row_count, head_count, HEAD) * factor_b[:, :, None]
    )
    return (
        weighted.reshape(row_count, head_count * HEAD),
        maxima,
        totals_a * factor_a + totals_b * factor_b,
    )


def general_device(
    queries,
    keys,
    values,
    prefix_keys,
    prefix_values,
    lengths,
    groups,
    residual,
    out_proj,
    norm_gain,
    expert_ids,
    expert_gates,
    w_gate,
    w_up,
    w_down,
):
    row_tok, columns = queries.shape
    head_count = columns // HEAD
    tok_dev = residual.shape[0]
    request, position, tok_group = token_layout(lengths, groups)
    request, position, tok_group = (request[0], position[0], tok_group[0])
    all_groups = lax.all_gather(tok_group, "req", axis=0, tiled=True)
    partial_value = pack_parts(
        attend_prefix(
            lax.all_gather(queries, "req", axis=0, tiled=True),
            all_groups,
            prefix_keys,
            prefix_values,
        )
    )
    returned = lax.all_to_all(partial_value, "req", split_axis=0, concat_axis=0, tiled=True)
    owners = returned.shape[0] // row_tok
    back_w, back_m, back_t = unpack_parts(returned, head_count)
    all_weighted = back_w.reshape(owners, row_tok, head_count, HEAD)
    all_maxima = back_m.reshape(owners, row_tok, head_count)
    all_totals = back_t.reshape(owners, row_tok, head_count)
    maxima = jnp.max(all_maxima, axis=0)
    factor = jnp.exp(all_maxima - maxima[None])
    weighted = jnp.sum(all_weighted * factor[..., None], axis=0).reshape(row_tok, columns)
    prefix_part = (weighted, maxima, jnp.sum(all_totals * factor, axis=0))
    suffix_part = attend_suffix(queries, keys, values, request, position)
    weighted, maxima, totals = combine(prefix_part, suffix_part)
    attended = (
        (weighted.reshape(row_tok, head_count, HEAD) / totals[:, :, None])
        .reshape(row_tok, columns)
        .astype(jnp.bfloat16)
    )
    projected = lax.psum_scatter(
        jnp.dot(attended, out_proj, preferred_element_type=jnp.float32),
        "exp",
        scatter_dimension=0,
        tiled=True,
    )
    stream = residual.astype(jnp.float32) + projected
    meansq = jnp.mean(stream * stream, axis=-1, keepdims=True)
    normed = (stream * lax.rsqrt(meansq + 1e-06) * norm_gain.astype(jnp.float32)).astype(
        jnp.bfloat16
    )
    capacity = max(2, tok_dev // 4)
    flat_ids = expert_ids.reshape(-1)
    onehot = (flat_ids[:, None] == jnp.arange(EXPERTS, dtype=jnp.int32)[None, :]).astype(jnp.int32)
    slot_of = jnp.sum(onehot * (jnp.cumsum(onehot, axis=0) - 1), axis=1)
    source_rows = jnp.arange(tok_dev * TOPK, dtype=jnp.int32) // TOPK
    buffer = (
        jnp.zeros((EXPERTS, capacity, normed.shape[1]), jnp.bfloat16)
        .at[flat_ids, slot_of]
        .set(normed[source_rows])
    )
    exp_count = lax.axis_size("exp")
    exp_dev = w_gate.shape[0]
    received = lax.all_to_all(buffer, "exp", split_axis=0, concat_axis=0, tiled=True)
    slots = received.shape[1]
    grid_in = received.reshape(exp_count, exp_dev, slots, received.shape[2])
    gate_h = jnp.einsum("secd,edf->secf", grid_in, w_gate, preferred_element_type=jnp.float32)
    up_h = jnp.einsum("secd,edf->secf", grid_in, w_up, preferred_element_type=jnp.float32)
    hidden = (jax.nn.silu(gate_h) * up_h).astype(jnp.bfloat16)
    expert_out = jnp.einsum("secf,efd->secd", hidden, w_down, preferred_element_type=jnp.float32)
    returned = lax.all_to_all(
        expert_out.reshape(EXPERTS, slots, received.shape[2]),
        "exp",
        split_axis=0,
        concat_axis=0,
        tiled=True,
    )
    gathered = returned[flat_ids, slot_of] * expert_gates.reshape(-1).astype(jnp.float32)[:, None]
    mixture = jnp.sum(gathered.reshape(tok_dev, TOPK, gathered.shape[1]), axis=1)
    return (stream + mixture).astype(jnp.bfloat16)


BLK = 128
LOG2E = 1.4426950408889634
SCORE_SCALE = LOG2E / math.sqrt(HEAD)
VMEM_BIG = 56 * 1024 * 1024


def core_swap(array):
    return lax.ppermute(array, "req", [(i, i ^ 1) for i in range(4)])


def x_swap(array):
    return lax.ppermute(array, "req", [(i, i ^ 2) for i in range(4)])


def y_swap(array):
    return lax.ppermute(array, "exp", [(i, i ^ 1) for i in range(8)])


def z_swap(array, distance):
    return lax.ppermute(array, "exp", [(i, i ^ (2 * distance)) for i in range(8)])


def split_kernel(sc_ref, q, k, v, pk, pv, out_tokens, out_prefix):
    for i, part in enumerate((q, k, v)):
        out_tokens[i] = part[...]
    out_prefix[0] = pk[...]
    out_prefix[1] = pv[...]


def split_theirs(place, q, k, v, pk, pv):
    rows, span = q.shape[0], pk.shape[1]
    part = rows // G
    tokens = pl.BlockSpec((part, HEAD), lambda i, s: (i, 1 - s[0]))
    prefix = pl.BlockSpec((1, span, HEAD), lambda i, s: (i, 0, 1 - s[0]))
    return pl.pallas_call(
        split_kernel,
        grid_spec=pltpu.PrefetchScalarGridSpec(
            num_scalar_prefetch=1,
            grid=(G,),
            in_specs=[tokens] * 3 + [prefix] * 2,
            out_specs=[
                pl.BlockSpec((3, part, HEAD), lambda i, s: (0, i, 0)),
                pl.BlockSpec((2, 1, span, HEAD), lambda i, s: (0, i, 0, 0)),
            ],
        ),
        out_shape=(
            jax.ShapeDtypeStruct((3, rows, HEAD), q.dtype),
            jax.ShapeDtypeStruct((2, G, span, HEAD), q.dtype),
        ),
        name="split_theirs",
    )(place, q, k, v, pk, pv)


def as_row(column):
    return jnp.transpose(jnp.broadcast_to(column, (BLK, BLK)))[0:1, :]


SUF = 256
SUB = 32
PER_ITEM = 8
ITEMS = 16


def build_work(shapes, item_group, item_block):
    per_row = ROW_TOK // SUB
    spans = []
    for r, (shape, at) in enumerate(shapes):
        start = 0
        for j in range(RQ):
            end = start + shape[at, j]
            first, last = r * per_row + start // SUB, r * per_row + (end - 1) // SUB
            spans.append((first, last, shape[at, RQ + j]))
            start = end

    def of_group(g, begin):
        at, done = begin, jnp.int32(-1)
        for first, last, group in spans:
            first = jnp.maximum(first, done + 1)
            match = group == g
            count = jnp.where(match, last - first + 1, 0)

            def put(i, carry, at=at, first=first):
                item_block[at + i] = first + i
                return carry

            lax.fori_loop(0, count, put, 0)
            at = at + count
            done = jnp.where(match, last, done)
        stop = (at + PER_ITEM - 1) // PER_ITEM * PER_ITEM

        def fill(i, carry):
            item_block[i] = item_block[begin]
            return carry

        def name(i, carry):
            item_group[i] = g
            return carry

        lax.fori_loop(at, stop, fill, 0)
        lax.fori_loop(begin // PER_ITEM, stop // PER_ITEM, name, 0)
        return stop

    return lax.fori_loop(0, G, of_group, jnp.int32(0)) // PER_ITEM


def prefix_kernel(
    far, sc_ref, shape_a, shape_b, q0, q1, pk, pv, other, o_ref, lse_ref,
    q_ref, ka, kb, va, vb, grp, lse, sa, sb, ta, tb, item_group, item_block, sems,
):
    tokens = q_ref.shape[0]
    span = ka.shape[1]
    shapes = ((shape_a, 0), (shape_b, far))
    mine = pl.ds(pl.multiple_of(sc_ref[0] * HEAD, HEAD), HEAD)
    copies = [
        pltpu.make_async_copy(q0.at[:, mine], q_ref.at[:ROW_TOK, :], sems.at[0]),
        pltpu.make_async_copy(q1, q_ref.at[ROW_TOK:, :], sems.at[1]),
        pltpu.make_async_copy(pk.at[:, :, mine], ka, sems.at[2]),
        pltpu.make_async_copy(other.at[0], kb, sems.at[3]),
        pltpu.make_async_copy(pv.at[:, :, mine], va, sems.at[4]),
        pltpu.make_async_copy(other.at[1], vb, sems.at[5]),
    ]
    for copy in copies:
        copy.start()
    for r, (shape, at) in enumerate(shapes):
        token = lax.broadcasted_iota(jnp.int32, (ROW_TOK, HEAD), 0)
        group = jnp.full((ROW_TOK, HEAD), shape[at, RQ], jnp.int32)
        start = 0
        for j in range(1, RQ):
            start = start + shape[at, j - 1]
            group = jnp.where(token >= start, shape[at, RQ + j], group)
        grp[r * ROW_TOK : (r + 1) * ROW_TOK, :] = group
    count = build_work(shapes, item_group, item_block)
    for copy in copies:
        copy.wait()
    step = 512

    def held(item):
        return jnp.where(item < count, item, 0)

    def places(item):
        at = held(item) * PER_ITEM
        return [
            pl.ds(pl.multiple_of(item_block[at + i] * SUB, SUB), SUB) for i in range(PER_ITEM)
        ]

    def group_of(item):
        return item_group[held(item)]

    def lanes(x, op):
        parts = [x[:, c : c + HEAD] for c in range(0, x.shape[1], HEAD)]
        while len(parts) > 1:
            parts = [op(a, b) for a, b in zip(parts[::2], parts[1::2])]
        return parts[0]

    def score(item, s, tops):
        g = group_of(item)
        q = jnp.concatenate([q_ref[place, :] for place in places(item)], axis=0)
        for half, k in enumerate((ka, kb)):
            for c in range(0, span, step):
                x = lax.dot_general(
                    q,
                    k[g, c : c + step, :],
                    (((1,), (1,)), ((), ())),
                    preferred_element_type=jnp.float32,
                )
                s[:, half * span + c : half * span + c + step] = x
                top = lanes(x, jnp.maximum)
                tops[...] = top if half == 0 and c == 0 else jnp.maximum(tops[...], top)

    def weigh(item, s, tops):
        g = group_of(item)
        where = places(item)
        for part in range(2):
            here = slice(part * BLK, (part + 1) * BLK)
            top = jnp.max(tops[here, :], axis=1, keepdims=True)
            out = jnp.zeros((BLK, HEAD), jnp.float32)
            total = jnp.zeros((BLK, HEAD), jnp.float32)
            for half, v in enumerate((va, vb)):
                for c in range(0, span, step):
                    x = s[here, half * span + c : half * span + c + step]
                    p = jnp.exp2((x - top) * SCORE_SCALE)
                    total = total + lanes(p, jnp.add)
                    out = out + jnp.dot(
                        p.astype(jnp.bfloat16),
                        v[g, c : c + step, :],
                        preferred_element_type=jnp.float32,
                    )
            total = jnp.sum(total, axis=1, keepdims=True)
            out = out * (1.0 / total)
            here_lse = jnp.broadcast_to(top * SCORE_SCALE + jnp.log2(total), (BLK, HEAD))
            for i in range(BLK // SUB):
                place = where[part * (BLK // SUB) + i]
                sub = slice(i * SUB, (i + 1) * SUB)
                mine = grp[place, :] == g
                o_ref[place, :] = jnp.where(
                    mine, out[sub], o_ref[place, :].astype(jnp.float32)
                ).astype(o_ref.dtype)
                lse[place, :] = jnp.where(mine, here_lse[sub], lse[place, :])

    score(0, sa, ta)

    def pair(i, carry):
        score(2 * i + 1, sb, tb)
        weigh(2 * i, sa, ta)
        score(2 * i + 2, sa, ta)
        weigh(2 * i + 1, sb, tb)
        return carry

    lax.fori_loop(0, (count + 1) // 2, pair, 0)
    for b in range(tokens // BLK):
        lse_ref[b // 8, b % 8 : b % 8 + 1, :] = jnp.transpose(lse[b * BLK : (b + 1) * BLK, :])[
            0:1, :
        ]


def prefix_attend(place, far, shape_a, shape_b, q0, q1, pk, pv, other, out_dtype):
    rows = 2
    tokens = rows * ROW_TOK
    span = pk.shape[1]
    blocks = ROW_TOK // BLK
    smem = pl.BlockSpec(memory_space=pltpu.SMEM)
    vmem = pl.BlockSpec(memory_space=pltpu.VMEM)
    anywhere = pl.BlockSpec(memory_space=pl.ANY)
    prefix_buffer = pltpu.VMEM((G, span, HEAD), pk.dtype)
    per_token = pltpu.VMEM((tokens, HEAD), jnp.float32)
    scores = pltpu.VMEM((PER_ITEM * SUB, 2 * span), jnp.float32)
    tops = pltpu.VMEM((PER_ITEM * SUB, HEAD), jnp.float32)
    return pl.pallas_call(
        functools.partial(prefix_kernel, far),
        in_specs=[smem] * 3 + [anywhere] * 5,
        out_specs=(vmem, vmem),
        out_shape=(
            jax.ShapeDtypeStruct((tokens, HEAD), out_dtype),
            jax.ShapeDtypeStruct((rows, blocks, BLK), jnp.float32),
        ),
        scratch_shapes=[
            pltpu.VMEM((tokens, HEAD), q0.dtype),
            prefix_buffer,
            prefix_buffer,
            prefix_buffer,
            prefix_buffer,
            pltpu.VMEM((tokens, HEAD), jnp.int32),
            per_token,
            scores,
            scores,
            tops,
            tops,
            pltpu.SMEM((ITEMS,), jnp.int32),
            pltpu.SMEM((ITEMS * PER_ITEM,), jnp.int32),
            pltpu.SemaphoreType.DMA((6,)),
        ],
        compiler_params=pltpu.CompilerParams(vmem_limit_bytes=VMEM_BIG),
        cost_estimate=pl.CostEstimate(
            flops=tokens * span * HEAD * 8 * 4,
            bytes_accessed=4 * G * span * HEAD * 2,
            transcendentals=0,
        ),
        name="prefix_attend",
    )(place, shape_a, shape_b, q0, q1, pk, pv, other)


def suffix_kernel(sc_ref, shape_a, shape_b, q, k, v, other_row, o_ref, lse_ref):
    count = ROW_TOK // SUF
    rows = ((shape_a, (q, k, v)), (shape_b, [other_row.at[i] for i in range(3)]))
    for row, (shape, qkv) in enumerate(rows):
        token = lax.broadcasted_iota(jnp.int32, (ROW_TOK, 1), 0)
        first = jnp.zeros((ROW_TOK, 1), jnp.int32)
        start = 0
        for j in range(1, RQ):
            start = start + shape[0, j - 1]
            first = jnp.where(token >= start, start, first)

        def bounds(i):
            low = max(0, i * SUF - ROW_TOK // 2)
            return low, slice(i * SUF, (i + 1) * SUF), slice(low, (i + 1) * SUF)

        def score(i, qkv=qkv, first=first, token=token):
            low, here, seen = bounds(i)
            s = lax.dot_general(
                qkv[0][here, :],
                qkv[1][seen, :],
                (((1,), (1,)), ((), ())),
                preferred_element_type=jnp.float32,
            )
            other = low + lax.broadcasted_iota(jnp.int32, s.shape, 1)
            return jnp.where((other >= first[here]) & (other <= token[here]), s, NEG)

        def weigh(i, s, row=row, qkv=qkv):
            unused, here, seen = bounds(i)
            top = jnp.max(s, axis=1, keepdims=True)
            p = jnp.exp2((s - top) * SCORE_SCALE)
            total = jnp.sum(p, axis=1, keepdims=True)
            out = jnp.dot(
                p.astype(jnp.bfloat16), qkv[2][seen, :], preferred_element_type=jnp.float32
            )
            o_ref[row * ROW_TOK + i * SUF : row * ROW_TOK + (i + 1) * SUF, :] = out * (1.0 / total)
            lse = top * SCORE_SCALE + jnp.log2(total)
            for part in range(SUF // BLK):
                at = i * (SUF // BLK) + part
                lse_ref[row, at : at + 1, :] = as_row(lse[part * BLK : (part + 1) * BLK])

        held = score(0)
        for i in range(count):
            later = score(i + 1) if i + 1 < count else None
            weigh(i, held)
            held = later


def suffix_attend(place, shape_a, shape_b, q, k, v, other):
    rows, tokens = 2, q.shape[0]
    blocks = tokens // BLK
    smem = pl.BlockSpec(memory_space=pltpu.SMEM)
    mine = pl.BlockSpec((tokens, HEAD), lambda i, s: (0, s[0]))
    return pl.pallas_call(
        suffix_kernel,
        grid_spec=pltpu.PrefetchScalarGridSpec(
            num_scalar_prefetch=1,
            grid=(1,),
            in_specs=[smem, smem]
            + [mine] * 3
            + [pl.BlockSpec((3, tokens, HEAD), lambda i, s: (0, 0, 0))],
            out_specs=[
                pl.BlockSpec((rows * tokens, HEAD), lambda i, s: (0, 0)),
                pl.BlockSpec((rows, blocks, BLK), lambda i, s: (0, 0, 0)),
            ],
        ),
        out_shape=(
            jax.ShapeDtypeStruct((rows * tokens, HEAD), jnp.float32),
            jax.ShapeDtypeStruct((rows, blocks, BLK), jnp.float32),
        ),
        compiler_params=pltpu.CompilerParams(vmem_limit_bytes=VMEM_BIG),
        cost_estimate=pl.CostEstimate(
            flops=rows * tokens * tokens * HEAD * 4 * 4, bytes_accessed=1 << 20, transcendentals=0
        ),
        name="suffix_attend",
    )(place, shape_a, shape_b, q, k, v, other)


MERGE_BLOCKS = 4


def merge_kernel(*refs):
    parts, tab_ref, out_ref = refs[:-2], refs[-2], refs[-1]
    step = pl.program_id(0)
    for block in range(MERGE_BLOCKS):
        out_ref[block, 2 * BLK :, :] = tab_ref[...]
    half = len(parts) // 2
    for row in range(2):
        sources = parts[row * half : (row + 1) * half]
        for block in range(MERGE_BLOCKS):
            here = slice(block * BLK, (block + 1) * BLK)
            at = pl.ds(step * MERGE_BLOCKS + block, 1)
            lses = [
                jnp.transpose(jnp.broadcast_to(lse[0, at, :], (BLK, BLK))) for lse in sources[1::2]
            ]
            top = lses[0]
            for lse in lses[1:]:
                top = jnp.maximum(top, lse)
            total, summed = 0.0, 0.0
            for lse, o in zip(lses, sources[0::2]):
                weight = jnp.exp2(lse - top)
                total = total + weight
                summed = summed + weight * o[here, :].astype(jnp.float32)
            out_ref[block, row * BLK : (row + 1) * BLK, :] = (summed / total).astype(out_ref.dtype)


def merge_parts(parts, tab):
    extra = tab.shape[0]
    blocks = ROW_TOK // BLK
    steps = blocks // MERGE_BLOCKS
    specs, operands = [], []
    for row in range(2):
        for o, lse in parts:
            operands += [o, lse]
            specs += [
                pl.BlockSpec((MERGE_BLOCKS * BLK, HEAD), lambda b, row=row: (row * steps + b, 0)),
                pl.BlockSpec((1, blocks, BLK), lambda b, row=row: (row, 0, 0)),
            ]
    return pl.pallas_call(
        merge_kernel,
        grid=(steps,),
        in_specs=specs + [pl.BlockSpec((extra, BLK), lambda b: (0, 0))],
        out_specs=pl.BlockSpec((MERGE_BLOCKS, 2 * BLK + extra, HEAD), lambda b: (b, 0, 0)),
        out_shape=jax.ShapeDtypeStruct((blocks, 2 * BLK + extra, HEAD), jnp.bfloat16),
        name="merge_parts",
    )(*operands, tab)


def project_kernel(a_ref, w_ref, keep_ref, send_ref, lhs):
    @pl.when(pl.program_id(0) == 0)
    def first():
        for h in range(a_ref.shape[0]):
            lhs[:, h * HEAD : (h + 1) * HEAD] = a_ref[h, : 2 * BLK, :]

    out = jnp.dot(lhs[...], w_ref[...], preferred_element_type=jnp.float32)
    rows = keep_ref.shape[0]
    keep_ref[...] = out[:rows]
    send_ref[...] = out[rows:].astype(send_ref.dtype)


def project(attended, weights):
    heads, held, unused = attended.shape
    tokens = 2 * BLK
    depth, width = weights.shape
    rows, tile = tokens // 2, 1024
    out_spec = pl.BlockSpec((rows, tile), lambda i: (0, i))
    return pl.pallas_call(
        project_kernel,
        grid=(width // tile,),
        in_specs=[
            pl.BlockSpec((heads, held, HEAD), lambda i: (0, 0, 0)),
            pl.BlockSpec((depth, tile), lambda i: (0, i)),
        ],
        out_specs=[out_spec, out_spec],
        out_shape=(
            jax.ShapeDtypeStruct((rows, width), jnp.float32),
            jax.ShapeDtypeStruct((rows, width), jnp.bfloat16),
        ),
        scratch_shapes=[pltpu.VMEM((tokens, depth), jnp.bfloat16)],
        compiler_params=pltpu.CompilerParams(vmem_limit_bytes=VMEM_BIG),
        name="project",
    )(attended, weights)


def norm_kernel(keep, got, residual, gain, stream_ref, normed_ref):
    stream = residual[...].astype(jnp.float32) + (keep[...] + got[...].astype(jnp.float32))
    meansq = jnp.mean(stream * stream, axis=-1, keepdims=True)
    stream_ref[...] = stream
    normed = stream * lax.rsqrt(meansq + 1e-06) * gain[...].astype(jnp.float32)
    normed_ref[...] = normed.astype(normed_ref.dtype)


def norm_rows(keep, got, residual, gain):
    return pl.pallas_call(
        norm_kernel,
        out_shape=(
            jax.ShapeDtypeStruct(keep.shape, jnp.float32),
            jax.ShapeDtypeStruct(keep.shape, jnp.bfloat16),
        ),
        name="norm_rows",
    )(keep, got, residual, gain)


EXP_DEV = 4
SLOTS = 32
SLOTS_XOR = (0, 2, 4, 6, 1, 3, 5, 7)


def route_kernel(sc_ref, tab_ref, pick_ref, give_ref):
    before = (
        lax.broadcasted_iota(jnp.int32, (BLK, BLK), 0)
        < lax.broadcasted_iota(jnp.int32, (BLK, BLK), 1)
    ).astype(jnp.bfloat16)
    place = lax.broadcasted_iota(jnp.int32, (SLOTS, BLK), 0).astype(jnp.float32)
    place_here = sc_ref[1]
    for slot, offset in enumerate(SLOTS_XOR):
        tab = tab_ref[place_here ^ offset].astype(jnp.float32)
        ids, gates = tab[:TOPK], tab[TOPK : 2 * TOPK]
        chosen, weights = [], []
        for j in range(EXP_DEV):
            match = ids == (place_here * EXP_DEV + j).astype(jnp.float32)
            chosen.append(jnp.sum(match.astype(jnp.float32), axis=0, keepdims=True))
            weights.append(jnp.sum(jnp.where(match, gates, 0.0), axis=0, keepdims=True))
        held = jnp.concatenate(chosen + chosen, axis=0)
        places = jnp.dot(held.astype(jnp.bfloat16), before, preferred_element_type=jnp.float32)
        places = jnp.where(held > 0.5, places, -1.0)
        hits = [place == places[j : j + 1] for j in range(EXP_DEV)]
        pick_ref[slot] = jnp.concatenate(
            [hit.astype(jnp.float32) for hit in hits], axis=0
        ).astype(jnp.bfloat16)
        spread = jnp.concatenate(
            [jnp.where(hit, weight, 0.0) for hit, weight in zip(hits, weights)], axis=0
        )
        give_ref[slot] = jnp.transpose(spread).astype(jnp.bfloat16)


def route(place, heads):
    extra = heads.shape[1] - 2 * BLK
    shape = jax.ShapeDtypeStruct((8, BLK, EXP_DEV * SLOTS), jnp.bfloat16)
    return pl.pallas_call(
        route_kernel,
        grid=(1,),
        in_specs=[
            pl.BlockSpec(memory_space=pltpu.SMEM),
            pl.BlockSpec((8, extra, BLK), lambda i: (0, 2 * BLK // extra, 0)),
        ],
        out_specs=[pl.BlockSpec((8, BLK, BLK), lambda i: (0, 0, 0))] * 2,
        out_shape=(shape, shape),
        name="route",
    )(place, heads)


def experts_kernel(*refs):
    picked = refs[:8]
    give_ref, wg, wu, wd = refs[8:12]
    outs, rows_out = refs[12:-1], refs[-1]
    expert = pl.program_id(0)
    rows = jnp.concatenate([part[...] for part in picked], axis=0)
    contract = (((1,), (1,)), ((), ()))
    gate_h = lax.dot_general(rows, wg[0], contract, preferred_element_type=jnp.float32)
    up_h = lax.dot_general(rows, wu[0], contract, preferred_element_type=jnp.float32)
    hidden = (gate_h / (1.0 + jnp.exp(-gate_h)) * up_h).astype(jnp.bfloat16)
    out = jnp.dot(hidden, wd[0], preferred_element_type=jnp.float32).astype(jnp.bfloat16)
    here = pl.ds(pl.multiple_of(expert * SLOTS, SLOTS), SLOTS)
    for slot in range(8):
        rows_out[slot, here, :] = out[slot * SLOTS : (slot + 1) * SLOTS]

    @pl.when(expert == EXP_DEV - 1)
    def last():
        for slot in range(8):
            out = jnp.dot(give_ref[slot], rows_out[slot], preferred_element_type=jnp.float32)
            out = out.astype(jnp.bfloat16)
            at = slot + slot // 4
            if slot % 4 < 3:
                outs[at][...] = out
            else:
                outs[at][...] = out[: BLK // 2]
                outs[at + 1][...] = out[BLK // 2 :]


def run_experts(picked, give, w_gate, w_up, w_down):
    width = picked[0].shape[1]
    hidden = w_down.shape[1]
    once = pl.Buffered(1)
    heights = ([BLK] * 3 + [BLK // 2] * 2) * 2
    return pl.pallas_call(
        experts_kernel,
        grid=(EXP_DEV,),
        in_specs=[pl.BlockSpec((SLOTS, width), lambda j: (j, 0))] * 8
        + [pl.BlockSpec((8, BLK, BLK), lambda j: (0, 0, 0))]
        + [pl.BlockSpec((1, hidden, width), lambda j: (j, 0, 0))] * 3,
        out_specs=[pl.BlockSpec((n, width), lambda j: (0, 0), pipeline_mode=once) for n in heights],
        out_shape=[jax.ShapeDtypeStruct((n, width), jnp.bfloat16) for n in heights],
        scratch_shapes=[pltpu.VMEM((8, EXP_DEV * SLOTS, width), jnp.bfloat16)],
        compiler_params=pltpu.CompilerParams(vmem_limit_bytes=VMEM_BIG),
        name="experts",
    )(*picked, give, w_gate.transpose(0, 2, 1), w_up.transpose(0, 2, 1), w_down)


def gather_rows(own):
    half = own.shape[0] // 2
    there = [y_swap(own)]
    near = [z_swap(own, 1), z_swap(own, 2), z_swap(own[:half], 3), z_swap(own[half:], 3)]
    there += [y_swap(part) for part in near]
    return [own] + near, there


def pick_rows(pick, parts):
    half = parts[3].shape[0]
    picked = [jnp.dot(pick[i], parts[i], preferred_element_type=jnp.float32) for i in range(3)]
    picked.append(
        jnp.dot(pick[3][:, :half], parts[3], preferred_element_type=jnp.float32)
        + jnp.dot(pick[3][:, half:], parts[4], preferred_element_type=jnp.float32)
    )
    return [part.astype(jnp.bfloat16) for part in picked]


def scatter_sums(stream, own, there):
    def plus(a, b):
        return (a.astype(jnp.float32) + b.astype(jnp.float32)).astype(jnp.bfloat16)

    last = [z_swap(plus(own[i], y_swap(there[i])), 3) for i in (3, 4)]
    total = stream + jnp.concatenate(last, axis=0).astype(jnp.float32)
    for i in (2, 1):
        total = total + z_swap(plus(own[i], y_swap(there[i])), i).astype(jnp.float32)
    return total + own[0].astype(jnp.float32) + y_swap(there[0]).astype(jnp.float32)


def block_device(
    queries,
    keys,
    values,
    prefix_keys,
    prefix_values,
    lengths,
    groups,
    residual,
    out_proj,
    norm_gain,
    expert_ids,
    expert_gates,
    w_gate,
    w_up,
    w_down,
):
    core = lax.rem(lax.axis_index("req"), 2)
    place = jnp.stack([core, lax.axis_index("exp")]).astype(jnp.int32)

    far_queries = x_swap(queries)
    shape = jnp.concatenate([lengths, groups], axis=1)
    far_shape = x_swap(shape)
    other_shapes = core_swap(jnp.concatenate([shape, far_shape], axis=0))

    proj_rows = lax.dynamic_slice_in_dim(out_proj, core * HEAD, HEAD, 0)
    proj_rows = lax.all_gather(proj_rows, "exp", axis=0, tiled=True)

    theirs, prefix_theirs = split_theirs(place, queries, keys, values, prefix_keys, prefix_values)
    other, prefix_other = core_swap(theirs), core_swap(prefix_theirs)
    far_other = core_swap(jnp.where(core == 0, far_queries[:, HEAD:], far_queries[:, :HEAD]))

    def prefix(far, shape_a, q0, q1, dtype):
        return prefix_attend(
            place, far, shape_a, other_shapes, q0, q1, prefix_keys, prefix_values, prefix_other, dtype
        )

    tab = jnp.concatenate([expert_ids.T.astype(jnp.bfloat16), expert_gates.T], axis=0)
    tab = jnp.pad(tab, ((0, 16 - tab.shape[0]), (0, 0)))
    suffix = suffix_attend(place, shape, other_shapes, queries, keys, values, other)
    far = prefix(1, far_shape, far_queries, far_other, jnp.bfloat16)
    back = (x_swap(far[0]), x_swap(far[1]))
    near = prefix(0, shape, queries, other[0], jnp.float32)
    near_o, gain = lax.optimization_barrier((near[0], norm_gain.reshape(1, -1)))
    attended = merge_parts([suffix, (near_o, near[1]), back], tab)
    heads = lax.all_to_all(attended, "exp", split_axis=0, concat_axis=0, tiled=True)
    keep, send = project(heads, proj_rows)
    stream, normed = norm_rows(keep, core_swap(send), residual, gain)
    pick, give = route(place, heads)
    here, there = gather_rows(normed)
    picked = pick_rows(pick[:4], here) + pick_rows(pick[4:], there)
    sums = run_experts(picked, give, w_gate, w_up, w_down)
    return scatter_sums(stream, sums[:5], sums[5:]).astype(jnp.bfloat16)


def solution(mesh):
    in_specs = (
        P("req", "exp"),
        P("req", "exp"),
        P("req", "exp"),
        P(None, "req", "exp"),
        P(None, "req", "exp"),
        P("req", None),
        P("req", None),
        P(("req", "exp"), None),
        P("exp", None),
        P(),
        P(("req", "exp"), None),
        P(("req", "exp"), None),
        P("exp", None, None),
        P("exp", None, None),
        P("exp", None, None),
    )
    out_specs = P(("req", "exp"), None)
    blocked = mesh.shape["req"] == 4 and mesh.shape["exp"] == 8
    return jax.shard_map(
        block_device if blocked else general_device,
        mesh=mesh,
        in_specs=in_specs,
        out_specs=out_specs,
        check_vma=False,
    )
```

```python
import math

import jax
import jax.numpy as jnp
from jax import lax
from jax.experimental import pallas as pl
from jax.experimental.pallas import tpu as pltpu
from jax.sharding import PartitionSpec as P

HEAD = 128
TOPK = 4
EXPERTS = 32
G = 4
RQ = 8
ROW_TOK = 1024


NEG = -1e30


def token_layout(lengths, groups):
    req_ends = jnp.cumsum(lengths, axis=-1)
    starts = req_ends - lengths
    position = jnp.arange(ROW_TOK, dtype=jnp.int32)
    request = jnp.sum((position[None, :, None] >= req_ends[:, None, :]).astype(jnp.int32), axis=-1)
    onehot = request[:, :, None] == jnp.arange(RQ, dtype=jnp.int32)[None, None, :]
    first_tok = jnp.sum(jnp.where(onehot, starts[:, None, :], 0), axis=-1)
    tok_group = jnp.sum(jnp.where(onehot, groups[:, None, :], 0), axis=-1)
    return (request, position[None, :] - first_tok, tok_group)


def split_blocks(row_count):
    if row_count % 1024 == 0 and row_count > 1024:
        return row_count // 1024
    return 1


def pack_parts(parts):
    return jnp.concatenate([parts[0], parts[1], parts[2]], axis=1)


def unpack_parts(packed, head_count):
    columns = head_count * HEAD
    return (
        packed[:, :columns],
        packed[:, columns : columns + head_count],
        packed[:, columns + head_count :],
    )


def attend_prefix(query_rows, query_group, prefix_k, prefix_v):
    row_count, columns = query_rows.shape
    head_count = columns // HEAD
    span = prefix_k.shape[1]
    key_grid = prefix_k.reshape(G, span, head_count, HEAD)
    val_grid = prefix_v.reshape(G, span, head_count, HEAD)
    blocks = split_blocks(row_count)
    block_len = row_count // blocks
    scaling = 1.0 / math.sqrt(HEAD)

    def per_block(pieces):
        block_q, block_g = pieces
        query_grid = block_q.reshape(block_len, head_count, HEAD)
        scores = (
            jnp.einsum("qhd,gkhd->hqgk", query_grid, key_grid, preferred_element_type=jnp.float32)
            * scaling
        )
        member = block_g[:, None] == jnp.arange(G, dtype=jnp.int32)[None, :]
        scores = jnp.where(member[None, :, :, None], scores, NEG)
        maxima = jnp.max(scores, axis=(2, 3))
        exp_terms = jnp.exp(scores - maxima[:, :, None, None])
        totals = jnp.sum(exp_terms, axis=(2, 3))
        weighted = jnp.einsum(
            "hqgk,gkhd->qhd",
            exp_terms.astype(jnp.bfloat16),
            val_grid,
            preferred_element_type=jnp.float32,
        )
        return (weighted.reshape(block_len, columns), maxima.T, totals.T)

    weighted, maxima, totals = lax.map(
        per_block,
        (query_rows.reshape(blocks, block_len, columns), query_group.reshape(blocks, block_len)),
    )
    return (
        weighted.reshape(row_count, columns),
        maxima.reshape(row_count, head_count),
        totals.reshape(row_count, head_count),
    )


def attend_suffix(queries, keys, values, request, position):
    row_count, columns = queries.shape
    head_count = columns // HEAD
    blocks = split_blocks(row_count)
    block_len = row_count // blocks
    scaling = 1.0 / math.sqrt(HEAD)
    key_grid = keys.reshape(row_count, head_count, HEAD)
    val_grid = values.reshape(row_count, head_count, HEAD)

    def per_block(pieces):
        block_q, block_req, block_pos = pieces
        query_grid = block_q.reshape(block_len, head_count, HEAD)
        scores = (
            jnp.einsum("qhd,khd->hqk", query_grid, key_grid, preferred_element_type=jnp.float32)
            * scaling
        )
        allowed = (request[None, :] == block_req[:, None]) & (
            position[None, :] <= block_pos[:, None]
        )
        scores = jnp.where(allowed[None, :, :], scores, NEG)
        maxima = jnp.max(scores, axis=2)
        exp_terms = jnp.exp(scores - maxima[:, :, None])
        totals = jnp.sum(exp_terms, axis=2)
        weighted = jnp.einsum(
            "hqk,khd->qhd",
            exp_terms.astype(jnp.bfloat16),
            val_grid,
            preferred_element_type=jnp.float32,
        )
        return (weighted.reshape(block_len, columns), maxima.T, totals.T)

    weighted, maxima, totals = lax.map(
        per_block,
        (
            queries.reshape(blocks, block_len, columns),
            request.reshape(blocks, block_len),
            position.reshape(blocks, block_len),
        ),
    )
    return (
        weighted.reshape(row_count, columns),
        maxima.reshape(row_count, head_count),
        totals.reshape(row_count, head_count),
    )


def combine(former, latter):
    weighted_a, maxima_a, totals_a = former
    weighted_b, maxima_b, totals_b = latter
    row_count, head_count = maxima_a.shape
    maxima = jnp.maximum(maxima_a, maxima_b)
    factor_a = jnp.exp(maxima_a - maxima)
    factor_b = jnp.exp(maxima_b - maxima)
    weighted = (
        weighted_a.reshape(row_count, head_count, HEAD) * factor_a[:, :, None]
        + weighted_b.reshape(row_count, head_count, HEAD) * factor_b[:, :, None]
    )
    return (
        weighted.reshape(row_count, head_count * HEAD),
        maxima,
        totals_a * factor_a + totals_b * factor_b,
    )


def general_device(
    queries,
    keys,
    values,
    prefix_keys,
    prefix_values,
    lengths,
    groups,
    residual,
    out_proj,
    norm_gain,
    expert_ids,
    expert_gates,
    w_gate,
    w_up,
    w_down,
):
    row_tok, columns = queries.shape
    head_count = columns // HEAD
    tok_dev = residual.shape[0]
    request, position, tok_group = token_layout(lengths, groups)
    request, position, tok_group = (request[0], position[0], tok_group[0])
    all_groups = lax.all_gather(tok_group, "req", axis=0, tiled=True)
    partial_value = pack_parts(
        attend_prefix(
            lax.all_gather(queries, "req", axis=0, tiled=True),
            all_groups,
            prefix_keys,
            prefix_values,
        )
    )
    returned = lax.all_to_all(partial_value, "req", split_axis=0, concat_axis=0, tiled=True)
    owners = returned.shape[0] // row_tok
    back_w, back_m, back_t = unpack_parts(returned, head_count)
    all_weighted = back_w.reshape(owners, row_tok, head_count, HEAD)
    all_maxima = back_m.reshape(owners, row_tok, head_count)
    all_totals = back_t.reshape(owners, row_tok, head_count)
    maxima = jnp.max(all_maxima, axis=0)
    factor = jnp.exp(all_maxima - maxima[None])
    weighted = jnp.sum(all_weighted * factor[..., None], axis=0).reshape(row_tok, columns)
    prefix_part = (weighted, maxima, jnp.sum(all_totals * factor, axis=0))
    suffix_part = attend_suffix(queries, keys, values, request, position)
    weighted, maxima, totals = combine(prefix_part, suffix_part)
    attended = (
        (weighted.reshape(row_tok, head_count, HEAD) / totals[:, :, None])
        .reshape(row_tok, columns)
        .astype(jnp.bfloat16)
    )
    projected = lax.psum_scatter(
        jnp.dot(attended, out_proj, preferred_element_type=jnp.float32),
        "exp",
        scatter_dimension=0,
        tiled=True,
    )
    stream = residual.astype(jnp.float32) + projected
    meansq = jnp.mean(stream * stream, axis=-1, keepdims=True)
    normed = (stream * lax.rsqrt(meansq + 1e-06) * norm_gain.astype(jnp.float32)).astype(
        jnp.bfloat16
    )
    capacity = max(2, tok_dev // 4)
    flat_ids = expert_ids.reshape(-1)
    onehot = (flat_ids[:, None] == jnp.arange(EXPERTS, dtype=jnp.int32)[None, :]).astype(jnp.int32)
    slot_of = jnp.sum(onehot * (jnp.cumsum(onehot, axis=0) - 1), axis=1)
    source_rows = jnp.arange(tok_dev * TOPK, dtype=jnp.int32) // TOPK
    buffer = (
        jnp.zeros((EXPERTS, capacity, normed.shape[1]), jnp.bfloat16)
        .at[flat_ids, slot_of]
        .set(normed[source_rows])
    )
    exp_count = lax.axis_size("exp")
    exp_dev = w_gate.shape[0]
    received = lax.all_to_all(buffer, "exp", split_axis=0, concat_axis=0, tiled=True)
    slots = received.shape[1]
    grid_in = received.reshape(exp_count, exp_dev, slots, received.shape[2])
    gate_h = jnp.einsum("secd,edf->secf", grid_in, w_gate, preferred_element_type=jnp.float32)
    up_h = jnp.einsum("secd,edf->secf", grid_in, w_up, preferred_element_type=jnp.float32)
    hidden = (jax.nn.silu(gate_h) * up_h).astype(jnp.bfloat16)
    expert_out = jnp.einsum("secf,efd->secd", hidden, w_down, preferred_element_type=jnp.float32)
    returned = lax.all_to_all(
        expert_out.reshape(EXPERTS, slots, received.shape[2]),
        "exp",
        split_axis=0,
        concat_axis=0,
        tiled=True,
    )
    gathered = returned[flat_ids, slot_of] * expert_gates.reshape(-1).astype(jnp.float32)[:, None]
    mixture = jnp.sum(gathered.reshape(tok_dev, TOPK, gathered.shape[1]), axis=1)
    return (stream + mixture).astype(jnp.bfloat16)


BLK = 128
LOG2E = 1.4426950408889634
SCORE_SCALE = LOG2E / math.sqrt(HEAD)
VMEM_BIG = 56 * 1024 * 1024


def core_swap(array):
    return lax.ppermute(array, "req", [(i, i ^ 1) for i in range(4)])


def x_swap(array):
    return lax.ppermute(array, "req", [(i, i ^ 2) for i in range(4)])


def y_swap(array):
    return lax.ppermute(array, "exp", [(i, i ^ 1) for i in range(8)])


def outer_swap(array):
    return lax.ppermute(array, "exp", [(i, i ^ 2) for i in range(8)])


def middle_swap(array):
    return lax.ppermute(array, "exp", [(2, 4), (3, 5), (4, 2), (5, 3)])


def split_kernel(sc_ref, q, k, v, pk, pv, out_tokens, out_prefix):
    for i, part in enumerate((q, k, v)):
        out_tokens[i] = part[...]
    out_prefix[0] = pk[...]
    out_prefix[1] = pv[...]


def split_theirs(place, q, k, v, pk, pv):
    rows, span = q.shape[0], pk.shape[1]
    part = rows // G
    tokens = pl.BlockSpec((part, HEAD), lambda i, s: (i, 1 - s[0]))
    prefix = pl.BlockSpec((1, span, HEAD), lambda i, s: (i, 0, 1 - s[0]))
    return pl.pallas_call(
        split_kernel,
        grid_spec=pltpu.PrefetchScalarGridSpec(
            num_scalar_prefetch=1,
            grid=(G,),
            in_specs=[tokens] * 3 + [prefix] * 2,
            out_specs=[
                pl.BlockSpec((3, part, HEAD), lambda i, s: (0, i, 0)),
                pl.BlockSpec((2, 1, span, HEAD), lambda i, s: (0, i, 0, 0)),
            ],
        ),
        out_shape=(
            jax.ShapeDtypeStruct((3, rows, HEAD), q.dtype),
            jax.ShapeDtypeStruct((2, G, span, HEAD), q.dtype),
        ),
        name="split_theirs",
    )(place, q, k, v, pk, pv)


def as_row(column):
    return jnp.transpose(jnp.broadcast_to(column, (BLK, BLK)))[0:1, :]


SUF = 256
SUB = 32
PER_ITEM = 8
ITEMS = 16


def build_work(shapes, item_group, item_block):
    per_row = ROW_TOK // SUB
    spans = []
    for r, (shape, at) in enumerate(shapes):
        start = 0
        for j in range(RQ):
            end = start + shape[at, j]
            first, last = r * per_row + start // SUB, r * per_row + (end - 1) // SUB
            spans.append((first, last, shape[at, RQ + j]))
            start = end

    def of_group(g, begin):
        at, done = begin, jnp.int32(-1)
        for first, last, group in spans:
            first = jnp.maximum(first, done + 1)
            match = group == g
            count = jnp.where(match, last - first + 1, 0)

            def put(i, carry, at=at, first=first):
                item_block[at + i] = first + i
                return carry

            lax.fori_loop(0, count, put, 0)
            at = at + count
            done = jnp.where(match, last, done)
        stop = (at + PER_ITEM - 1) // PER_ITEM * PER_ITEM

        def fill(i, carry):
            item_block[i] = item_block[begin]
            return carry

        def name(i, carry):
            item_group[i] = g
            return carry

        lax.fori_loop(at, stop, fill, 0)
        lax.fori_loop(begin // PER_ITEM, stop // PER_ITEM, name, 0)
        return stop

    return lax.fori_loop(0, G, of_group, jnp.int32(0)) // PER_ITEM


def prefix_kernel(
    sc_ref, shape_a, shape_b, q0, q1, pk, pv, other, o_ref, lse_ref,
    q_ref, ka, kb, va, vb, grp, lse, sa, sb, ta, tb, item_group, item_block, sems,
):
    tokens = q_ref.shape[0]
    span = ka.shape[1]
    shapes = ((shape_a, 0), (shape_b, 0))
    mine = pl.ds(pl.multiple_of(sc_ref[0] * HEAD, HEAD), HEAD)
    copies = [
        pltpu.make_async_copy(q0.at[:, mine], q_ref.at[:ROW_TOK, :], sems.at[0]),
        pltpu.make_async_copy(q1.at[0], q_ref.at[ROW_TOK:, :], sems.at[1]),
        pltpu.make_async_copy(pk.at[:, :, mine], ka, sems.at[2]),
        pltpu.make_async_copy(other.at[0], kb, sems.at[3]),
        pltpu.make_async_copy(pv.at[:, :, mine], va, sems.at[4]),
        pltpu.make_async_copy(other.at[1], vb, sems.at[5]),
    ]
    for copy in copies:
        copy.start()
    for r, (shape, at) in enumerate(shapes):
        token = lax.broadcasted_iota(jnp.int32, (ROW_TOK, HEAD), 0)
        group = jnp.full((ROW_TOK, HEAD), shape[at, RQ], jnp.int32)
        start = 0
        for j in range(1, RQ):
            start = start + shape[at, j - 1]
            group = jnp.where(token >= start, shape[at, RQ + j], group)
        grp[r * ROW_TOK : (r + 1) * ROW_TOK, :] = group
    count = build_work(shapes, item_group, item_block)
    for copy in copies:
        copy.wait()
    step = 512

    def held(item):
        return jnp.where(item < count, item, 0)

    def places(item):
        at = held(item) * PER_ITEM
        return [
            pl.ds(pl.multiple_of(item_block[at + i] * SUB, SUB), SUB) for i in range(PER_ITEM)
        ]

    def group_of(item):
        return item_group[held(item)]

    def lanes(x, op):
        parts = [x[:, c : c + HEAD] for c in range(0, x.shape[1], HEAD)]
        while len(parts) > 1:
            parts = [op(a, b) for a, b in zip(parts[::2], parts[1::2])]
        return parts[0]

    def score(item, s, tops):
        g = group_of(item)
        q = jnp.concatenate([q_ref[place, :] for place in places(item)], axis=0)
        for half, k in enumerate((ka, kb)):
            for c in range(0, span, step):
                x = lax.dot_general(
                    q,
                    k[g, c : c + step, :],
                    (((1,), (1,)), ((), ())),
                    preferred_element_type=jnp.float32,
                )
                s[:, half * span + c : half * span + c + step] = x
                top = lanes(x, jnp.maximum)
                tops[...] = top if half == 0 and c == 0 else jnp.maximum(tops[...], top)

    def weigh(item, s, tops):
        g = group_of(item)
        where = places(item)
        for part in range(2):
            here = slice(part * BLK, (part + 1) * BLK)
            top = jnp.max(tops[here, :], axis=1, keepdims=True)
            out = jnp.zeros((BLK, HEAD), jnp.float32)
            total = jnp.zeros((BLK, HEAD), jnp.float32)
            for half, v in enumerate((va, vb)):
                for c in range(0, span, step):
                    x = s[here, half * span + c : half * span + c + step]
                    p = jnp.exp2((x - top) * SCORE_SCALE)
                    total = total + lanes(p, jnp.add)
                    out = out + jnp.dot(
                        p.astype(jnp.bfloat16),
                        v[g, c : c + step, :],
                        preferred_element_type=jnp.float32,
                    )
            total = jnp.sum(total, axis=1, keepdims=True)
            out = out * (1.0 / total)
            here_lse = jnp.broadcast_to(top * SCORE_SCALE + jnp.log2(total), (BLK, HEAD))
            for i in range(BLK // SUB):
                place = where[part * (BLK // SUB) + i]
                sub = slice(i * SUB, (i + 1) * SUB)
                mine = grp[place, :] == g
                o_ref[place, :] = jnp.where(
                    mine, out[sub], o_ref[place, :].astype(jnp.float32)
                ).astype(o_ref.dtype)
                lse[place, :] = jnp.where(mine, here_lse[sub], lse[place, :])

    score(0, sa, ta)

    def pair(i, carry):
        score(2 * i + 1, sb, tb)
        weigh(2 * i, sa, ta)
        score(2 * i + 2, sa, ta)
        weigh(2 * i + 1, sb, tb)
        return carry

    lax.fori_loop(0, (count + 1) // 2, pair, 0)
    for b in range(tokens // BLK):
        lse_ref[b // 8, b % 8 : b % 8 + 1, :] = jnp.transpose(lse[b * BLK : (b + 1) * BLK, :])[
            0:1, :
        ]


def prefix_attend(place, shape_a, shape_b, q0, q1, pk, pv, other, out_dtype):
    rows = 2
    tokens = rows * ROW_TOK
    span = pk.shape[1]
    blocks = ROW_TOK // BLK
    smem = pl.BlockSpec(memory_space=pltpu.SMEM)
    vmem = pl.BlockSpec(memory_space=pltpu.VMEM)
    anywhere = pl.BlockSpec(memory_space=pl.ANY)
    prefix_buffer = pltpu.VMEM((G, span, HEAD), pk.dtype)
    per_token = pltpu.VMEM((tokens, HEAD), jnp.float32)
    scores = pltpu.VMEM((PER_ITEM * SUB, 2 * span), jnp.float32)
    tops = pltpu.VMEM((PER_ITEM * SUB, HEAD), jnp.float32)
    return pl.pallas_call(
        prefix_kernel,
        in_specs=[smem] * 3 + [anywhere] * 5,
        out_specs=(vmem, vmem),
        out_shape=(
            jax.ShapeDtypeStruct((tokens, HEAD), out_dtype),
            jax.ShapeDtypeStruct((rows, blocks, BLK), jnp.float32),
        ),
        scratch_shapes=[
            pltpu.VMEM((tokens, HEAD), q0.dtype),
            prefix_buffer,
            prefix_buffer,
            prefix_buffer,
            prefix_buffer,
            pltpu.VMEM((tokens, HEAD), jnp.int32),
            per_token,
            scores,
            scores,
            tops,
            tops,
            pltpu.SMEM((ITEMS,), jnp.int32),
            pltpu.SMEM((ITEMS * PER_ITEM,), jnp.int32),
            pltpu.SemaphoreType.DMA((6,)),
        ],
        compiler_params=pltpu.CompilerParams(vmem_limit_bytes=VMEM_BIG),
        cost_estimate=pl.CostEstimate(
            flops=tokens * span * HEAD * 8 * 4,
            bytes_accessed=4 * G * span * HEAD * 2,
            transcendentals=0,
        ),
        name="prefix_attend",
    )(place, shape_a, shape_b, q0, q1, pk, pv, other)


def suffix_kernel(sc_ref, shape_a, shape_b, q, k, v, other_row, o_ref, lse_ref):
    count = ROW_TOK // SUF
    rows = ((shape_a, (q, k, v)), (shape_b, [other_row.at[i] for i in range(3)]))
    for row, (shape, qkv) in enumerate(rows):
        token = lax.broadcasted_iota(jnp.int32, (ROW_TOK, 1), 0)
        first = jnp.zeros((ROW_TOK, 1), jnp.int32)
        start = 0
        for j in range(1, RQ):
            start = start + shape[0, j - 1]
            first = jnp.where(token >= start, start, first)

        def bounds(i):
            low = max(0, i * SUF - ROW_TOK // 2)
            return low, slice(i * SUF, (i + 1) * SUF), slice(low, (i + 1) * SUF)

        def score(i, qkv=qkv, first=first, token=token):
            low, here, seen = bounds(i)
            s = lax.dot_general(
                qkv[0][here, :],
                qkv[1][seen, :],
                (((1,), (1,)), ((), ())),
                preferred_element_type=jnp.float32,
            )
            other = low + lax.broadcasted_iota(jnp.int32, s.shape, 1)
            return jnp.where((other >= first[here]) & (other <= token[here]), s, NEG)

        def weigh(i, s, row=row, qkv=qkv):
            unused, here, seen = bounds(i)
            top = jnp.max(s, axis=1, keepdims=True)
            p = jnp.exp2((s - top) * SCORE_SCALE)
            total = jnp.sum(p, axis=1, keepdims=True)
            out = jnp.dot(
                p.astype(jnp.bfloat16), qkv[2][seen, :], preferred_element_type=jnp.float32
            )
            o_ref[row * ROW_TOK + i * SUF : row * ROW_TOK + (i + 1) * SUF, :] = out * (1.0 / total)
            lse = top * SCORE_SCALE + jnp.log2(total)
            for part in range(SUF // BLK):
                at = i * (SUF // BLK) + part
                lse_ref[row, at : at + 1, :] = as_row(lse[part * BLK : (part + 1) * BLK])

        held = score(0)
        for i in range(count):
            later = score(i + 1) if i + 1 < count else None
            weigh(i, held)
            held = later


def suffix_attend(place, shape_a, shape_b, q, k, v, other):
    rows, tokens = 2, q.shape[0]
    blocks = tokens // BLK
    smem = pl.BlockSpec(memory_space=pltpu.SMEM)
    mine = pl.BlockSpec((tokens, HEAD), lambda i, s: (0, s[0]))
    return pl.pallas_call(
        suffix_kernel,
        grid_spec=pltpu.PrefetchScalarGridSpec(
            num_scalar_prefetch=1,
            grid=(1,),
            in_specs=[smem, smem]
            + [mine] * 3
            + [pl.BlockSpec((3, tokens, HEAD), lambda i, s: (0, 0, 0))],
            out_specs=[
                pl.BlockSpec((rows * tokens, HEAD), lambda i, s: (0, 0)),
                pl.BlockSpec((rows, blocks, BLK), lambda i, s: (0, 0, 0)),
            ],
        ),
        out_shape=(
            jax.ShapeDtypeStruct((rows * tokens, HEAD), jnp.float32),
            jax.ShapeDtypeStruct((rows, blocks, BLK), jnp.float32),
        ),
        compiler_params=pltpu.CompilerParams(vmem_limit_bytes=VMEM_BIG),
        cost_estimate=pl.CostEstimate(
            flops=rows * tokens * tokens * HEAD * 4 * 4, bytes_accessed=1 << 20, transcendentals=0
        ),
        name="suffix_attend",
    )(place, shape_a, shape_b, q, k, v, other)


MERGE_BLOCKS = 4


def merge_kernel(*refs):
    parts, tab_ref, out_ref = refs[:-2], refs[-2], refs[-1]
    step = pl.program_id(0)
    for block in range(MERGE_BLOCKS):
        out_ref[block, 2 * BLK :, :] = tab_ref[...]
    half = len(parts) // 2
    for row in range(2):
        sources = parts[row * half : (row + 1) * half]
        for block in range(MERGE_BLOCKS):
            here = slice(block * BLK, (block + 1) * BLK)
            at = pl.ds(step * MERGE_BLOCKS + block, 1)
            lses = [
                jnp.transpose(jnp.broadcast_to(lse[0, at, :], (BLK, BLK))) for lse in sources[1::2]
            ]
            top = lses[0]
            for lse in lses[1:]:
                top = jnp.maximum(top, lse)
            total, summed = 0.0, 0.0
            for lse, o in zip(lses, sources[0::2]):
                weight = jnp.exp2(lse - top)
                total = total + weight
                summed = summed + weight * o[here, :].astype(jnp.float32)
            out_ref[block, row * BLK : (row + 1) * BLK, :] = (summed / total).astype(out_ref.dtype)


def merge_parts(parts, tab):
    extra = tab.shape[0]
    blocks = ROW_TOK // BLK
    steps = blocks // MERGE_BLOCKS
    specs, operands = [], []
    for row in range(2):
        for o, lse in parts:
            operands += [o, lse]
            specs += [
                pl.BlockSpec((MERGE_BLOCKS * BLK, HEAD), lambda b, row=row: (row * steps + b, 0)),
                pl.BlockSpec((1, blocks, BLK), lambda b, row=row: (row, 0, 0)),
            ]
    return pl.pallas_call(
        merge_kernel,
        grid=(steps,),
        in_specs=specs + [pl.BlockSpec((extra, BLK), lambda b: (0, 0))],
        out_specs=pl.BlockSpec((MERGE_BLOCKS, 2 * BLK + extra, HEAD), lambda b: (b, 0, 0)),
        out_shape=jax.ShapeDtypeStruct((blocks, 2 * BLK + extra, HEAD), jnp.bfloat16),
        name="merge_parts",
    )(*operands, tab)


def project_kernel(a_ref, w_ref, keep_ref, send_ref, lhs):
    @pl.when(pl.program_id(0) == 0)
    def first():
        for h in range(a_ref.shape[0]):
            lhs[:, h * HEAD : (h + 1) * HEAD] = a_ref[h, : 2 * BLK, :]

    out = jnp.dot(lhs[...], w_ref[...], preferred_element_type=jnp.float32)
    rows = keep_ref.shape[0]
    keep_ref[...] = out[:rows]
    send_ref[...] = out[rows:].astype(send_ref.dtype)


def project(attended, weights):
    heads, held, unused = attended.shape
    tokens = 2 * BLK
    depth, width = weights.shape
    rows, tile = tokens // 2, 1024
    out_spec = pl.BlockSpec((rows, tile), lambda i: (0, i))
    return pl.pallas_call(
        project_kernel,
        grid=(width // tile,),
        in_specs=[
            pl.BlockSpec((heads, held, HEAD), lambda i: (0, 0, 0)),
            pl.BlockSpec((depth, tile), lambda i: (0, i)),
        ],
        out_specs=[out_spec, out_spec],
        out_shape=(
            jax.ShapeDtypeStruct((rows, width), jnp.float32),
            jax.ShapeDtypeStruct((rows, width), jnp.bfloat16),
        ),
        scratch_shapes=[pltpu.VMEM((tokens, depth), jnp.bfloat16)],
        compiler_params=pltpu.CompilerParams(vmem_limit_bytes=VMEM_BIG),
        name="project",
    )(attended, weights)


def norm_kernel(keep, got, residual, gain, stream_ref, normed_ref):
    stream = residual[...].astype(jnp.float32) + (keep[...] + got[...].astype(jnp.float32))
    meansq = jnp.mean(stream * stream, axis=-1, keepdims=True)
    stream_ref[...] = stream
    normed = stream * lax.rsqrt(meansq + 1e-06) * gain[...].astype(jnp.float32)
    normed_ref[...] = normed.astype(normed_ref.dtype)


def norm_rows(keep, got, residual, gain):
    return pl.pallas_call(
        norm_kernel,
        out_shape=(
            jax.ShapeDtypeStruct(keep.shape, jnp.float32),
            jax.ShapeDtypeStruct(keep.shape, jnp.bfloat16),
        ),
        name="norm_rows",
    )(keep, got, residual, gain)


EXP_DEV = 4
SLOTS = 32
SLOT_Z = ((0, 1, 2, 3), (1, 0, 3, 2), (2, 3, 0, 1), (3, 2, 1, 0))


def route_kernel(sc_ref, tab_ref, pick_ref, give_ref):
    before = (
        lax.broadcasted_iota(jnp.int32, (BLK, BLK), 0)
        < lax.broadcasted_iota(jnp.int32, (BLK, BLK), 1)
    ).astype(jnp.bfloat16)
    place = lax.broadcasted_iota(jnp.int32, (SLOTS, BLK), 0).astype(jnp.float32)
    place_here = sc_ref[1]
    here_z, here_y = place_here // 2, place_here % 2
    for slot in range(8):
        of = SLOT_Z[3][slot % 4]
        for z in range(3):
            of = jnp.where(here_z == z, SLOT_Z[z][slot % 4], of)
        tab = tab_ref[of * 2 + (here_y if slot < 4 else 1 - here_y)].astype(jnp.float32)
        ids, gates = tab[:TOPK], tab[TOPK : 2 * TOPK]
        chosen, weights = [], []
        for j in range(EXP_DEV):
            match = ids == (place_here * EXP_DEV + j).astype(jnp.float32)
            chosen.append(jnp.sum(match.astype(jnp.float32), axis=0, keepdims=True))
            weights.append(jnp.sum(jnp.where(match, gates, 0.0), axis=0, keepdims=True))
        held = jnp.concatenate(chosen + chosen, axis=0)
        places = jnp.dot(held.astype(jnp.bfloat16), before, preferred_element_type=jnp.float32)
        places = jnp.where(held > 0.5, places, -1.0)
        hits = [place == places[j : j + 1] for j in range(EXP_DEV)]
        pick_ref[slot] = jnp.concatenate(
            [hit.astype(jnp.float32) for hit in hits], axis=0
        ).astype(jnp.bfloat16)
        spread = jnp.concatenate(
            [jnp.where(hit, weight, 0.0) for hit, weight in zip(hits, weights)], axis=0
        )
        give_ref[slot] = jnp.transpose(spread).astype(jnp.bfloat16)


def route(place, heads):
    extra = heads.shape[1] - 2 * BLK
    shape = jax.ShapeDtypeStruct((8, BLK, EXP_DEV * SLOTS), jnp.bfloat16)
    return pl.pallas_call(
        route_kernel,
        grid=(1,),
        in_specs=[
            pl.BlockSpec(memory_space=pltpu.SMEM),
            pl.BlockSpec((8, extra, BLK), lambda i: (0, 2 * BLK // extra, 0)),
        ],
        out_specs=[pl.BlockSpec((8, BLK, BLK), lambda i: (0, 0, 0))] * 2,
        out_shape=(shape, shape),
        name="route",
    )(place, heads)


def experts_kernel(*refs):
    picked = refs[:8]
    give_ref, wg, wu, wd = refs[8:12]
    outs, rows_out = refs[12:-1], refs[-1]
    expert = pl.program_id(0)
    rows = jnp.concatenate([part[...] for part in picked], axis=0)
    contract = (((1,), (1,)), ((), ()))
    gate_h = lax.dot_general(rows, wg[0], contract, preferred_element_type=jnp.float32)
    up_h = lax.dot_general(rows, wu[0], contract, preferred_element_type=jnp.float32)
    hidden = (gate_h / (1.0 + jnp.exp(-gate_h)) * up_h).astype(jnp.bfloat16)
    out = jnp.dot(hidden, wd[0], preferred_element_type=jnp.float32).astype(jnp.bfloat16)
    here = pl.ds(pl.multiple_of(expert * SLOTS, SLOTS), SLOTS)
    for slot in range(8):
        rows_out[slot, here, :] = out[slot * SLOTS : (slot + 1) * SLOTS]

    @pl.when(expert == EXP_DEV - 1)
    def last():
        for slot in range(8):
            out = jnp.dot(give_ref[slot], rows_out[slot], preferred_element_type=jnp.float32)
            out = out.astype(jnp.bfloat16)
            if slot < 7:
                outs[slot][...] = out
            else:
                outs[7][...] = out[: BLK // 2]
                outs[8][...] = out[BLK // 2 :]


def run_experts(picked, give, w_gate, w_up, w_down):
    width = picked[0].shape[1]
    hidden = w_down.shape[1]
    once = pl.Buffered(1)
    heights = [BLK] * 7 + [BLK // 2] * 2
    return pl.pallas_call(
        experts_kernel,
        grid=(EXP_DEV,),
        in_specs=[pl.BlockSpec((SLOTS, width), lambda j: (j, 0))] * 8
        + [pl.BlockSpec((8, BLK, BLK), lambda j: (0, 0, 0))]
        + [pl.BlockSpec((1, hidden, width), lambda j: (j, 0, 0))] * 3,
        out_specs=[pl.BlockSpec((n, width), lambda j: (0, 0), pipeline_mode=once) for n in heights],
        out_shape=[jax.ShapeDtypeStruct((n, width), jnp.bfloat16) for n in heights],
        scratch_shapes=[pltpu.VMEM((8, EXP_DEV * SLOTS, width), jnp.bfloat16)],
        compiler_params=pltpu.CompilerParams(vmem_limit_bytes=VMEM_BIG),
        name="experts",
    )(*picked, give, w_gate.transpose(0, 2, 1), w_up.transpose(0, 2, 1), w_down)


def together(*arrays):
    return lax.optimization_barrier(arrays)


def gather_rows(middle, own):
    half = own.shape[0] // 2
    outer0, middle0, there0 = together(outer_swap(own), middle_swap(own), y_swap(own))
    outer1, middle1, there1 = together(
        outer_swap(middle0), middle_swap(outer0), y_swap(outer0)
    )
    second = jnp.where(middle, middle1, outer1)
    outer2, there2 = together(outer_swap(middle1), y_swap(second))
    third = jnp.where(middle, middle0, outer2)
    there3, late_outer, late_middle = together(
        y_swap(third[:half]), outer_swap(there2[half:]), middle_swap(there0[half:])
    )
    late = jnp.where(middle, late_middle, late_outer)
    return [own, outer0, second, third], [there0, there1, there2, there3, late]


def pick_rows(pick, parts):
    picked = [
        jnp.dot(matrix, part, preferred_element_type=jnp.float32)
        for matrix, part in zip(pick, parts[:4])
        if part.shape[0] == matrix.shape[1]
    ]
    if len(parts) == 5:
        half = parts[3].shape[0]
        picked.append(
            jnp.dot(pick[3][:, :half], parts[3], preferred_element_type=jnp.float32)
            + jnp.dot(pick[3][:, half:], parts[4], preferred_element_type=jnp.float32)
        )
    return [part.astype(jnp.bfloat16) for part in picked]


def scatter_sums(middle, stream, own, there):
    half = there[3].shape[0]

    def plus(*parts):
        total = parts[0].astype(jnp.float32)
        for part in parts[1:]:
            total = total + part.astype(jnp.float32)
        return total

    def plus16(*parts):
        return plus(*parts).astype(jnp.bfloat16)

    def in_middle(array):
        return jnp.where(middle, array.astype(jnp.float32), 0.0)

    got, late_outer, late_middle = together(
        y_swap(there[3]), outer_swap(there[4]), middle_swap(there[4])
    )
    sum3 = jnp.concatenate([plus16(own[3][:half], got), own[3][half:]], axis=0)
    there2 = jnp.concatenate(
        [there[2][:half], plus16(there[2][half:], in_middle(late_outer))], axis=0
    )
    there0 = jnp.concatenate(
        [there[0][:half], plus16(there[0][half:], in_middle(late_middle))], axis=0
    )
    got, outer = together(y_swap(there2), outer_swap(sum3))
    sum2 = plus16(own[2], got, in_middle(outer))
    got, outer, across = together(y_swap(there[1]), outer_swap(sum2), middle_swap(sum2))
    sum1 = plus16(own[1], got, in_middle(across))
    sum3 = plus16(sum3, in_middle(outer))
    got, outer, across = together(y_swap(there0), outer_swap(sum1), middle_swap(sum3))
    return plus(stream, own[0], got, outer, in_middle(across))


def block_device(
    queries,
    keys,
    values,
    prefix_keys,
    prefix_values,
    lengths,
    groups,
    residual,
    out_proj,
    norm_gain,
    expert_ids,
    expert_gates,
    w_gate,
    w_up,
    w_down,
):
    core = lax.rem(lax.axis_index("req"), 2)
    z = lax.axis_index("exp") // 2
    middle = (z == 1) | (z == 2)
    place = jnp.stack([core, lax.axis_index("exp")]).astype(jnp.int32)

    shape = jnp.concatenate([lengths, groups], axis=1)
    other_shape = core_swap(shape)
    far_shape = x_swap(shape)
    far_queries = x_swap(queries)
    far_other_shape = core_swap(far_shape)

    proj_rows = lax.dynamic_slice_in_dim(out_proj, core * HEAD, HEAD, 0)
    proj_rows = lax.all_gather(proj_rows, "exp", axis=0, tiled=True)

    theirs, prefix_theirs = split_theirs(place, queries, keys, values, prefix_keys, prefix_values)
    other, prefix_other = core_swap(theirs), core_swap(prefix_theirs)
    far_other = core_swap(jnp.where(core == 0, far_queries[:, HEAD:], far_queries[:, :HEAD])[None])

    def prefix(shape_a, shape_b, q0, q1, dtype):
        return prefix_attend(
            place, shape_a, shape_b, q0, q1, prefix_keys, prefix_values, prefix_other, dtype
        )

    tab = jnp.concatenate([expert_ids.T.astype(jnp.bfloat16), expert_gates.T], axis=0)
    tab = jnp.pad(tab, ((0, 16 - tab.shape[0]), (0, 0)))
    suffix = suffix_attend(place, shape, other_shape, queries, keys, values, other)
    far = prefix(far_shape, far_other_shape, far_queries, far_other, jnp.bfloat16)
    back = (x_swap(far[0]), x_swap(far[1]))
    near = prefix(shape, other_shape, queries, other, jnp.float32)
    near_o, gain = lax.optimization_barrier((near[0], norm_gain.reshape(1, -1)))
    attended = merge_parts([suffix, (near_o, near[1]), back], tab)
    heads = lax.all_to_all(attended, "exp", split_axis=0, concat_axis=0, tiled=True)
    keep, send = project(heads, proj_rows)
    stream, normed = norm_rows(keep, core_swap(send), residual, gain)
    pick, give = route(place, heads)
    here, there = gather_rows(middle, normed)
    picked = pick_rows(pick[:4], here) + pick_rows(pick[4:], there)
    sums = run_experts(picked, give, w_gate, w_up, w_down)
    return scatter_sums(middle, stream, sums[:4], sums[4:]).astype(jnp.bfloat16)


def solution(mesh):
    in_specs = (
        P("req", "exp"),
        P("req", "exp"),
        P("req", "exp"),
        P(None, "req", "exp"),
        P(None, "req", "exp"),
        P("req", None),
        P("req", None),
        P(("req", "exp"), None),
        P("exp", None),
        P(),
        P(("req", "exp"), None),
        P(("req", "exp"), None),
        P("exp", None, None),
        P("exp", None, None),
        P("exp", None, None),
    )
    out_specs = P(("req", "exp"), None)
    blocked = mesh.shape["req"] == 4 and mesh.shape["exp"] == 8
    return jax.shard_map(
        block_device if blocked else general_device,
        mesh=mesh,
        in_specs=in_specs,
        out_specs=out_specs,
        check_vma=False,
    )
```

```python
import math

import jax
import jax.numpy as jnp
from jax import lax
from jax.experimental import pallas as pl
from jax.experimental.pallas import tpu as pltpu
from jax.sharding import PartitionSpec as P

HEAD = 128
TOPK = 4
EXPERTS = 32
G = 4
RQ = 8
ROW_TOK = 1024


NEG = -1e30


def token_layout(lengths, groups):
    req_ends = jnp.cumsum(lengths, axis=-1)
    starts = req_ends - lengths
    position = jnp.arange(ROW_TOK, dtype=jnp.int32)
    request = jnp.sum((position[None, :, None] >= req_ends[:, None, :]).astype(jnp.int32), axis=-1)
    onehot = request[:, :, None] == jnp.arange(RQ, dtype=jnp.int32)[None, None, :]
    first_tok = jnp.sum(jnp.where(onehot, starts[:, None, :], 0), axis=-1)
    tok_group = jnp.sum(jnp.where(onehot, groups[:, None, :], 0), axis=-1)
    return (request, position[None, :] - first_tok, tok_group)


def split_blocks(row_count):
    if row_count % 1024 == 0 and row_count > 1024:
        return row_count // 1024
    return 1


def pack_parts(parts):
    return jnp.concatenate([parts[0], parts[1], parts[2]], axis=1)


def unpack_parts(packed, head_count):
    columns = head_count * HEAD
    return (
        packed[:, :columns],
        packed[:, columns : columns + head_count],
        packed[:, columns + head_count :],
    )


def attend_prefix(query_rows, query_group, prefix_k, prefix_v):
    row_count, columns = query_rows.shape
    head_count = columns // HEAD
    span = prefix_k.shape[1]
    key_grid = prefix_k.reshape(G, span, head_count, HEAD)
    val_grid = prefix_v.reshape(G, span, head_count, HEAD)
    blocks = split_blocks(row_count)
    block_len = row_count // blocks
    scaling = 1.0 / math.sqrt(HEAD)

    def per_block(pieces):
        block_q, block_g = pieces
        query_grid = block_q.reshape(block_len, head_count, HEAD)
        scores = (
            jnp.einsum("qhd,gkhd->hqgk", query_grid, key_grid, preferred_element_type=jnp.float32)
            * scaling
        )
        member = block_g[:, None] == jnp.arange(G, dtype=jnp.int32)[None, :]
        scores = jnp.where(member[None, :, :, None], scores, NEG)
        maxima = jnp.max(scores, axis=(2, 3))
        exp_terms = jnp.exp(scores - maxima[:, :, None, None])
        totals = jnp.sum(exp_terms, axis=(2, 3))
        weighted = jnp.einsum(
            "hqgk,gkhd->qhd",
            exp_terms.astype(jnp.bfloat16),
            val_grid,
            preferred_element_type=jnp.float32,
        )
        return (weighted.reshape(block_len, columns), maxima.T, totals.T)

    weighted, maxima, totals = lax.map(
        per_block,
        (query_rows.reshape(blocks, block_len, columns), query_group.reshape(blocks, block_len)),
    )
    return (
        weighted.reshape(row_count, columns),
        maxima.reshape(row_count, head_count),
        totals.reshape(row_count, head_count),
    )


def attend_suffix(queries, keys, values, request, position):
    row_count, columns = queries.shape
    head_count = columns // HEAD
    blocks = split_blocks(row_count)
    block_len = row_count // blocks
    scaling = 1.0 / math.sqrt(HEAD)
    key_grid = keys.reshape(row_count, head_count, HEAD)
    val_grid = values.reshape(row_count, head_count, HEAD)

    def per_block(pieces):
        block_q, block_req, block_pos = pieces
        query_grid = block_q.reshape(block_len, head_count, HEAD)
        scores = (
            jnp.einsum("qhd,khd->hqk", query_grid, key_grid, preferred_element_type=jnp.float32)
            * scaling
        )
        allowed = (request[None, :] == block_req[:, None]) & (
            position[None, :] <= block_pos[:, None]
        )
        scores = jnp.where(allowed[None, :, :], scores, NEG)
        maxima = jnp.max(scores, axis=2)
        exp_terms = jnp.exp(scores - maxima[:, :, None])
        totals = jnp.sum(exp_terms, axis=2)
        weighted = jnp.einsum(
            "hqk,khd->qhd",
            exp_terms.astype(jnp.bfloat16),
            val_grid,
            preferred_element_type=jnp.float32,
        )
        return (weighted.reshape(block_len, columns), maxima.T, totals.T)

    weighted, maxima, totals = lax.map(
        per_block,
        (
            queries.reshape(blocks, block_len, columns),
            request.reshape(blocks, block_len),
            position.reshape(blocks, block_len),
        ),
    )
    return (
        weighted.reshape(row_count, columns),
        maxima.reshape(row_count, head_count),
        totals.reshape(row_count, head_count),
    )


def combine(former, latter):
    weighted_a, maxima_a, totals_a = former
    weighted_b, maxima_b, totals_b = latter
    row_count, head_count = maxima_a.shape
    maxima = jnp.maximum(maxima_a, maxima_b)
    factor_a = jnp.exp(maxima_a - maxima)
    factor_b = jnp.exp(maxima_b - maxima)
    weighted = (
        weighted_a.reshape(row_count, head_count, HEAD) * factor_a[:, :, None]
        + weighted_b.reshape(row_count, head_count, HEAD) * factor_b[:, :, None]
    )
    return (
        weighted.reshape(row_count, head_count * HEAD),
        maxima,
        totals_a * factor_a + totals_b * factor_b,
    )


def general_device(
    queries,
    keys,
    values,
    prefix_keys,
    prefix_values,
    lengths,
    groups,
    residual,
    out_proj,
    norm_gain,
    expert_ids,
    expert_gates,
    w_gate,
    w_up,
    w_down,
):
    row_tok, columns = queries.shape
    head_count = columns // HEAD
    tok_dev = residual.shape[0]
    request, position, tok_group = token_layout(lengths, groups)
    request, position, tok_group = (request[0], position[0], tok_group[0])
    all_groups = lax.all_gather(tok_group, "req", axis=0, tiled=True)
    partial_value = pack_parts(
        attend_prefix(
            lax.all_gather(queries, "req", axis=0, tiled=True),
            all_groups,
            prefix_keys,
            prefix_values,
        )
    )
    returned = lax.all_to_all(partial_value, "req", split_axis=0, concat_axis=0, tiled=True)
    owners = returned.shape[0] // row_tok
    back_w, back_m, back_t = unpack_parts(returned, head_count)
    all_weighted = back_w.reshape(owners, row_tok, head_count, HEAD)
    all_maxima = back_m.reshape(owners, row_tok, head_count)
    all_totals = back_t.reshape(owners, row_tok, head_count)
    maxima = jnp.max(all_maxima, axis=0)
    factor = jnp.exp(all_maxima - maxima[None])
    weighted = jnp.sum(all_weighted * factor[..., None], axis=0).reshape(row_tok, columns)
    prefix_part = (weighted, maxima, jnp.sum(all_totals * factor, axis=0))
    suffix_part = attend_suffix(queries, keys, values, request, position)
    weighted, maxima, totals = combine(prefix_part, suffix_part)
    attended = (
        (weighted.reshape(row_tok, head_count, HEAD) / totals[:, :, None])
        .reshape(row_tok, columns)
        .astype(jnp.bfloat16)
    )
    projected = lax.psum_scatter(
        jnp.dot(attended, out_proj, preferred_element_type=jnp.float32),
        "exp",
        scatter_dimension=0,
        tiled=True,
    )
    stream = residual.astype(jnp.float32) + projected
    meansq = jnp.mean(stream * stream, axis=-1, keepdims=True)
    normed = (stream * lax.rsqrt(meansq + 1e-06) * norm_gain.astype(jnp.float32)).astype(
        jnp.bfloat16
    )
    capacity = max(2, tok_dev // 4)
    flat_ids = expert_ids.reshape(-1)
    onehot = (flat_ids[:, None] == jnp.arange(EXPERTS, dtype=jnp.int32)[None, :]).astype(jnp.int32)
    slot_of = jnp.sum(onehot * (jnp.cumsum(onehot, axis=0) - 1), axis=1)
    source_rows = jnp.arange(tok_dev * TOPK, dtype=jnp.int32) // TOPK
    buffer = (
        jnp.zeros((EXPERTS, capacity, normed.shape[1]), jnp.bfloat16)
        .at[flat_ids, slot_of]
        .set(normed[source_rows])
    )
    exp_count = lax.axis_size("exp")
    exp_dev = w_gate.shape[0]
    received = lax.all_to_all(buffer, "exp", split_axis=0, concat_axis=0, tiled=True)
    slots = received.shape[1]
    grid_in = received.reshape(exp_count, exp_dev, slots, received.shape[2])
    gate_h = jnp.einsum("secd,edf->secf", grid_in, w_gate, preferred_element_type=jnp.float32)
    up_h = jnp.einsum("secd,edf->secf", grid_in, w_up, preferred_element_type=jnp.float32)
    hidden = (jax.nn.silu(gate_h) * up_h).astype(jnp.bfloat16)
    expert_out = jnp.einsum("secf,efd->secd", hidden, w_down, preferred_element_type=jnp.float32)
    returned = lax.all_to_all(
        expert_out.reshape(EXPERTS, slots, received.shape[2]),
        "exp",
        split_axis=0,
        concat_axis=0,
        tiled=True,
    )
    gathered = returned[flat_ids, slot_of] * expert_gates.reshape(-1).astype(jnp.float32)[:, None]
    mixture = jnp.sum(gathered.reshape(tok_dev, TOPK, gathered.shape[1]), axis=1)
    return (stream + mixture).astype(jnp.bfloat16)


BLK = 128
LOG2E = 1.4426950408889634
SCORE_SCALE = LOG2E / math.sqrt(HEAD)
VMEM_BIG = 56 * 1024 * 1024
VMEM_SMALL = 12 * 1024 * 1024


def core_swap(array):
    return lax.ppermute(array, "req", [(i, i ^ 1) for i in range(4)])


def x_swap(array):
    return lax.ppermute(array, "req", [(i, i ^ 2) for i in range(4)])


def y_swap(array):
    return lax.ppermute(array, "exp", [(i, i ^ 1) for i in range(8)])


def outer_swap(array):
    return lax.ppermute(array, "exp", [(i, i ^ 2) for i in range(8)])


def middle_swap(array):
    return lax.ppermute(array, "exp", [(2, 4), (3, 5), (4, 2), (5, 3)])


def split_kernel(sc_ref, q, k, v, pk, pv, out_tokens, out_prefix):
    for i, part in enumerate((q, k, v)):
        out_tokens[i] = part[...]
    out_prefix[0] = pk[...]
    out_prefix[1] = pv[...]


def split_theirs(place, q, k, v, pk, pv):
    rows, span = q.shape[0], pk.shape[1]
    part = rows // G
    tokens = pl.BlockSpec((part, HEAD), lambda i, s: (i, 1 - s[0]))
    prefix = pl.BlockSpec((1, span, HEAD), lambda i, s: (i, 0, 1 - s[0]))
    return pl.pallas_call(
        split_kernel,
        grid_spec=pltpu.PrefetchScalarGridSpec(
            num_scalar_prefetch=1,
            grid=(G,),
            in_specs=[tokens] * 3 + [prefix] * 2,
            out_specs=[
                pl.BlockSpec((3, part, HEAD), lambda i, s: (0, i, 0)),
                pl.BlockSpec((2, 1, span, HEAD), lambda i, s: (0, i, 0, 0)),
            ],
        ),
        out_shape=(
            jax.ShapeDtypeStruct((3, rows, HEAD), q.dtype),
            jax.ShapeDtypeStruct((2, G, span, HEAD), q.dtype),
        ),
        name="split_theirs",
    )(place, q, k, v, pk, pv)


def as_row(column):
    return jnp.transpose(jnp.broadcast_to(column, (BLK, BLK)))[0:1, :]


SUF = 256
SUB = 32
PER_ITEM = 8
ITEMS = 16


def build_work(shapes, item_group, item_block):
    per_row = ROW_TOK // SUB
    spans = []
    for r, (shape, at) in enumerate(shapes):
        start = 0
        for j in range(RQ):
            end = start + shape[at, j]
            first, last = r * per_row + start // SUB, r * per_row + (end - 1) // SUB
            spans.append((first, last, shape[at, RQ + j]))
            start = end

    def of_group(g, begin):
        at, done = begin, jnp.int32(-1)
        for first, last, group in spans:
            first = jnp.maximum(first, done + 1)
            match = group == g
            count = jnp.where(match, last - first + 1, 0)

            def put(i, carry, at=at, first=first):
                item_block[at + i] = first + i
                return carry

            lax.fori_loop(0, count, put, 0)
            at = at + count
            done = jnp.where(match, last, done)
        stop = (at + PER_ITEM - 1) // PER_ITEM * PER_ITEM

        def fill(i, carry):
            item_block[i] = item_block[begin]
            return carry

        def name(i, carry):
            item_group[i] = g
            return carry

        lax.fori_loop(at, stop, fill, 0)
        lax.fori_loop(begin // PER_ITEM, stop // PER_ITEM, name, 0)
        return stop

    return lax.fori_loop(0, G, of_group, jnp.int32(0)) // PER_ITEM


def prefix_kernel(
    sc_ref, shape_a, shape_b, q0, q1, pk, pv, other, o_ref, lse_ref,
    q_ref, ka, kb, va, vb, grp, lse, sa, sb, ta, tb, item_group, item_block, sems,
):
    tokens = q_ref.shape[0]
    span = ka.shape[1]
    shapes = ((shape_a, 0), (shape_b, 0))
    mine = pl.ds(pl.multiple_of(sc_ref[0] * HEAD, HEAD), HEAD)
    copies = [
        pltpu.make_async_copy(q0.at[:, mine], q_ref.at[:ROW_TOK, :], sems.at[0]),
        pltpu.make_async_copy(q1.at[0], q_ref.at[ROW_TOK:, :], sems.at[1]),
        pltpu.make_async_copy(pk.at[:, :, mine], ka, sems.at[2]),
        pltpu.make_async_copy(other.at[0], kb, sems.at[3]),
        pltpu.make_async_copy(pv.at[:, :, mine], va, sems.at[4]),
        pltpu.make_async_copy(other.at[1], vb, sems.at[5]),
    ]
    for copy in copies:
        copy.start()
    for r, (shape, at) in enumerate(shapes):
        token = lax.broadcasted_iota(jnp.int32, (ROW_TOK, HEAD), 0)
        group = jnp.full((ROW_TOK, HEAD), shape[at, RQ], jnp.int32)
        start = 0
        for j in range(1, RQ):
            start = start + shape[at, j - 1]
            group = jnp.where(token >= start, shape[at, RQ + j], group)
        grp[r * ROW_TOK : (r + 1) * ROW_TOK, :] = group
    count = build_work(shapes, item_group, item_block)
    for copy in copies:
        copy.wait()
    step = 512

    def held(item):
        return jnp.where(item < count, item, 0)

    def places(item):
        at = held(item) * PER_ITEM
        return [
            pl.ds(pl.multiple_of(item_block[at + i] * SUB, SUB), SUB) for i in range(PER_ITEM)
        ]

    def group_of(item):
        return item_group[held(item)]

    def lanes(x, op):
        parts = [x[:, c : c + HEAD] for c in range(0, x.shape[1], HEAD)]
        while len(parts) > 1:
            parts = [op(a, b) for a, b in zip(parts[::2], parts[1::2])]
        return parts[0]

    def score(item, s, tops):
        g = group_of(item)
        q = jnp.concatenate([q_ref[place, :] for place in places(item)], axis=0)
        for half, k in enumerate((ka, kb)):
            for c in range(0, span, step):
                x = lax.dot_general(
                    q,
                    k[g, c : c + step, :],
                    (((1,), (1,)), ((), ())),
                    preferred_element_type=jnp.float32,
                )
                s[:, half * span + c : half * span + c + step] = x
                top = lanes(x, jnp.maximum)
                tops[...] = top if half == 0 and c == 0 else jnp.maximum(tops[...], top)

    def weigh(item, s, tops):
        g = group_of(item)
        where = places(item)
        for part in range(2):
            here = slice(part * BLK, (part + 1) * BLK)
            top = jnp.max(tops[here, :], axis=1, keepdims=True)
            out = jnp.zeros((BLK, HEAD), jnp.float32)
            total = jnp.zeros((BLK, HEAD), jnp.float32)
            for half, v in enumerate((va, vb)):
                for c in range(0, span, step):
                    x = s[here, half * span + c : half * span + c + step]
                    p = jnp.exp2((x - top) * SCORE_SCALE)
                    total = total + lanes(p, jnp.add)
                    out = out + jnp.dot(
                        p.astype(jnp.bfloat16),
                        v[g, c : c + step, :],
                        preferred_element_type=jnp.float32,
                    )
            total = jnp.sum(total, axis=1, keepdims=True)
            out = out * (1.0 / total)
            here_lse = jnp.broadcast_to(top * SCORE_SCALE + jnp.log2(total), (BLK, HEAD))
            for i in range(BLK // SUB):
                place = where[part * (BLK // SUB) + i]
                sub = slice(i * SUB, (i + 1) * SUB)
                mine = grp[place, :] == g
                o_ref[place, :] = jnp.where(
                    mine, out[sub], o_ref[place, :].astype(jnp.float32)
                ).astype(o_ref.dtype)
                lse[place, :] = jnp.where(mine, here_lse[sub], lse[place, :])

    score(0, sa, ta)

    def pair(i, carry):
        score(2 * i + 1, sb, tb)
        weigh(2 * i, sa, ta)
        score(2 * i + 2, sa, ta)
        weigh(2 * i + 1, sb, tb)
        return carry

    lax.fori_loop(0, (count + 1) // 2, pair, 0)
    for b in range(tokens // BLK):
        lse_ref[b // 8, b % 8 : b % 8 + 1, :] = jnp.transpose(lse[b * BLK : (b + 1) * BLK, :])[
            0:1, :
        ]


def prefix_attend(place, shape_a, shape_b, q0, q1, pk, pv, other, out_dtype):
    rows = 2
    tokens = rows * ROW_TOK
    span = pk.shape[1]
    blocks = ROW_TOK // BLK
    smem = pl.BlockSpec(memory_space=pltpu.SMEM)
    vmem = pl.BlockSpec(memory_space=pltpu.VMEM)
    anywhere = pl.BlockSpec(memory_space=pl.ANY)
    prefix_buffer = pltpu.VMEM((G, span, HEAD), pk.dtype)
    per_token = pltpu.VMEM((tokens, HEAD), jnp.float32)
    scores = pltpu.VMEM((PER_ITEM * SUB, 2 * span), jnp.float32)
    tops = pltpu.VMEM((PER_ITEM * SUB, HEAD), jnp.float32)
    return pl.pallas_call(
        prefix_kernel,
        in_specs=[smem] * 3 + [anywhere] * 5,
        out_specs=(vmem, vmem),
        out_shape=(
            jax.ShapeDtypeStruct((tokens, HEAD), out_dtype),
            jax.ShapeDtypeStruct((rows, blocks, BLK), jnp.float32),
        ),
        scratch_shapes=[
            pltpu.VMEM((tokens, HEAD), q0.dtype),
            prefix_buffer,
            prefix_buffer,
            prefix_buffer,
            prefix_buffer,
            pltpu.VMEM((tokens, HEAD), jnp.int32),
            per_token,
            scores,
            scores,
            tops,
            tops,
            pltpu.SMEM((ITEMS,), jnp.int32),
            pltpu.SMEM((ITEMS * PER_ITEM,), jnp.int32),
            pltpu.SemaphoreType.DMA((6,)),
        ],
        compiler_params=pltpu.CompilerParams(vmem_limit_bytes=VMEM_BIG),
        cost_estimate=pl.CostEstimate(
            flops=tokens * span * HEAD * 8 * 4,
            bytes_accessed=4 * G * span * HEAD * 2,
            transcendentals=0,
        ),
        name="prefix_attend",
    )(place, shape_a, shape_b, q0, q1, pk, pv, other)


def suffix_kernel(sc_ref, shape_a, shape_b, q, k, v, other_row, o_ref, lse_ref):
    count = ROW_TOK // SUF
    rows = ((shape_a, (q, k, v)), (shape_b, [other_row.at[i] for i in range(3)]))
    for row, (shape, qkv) in enumerate(rows):
        token = lax.broadcasted_iota(jnp.int32, (ROW_TOK, 1), 0)
        first = jnp.zeros((ROW_TOK, 1), jnp.int32)
        start = 0
        for j in range(1, RQ):
            start = start + shape[0, j - 1]
            first = jnp.where(token >= start, start, first)

        def bounds(i):
            low = max(0, i * SUF - ROW_TOK // 2)
            return low, slice(i * SUF, (i + 1) * SUF), slice(low, (i + 1) * SUF)

        def score(i, qkv=qkv, first=first, token=token):
            low, here, seen = bounds(i)
            s = lax.dot_general(
                qkv[0][here, :],
                qkv[1][seen, :],
                (((1,), (1,)), ((), ())),
                preferred_element_type=jnp.float32,
            )
            other = low + lax.broadcasted_iota(jnp.int32, s.shape, 1)
            return jnp.where((other >= first[here]) & (other <= token[here]), s, NEG)

        def weigh(i, s, row=row, qkv=qkv):
            unused, here, seen = bounds(i)
            top = jnp.max(s, axis=1, keepdims=True)
            p = jnp.exp2((s - top) * SCORE_SCALE)
            total = jnp.sum(p, axis=1, keepdims=True)
            out = jnp.dot(
                p.astype(jnp.bfloat16), qkv[2][seen, :], preferred_element_type=jnp.float32
            )
            o_ref[row * ROW_TOK + i * SUF : row * ROW_TOK + (i + 1) * SUF, :] = out * (1.0 / total)
            lse = top * SCORE_SCALE + jnp.log2(total)
            for part in range(SUF // BLK):
                at = i * (SUF // BLK) + part
                lse_ref[row, at : at + 1, :] = as_row(lse[part * BLK : (part + 1) * BLK])

        held = score(0)
        for i in range(count):
            later = score(i + 1) if i + 1 < count else None
            weigh(i, held)
            held = later


def suffix_attend(place, shape_a, shape_b, q, k, v, other):
    rows, tokens = 2, q.shape[0]
    blocks = tokens // BLK
    smem = pl.BlockSpec(memory_space=pltpu.SMEM)
    mine = pl.BlockSpec((tokens, HEAD), lambda i, s: (0, s[0]))
    return pl.pallas_call(
        suffix_kernel,
        grid_spec=pltpu.PrefetchScalarGridSpec(
            num_scalar_prefetch=1,
            grid=(1,),
            in_specs=[smem, smem]
            + [mine] * 3
            + [pl.BlockSpec((3, tokens, HEAD), lambda i, s: (0, 0, 0))],
            out_specs=[
                pl.BlockSpec((rows * tokens, HEAD), lambda i, s: (0, 0)),
                pl.BlockSpec((rows, blocks, BLK), lambda i, s: (0, 0, 0)),
            ],
        ),
        out_shape=(
            jax.ShapeDtypeStruct((rows * tokens, HEAD), jnp.float32),
            jax.ShapeDtypeStruct((rows, blocks, BLK), jnp.float32),
        ),
        compiler_params=pltpu.CompilerParams(vmem_limit_bytes=VMEM_BIG),
        cost_estimate=pl.CostEstimate(
            flops=rows * tokens * tokens * HEAD * 4 * 4, bytes_accessed=1 << 20, transcendentals=0
        ),
        name="suffix_attend",
    )(place, shape_a, shape_b, q, k, v, other)


MERGE_BLOCKS = 4


def merge_kernel(*refs):
    parts, tab_ref, out_ref = refs[:-2], refs[-2], refs[-1]
    step = pl.program_id(0)
    for block in range(MERGE_BLOCKS):
        out_ref[block, 2 * BLK :, :] = tab_ref[...]
    half = len(parts) // 2
    for row in range(2):
        sources = parts[row * half : (row + 1) * half]
        for block in range(MERGE_BLOCKS):
            here = slice(block * BLK, (block + 1) * BLK)
            at = pl.ds(step * MERGE_BLOCKS + block, 1)
            lses = [
                jnp.transpose(jnp.broadcast_to(lse[0, at, :], (BLK, BLK))) for lse in sources[1::2]
            ]
            top = lses[0]
            for lse in lses[1:]:
                top = jnp.maximum(top, lse)
            total, summed = 0.0, 0.0
            for lse, o in zip(lses, sources[0::2]):
                weight = jnp.exp2(lse - top)
                total = total + weight
                summed = summed + weight * o[here, :].astype(jnp.float32)
            out_ref[block, row * BLK : (row + 1) * BLK, :] = (summed / total).astype(out_ref.dtype)


def merge_parts(parts, tab):
    extra = tab.shape[0]
    blocks = ROW_TOK // BLK
    steps = blocks // MERGE_BLOCKS
    specs, operands = [], []
    for row in range(2):
        for o, lse in parts:
            operands += [o, lse]
            specs += [
                pl.BlockSpec((MERGE_BLOCKS * BLK, HEAD), lambda b, row=row: (row * steps + b, 0)),
                pl.BlockSpec((1, blocks, BLK), lambda b, row=row: (row, 0, 0)),
            ]
    return pl.pallas_call(
        merge_kernel,
        grid=(steps,),
        in_specs=specs + [pl.BlockSpec((extra, BLK), lambda b: (0, 0))],
        out_specs=pl.BlockSpec((MERGE_BLOCKS, 2 * BLK + extra, HEAD), lambda b: (b, 0, 0)),
        out_shape=jax.ShapeDtypeStruct((blocks, 2 * BLK + extra, HEAD), jnp.bfloat16),
        compiler_params=pltpu.CompilerParams(vmem_limit_bytes=VMEM_SMALL),
        name="merge_parts",
    )(*operands, tab)


def project_kernel(a_ref, w_ref, keep_ref, send_ref, lhs):
    @pl.when(pl.program_id(0) == 0)
    def first():
        for h in range(a_ref.shape[0]):
            lhs[:, h * HEAD : (h + 1) * HEAD] = a_ref[h, : 2 * BLK, :]

    out = jnp.dot(lhs[...], w_ref[...], preferred_element_type=jnp.float32)
    rows = keep_ref.shape[0]
    keep_ref[...] = out[:rows]
    send_ref[...] = out[rows:].astype(send_ref.dtype)


def project(attended, weights):
    heads, held, unused = attended.shape
    tokens = 2 * BLK
    depth, width = weights.shape
    rows, tile = tokens // 2, 1024
    out_spec = pl.BlockSpec((rows, tile), lambda i: (0, i))
    return pl.pallas_call(
        project_kernel,
        grid=(width // tile,),
        in_specs=[
            pl.BlockSpec((heads, held, HEAD), lambda i: (0, 0, 0)),
            pl.BlockSpec((depth, tile), lambda i: (0, i)),
        ],
        out_specs=[out_spec, out_spec],
        out_shape=(
            jax.ShapeDtypeStruct((rows, width), jnp.float32),
            jax.ShapeDtypeStruct((rows, width), jnp.bfloat16),
        ),
        scratch_shapes=[pltpu.VMEM((tokens, depth), jnp.bfloat16)],
        compiler_params=pltpu.CompilerParams(vmem_limit_bytes=VMEM_SMALL),
        name="project",
    )(attended, weights)


def norm_kernel(keep, got, residual, gain, stream_ref, normed_ref):
    stream = residual[...].astype(jnp.float32) + (keep[...] + got[...].astype(jnp.float32))
    meansq = jnp.mean(stream * stream, axis=-1, keepdims=True)
    stream_ref[...] = stream
    normed = stream * lax.rsqrt(meansq + 1e-06) * gain[...].astype(jnp.float32)
    normed_ref[...] = normed.astype(normed_ref.dtype)


def norm_rows(keep, got, residual, gain):
    return pl.pallas_call(
        norm_kernel,
        out_shape=(
            jax.ShapeDtypeStruct(keep.shape, jnp.float32),
            jax.ShapeDtypeStruct(keep.shape, jnp.bfloat16),
        ),
        compiler_params=pltpu.CompilerParams(vmem_limit_bytes=VMEM_SMALL),
        name="norm_rows",
    )(keep, got, residual, gain)


EXP_DEV = 4
VMEM_STAGE = 2 * 1024 * 1024
EXPERT_VMEM = 8 * 1024 * 1024
SLOTS = 32
SLOT_Z = ((0, 1, 2, 3), (1, 0, 3, 2), (2, 3, 0, 1), (3, 2, 1, 0))


def route_kernel(sc_ref, tab_ref, pick_ref, give_ref):
    before = (
        lax.broadcasted_iota(jnp.int32, (BLK, BLK), 0)
        < lax.broadcasted_iota(jnp.int32, (BLK, BLK), 1)
    ).astype(jnp.bfloat16)
    place = lax.broadcasted_iota(jnp.int32, (SLOTS, BLK), 0).astype(jnp.float32)
    place_here = sc_ref[1]
    here_z, here_y = place_here // 2, place_here % 2
    for slot in range(8):
        of = SLOT_Z[3][slot % 4]
        for z in range(3):
            of = jnp.where(here_z == z, SLOT_Z[z][slot % 4], of)
        tab = tab_ref[of * 2 + (here_y if slot < 4 else 1 - here_y)].astype(jnp.float32)
        ids, gates = tab[:TOPK], tab[TOPK : 2 * TOPK]
        chosen, weights = [], []
        for j in range(EXP_DEV):
            match = ids == (place_here * EXP_DEV + j).astype(jnp.float32)
            chosen.append(jnp.sum(match.astype(jnp.float32), axis=0, keepdims=True))
            weights.append(jnp.sum(jnp.where(match, gates, 0.0), axis=0, keepdims=True))
        held = jnp.concatenate(chosen + chosen, axis=0)
        places = jnp.dot(held.astype(jnp.bfloat16), before, preferred_element_type=jnp.float32)
        places = jnp.where(held > 0.5, places, -1.0)
        hits = [place == places[j : j + 1] for j in range(EXP_DEV)]
        pick_ref[slot] = jnp.concatenate(
            [hit.astype(jnp.float32) for hit in hits], axis=0
        ).astype(jnp.bfloat16)
        spread = jnp.concatenate(
            [jnp.where(hit, weight, 0.0) for hit, weight in zip(hits, weights)], axis=0
        )
        give_ref[slot] = jnp.transpose(spread).astype(jnp.bfloat16)


def route(place, heads):
    extra = heads.shape[1] - 2 * BLK
    shape = jax.ShapeDtypeStruct((8, BLK, EXP_DEV * SLOTS), jnp.bfloat16)
    return pl.pallas_call(
        route_kernel,
        grid=(1,),
        in_specs=[
            pl.BlockSpec(memory_space=pltpu.SMEM),
            pl.BlockSpec((8, extra, BLK), lambda i: (0, 2 * BLK // extra, 0)),
        ],
        out_specs=[pl.BlockSpec((8, BLK, BLK), lambda i: (0, 0, 0))] * 2,
        out_shape=(shape, shape),
        compiler_params=pltpu.CompilerParams(vmem_limit_bytes=VMEM_SMALL),
        name="route",
    )(place, heads)


def stage_kernel(source, held, sems):
    copies = [pltpu.make_async_copy(source.at[i], held.at[i], sems.at[i]) for i in range(EXP_DEV)]
    for copy in copies:
        copy.start()
    for copy in copies:
        copy.wait()


def stage(weights):
    return pl.pallas_call(
        stage_kernel,
        in_specs=[pl.BlockSpec(memory_space=pltpu.HBM)],
        out_specs=pl.BlockSpec(memory_space=pltpu.VMEM),
        out_shape=jax.ShapeDtypeStruct(weights.shape, weights.dtype),
        scratch_shapes=[pltpu.SemaphoreType.DMA((EXP_DEV,))],
        compiler_params=pltpu.CompilerParams(vmem_limit_bytes=VMEM_STAGE),
        cost_estimate=pl.CostEstimate(flops=0, bytes_accessed=2 * weights.size, transcendentals=0),
        name="stage",
    )(weights)


def experts_kernel(*refs):
    picked = refs[:8]
    give_ref, wg, wu, wd = refs[8:12]
    outs, rows_out = refs[12:-1], refs[-1]
    contract = (((1,), (1,)), ((), ()))

    def run(expert, carry):
        here = pl.ds(pl.multiple_of(expert * SLOTS, SLOTS), SLOTS)
        rows = jnp.concatenate([part[here, :] for part in picked], axis=0)
        gate_h = lax.dot_general(wg[expert], rows, contract, preferred_element_type=jnp.float32)
        up_h = lax.dot_general(wu[expert], rows, contract, preferred_element_type=jnp.float32)
        hidden = jnp.transpose((gate_h / (1.0 + jnp.exp(-gate_h)) * up_h).astype(jnp.bfloat16))
        out = jnp.dot(hidden, wd[expert], preferred_element_type=jnp.float32).astype(jnp.bfloat16)
        for slot in range(8):
            rows_out[slot, here, :] = out[slot * SLOTS : (slot + 1) * SLOTS]
        return carry

    lax.fori_loop(0, EXP_DEV, run, 0)
    for slot in range(8):
        out = jnp.dot(give_ref[slot], rows_out[slot], preferred_element_type=jnp.float32)
        out = out.astype(jnp.bfloat16)
        if slot < 7:
            outs[slot][...] = out
        else:
            outs[7][...] = out[: BLK // 2]
            outs[8][...] = out[BLK // 2 :]


def run_experts(picked, give, w_gate, w_up, w_down):
    width = picked[0].shape[1]
    heights = [BLK] * 7 + [BLK // 2] * 2
    vmem = pl.BlockSpec(memory_space=pltpu.VMEM)
    return pl.pallas_call(
        experts_kernel,
        in_specs=[vmem] * 12,
        out_specs=[vmem] * 9,
        out_shape=[jax.ShapeDtypeStruct((n, width), jnp.bfloat16) for n in heights],
        scratch_shapes=[pltpu.VMEM((8, EXP_DEV * SLOTS, width), jnp.bfloat16)],
        compiler_params=pltpu.CompilerParams(vmem_limit_bytes=EXPERT_VMEM),
        name="experts",
    )(*picked, give, w_gate, w_up, w_down)


def together(*arrays):
    return lax.optimization_barrier(arrays)


def gather_rows(middle, own, weights):
    half = own.shape[0] // 2
    own, *weights = together(own, *weights)
    outer0, middle0, there0, gate = together(
        outer_swap(own), middle_swap(own), y_swap(own), stage(weights[0])
    )
    outer1, middle1, there1, down = together(
        outer_swap(middle0), middle_swap(outer0), y_swap(outer0), stage(weights[2])
    )
    second = jnp.where(middle, middle1, outer1)
    outer2, there2 = together(outer_swap(middle1), y_swap(second))
    third = jnp.where(middle, middle0, outer2)
    there3, late_outer, late_middle = together(
        y_swap(third[:half]), outer_swap(there2[half:]), middle_swap(there0[half:])
    )
    late = jnp.where(middle, late_middle, late_outer)
    return [own, outer0, second, third], [there0, there1, there2, there3, late], (gate, weights[1], down)


def pick_rows(pick, parts):
    picked = [
        jnp.dot(matrix, part, preferred_element_type=jnp.float32)
        for matrix, part in zip(pick, parts[:4])
        if part.shape[0] == matrix.shape[1]
    ]
    if len(parts) == 5:
        half = parts[3].shape[0]
        picked.append(
            jnp.dot(pick[3][:, :half], parts[3], preferred_element_type=jnp.float32)
            + jnp.dot(pick[3][:, half:], parts[4], preferred_element_type=jnp.float32)
        )
    return [part.astype(jnp.bfloat16) for part in picked]


def scatter_sums(middle, stream, own, there):
    half = there[3].shape[0]

    def plus(*parts):
        total = parts[0].astype(jnp.float32)
        for part in parts[1:]:
            total = total + part.astype(jnp.float32)
        return total

    def plus16(*parts):
        return plus(*parts).astype(jnp.bfloat16)

    def in_middle(array):
        return jnp.where(middle, array.astype(jnp.float32), 0.0)

    got, late_outer, late_middle = together(
        y_swap(there[3]), outer_swap(there[4]), middle_swap(there[4])
    )
    sum3 = jnp.concatenate([plus16(own[3][:half], got), own[3][half:]], axis=0)
    there2 = jnp.concatenate(
        [there[2][:half], plus16(there[2][half:], in_middle(late_outer))], axis=0
    )
    there0 = jnp.concatenate(
        [there[0][:half], plus16(there[0][half:], in_middle(late_middle))], axis=0
    )
    got, outer = together(y_swap(there2), outer_swap(sum3))
    sum2 = plus16(own[2], got, in_middle(outer))
    got, outer, across = together(y_swap(there[1]), outer_swap(sum2), middle_swap(sum2))
    sum1 = plus16(own[1], got, in_middle(across))
    sum3 = plus16(sum3, in_middle(outer))
    got, outer, across = together(y_swap(there0), outer_swap(sum1), middle_swap(sum3))
    return plus(stream, own[0], got, outer, in_middle(across))


def block_device(
    queries,
    keys,
    values,
    prefix_keys,
    prefix_values,
    lengths,
    groups,
    residual,
    out_proj,
    norm_gain,
    expert_ids,
    expert_gates,
    w_gate,
    w_up,
    w_down,
):
    core = lax.rem(lax.axis_index("req"), 2)
    z = lax.axis_index("exp") // 2
    middle = (z == 1) | (z == 2)
    place = jnp.stack([core, lax.axis_index("exp")]).astype(jnp.int32)

    shape = jnp.concatenate([lengths, groups], axis=1)
    other_shape = core_swap(shape)
    far_shape = x_swap(shape)
    far_queries = x_swap(queries)

    proj_rows = lax.dynamic_slice_in_dim(out_proj, core * HEAD, HEAD, 0)
    proj_rows = lax.all_gather(proj_rows, "exp", axis=0, tiled=True)

    theirs, prefix_theirs = split_theirs(place, queries, keys, values, prefix_keys, prefix_values)
    other, prefix_other = core_swap(theirs), core_swap(prefix_theirs)

    def prefix(shape_a, shape_b, q0, q1, dtype):
        return prefix_attend(
            place, shape_a, shape_b, q0, q1, prefix_keys, prefix_values, prefix_other, dtype
        )

    tab = jnp.concatenate([expert_ids.T.astype(jnp.bfloat16), expert_gates.T], axis=0)
    tab = jnp.pad(tab, ((0, 16 - tab.shape[0]), (0, 0)))
    suffix = suffix_attend(place, shape, other_shape, queries, keys, values, other)
    unused, far_queries, far_shape = together(suffix[1], far_queries, far_shape)
    far_send = jnp.where(core == 0, far_queries[:, HEAD:], far_queries[:, :HEAD])[None]
    far_other, far_other_shape = core_swap(far_send), core_swap(far_shape)
    far = prefix(far_shape, far_other_shape, far_queries, far_other, jnp.bfloat16)
    back = (x_swap(far[0]), x_swap(far[1]))
    near = prefix(shape, other_shape, queries, other, jnp.float32)
    near_o, gain = lax.optimization_barrier((near[0], norm_gain.reshape(1, -1)))
    attended = merge_parts([suffix, (near_o, near[1]), back], tab)
    heads = lax.all_to_all(attended, "exp", split_axis=0, concat_axis=0, tiled=True)
    keep, send = project(heads, proj_rows)
    stream, normed = norm_rows(keep, core_swap(send), residual, gain)
    pick, give = route(place, heads)
    weights = (w_gate.transpose(0, 2, 1), w_up.transpose(0, 2, 1), w_down)
    here, there, weights = gather_rows(middle, normed, weights)
    picked = pick_rows(pick[:4], here) + pick_rows(pick[4:], there)
    sums = run_experts(picked, give, *weights)
    return scatter_sums(middle, stream, sums[:4], sums[4:]).astype(jnp.bfloat16)


def solution(mesh):
    in_specs = (
        P("req", "exp"),
        P("req", "exp"),
        P("req", "exp"),
        P(None, "req", "exp"),
        P(None, "req", "exp"),
        P("req", None),
        P("req", None),
        P(("req", "exp"), None),
        P("exp", None),
        P(),
        P(("req", "exp"), None),
        P(("req", "exp"), None),
        P("exp", None, None),
        P("exp", None, None),
        P("exp", None, None),
    )
    out_specs = P(("req", "exp"), None)
    blocked = mesh.shape["req"] == 4 and mesh.shape["exp"] == 8
    return jax.shard_map(
        block_device if blocked else general_device,
        mesh=mesh,
        in_specs=in_specs,
        out_specs=out_specs,
        check_vma=False,
    )
```

```python
import math

import jax
import jax.numpy as jnp
from jax import lax
from jax.experimental import pallas as pl
from jax.experimental.pallas import tpu as pltpu
from jax.sharding import PartitionSpec as P

HEAD = 128
TOPK = 4
EXPERTS = 32
G = 4
RQ = 8
ROW_TOK = 1024


NEG = -1e30


def token_layout(lengths, groups):
    req_ends = jnp.cumsum(lengths, axis=-1)
    starts = req_ends - lengths
    position = jnp.arange(ROW_TOK, dtype=jnp.int32)
    request = jnp.sum((position[None, :, None] >= req_ends[:, None, :]).astype(jnp.int32), axis=-1)
    onehot = request[:, :, None] == jnp.arange(RQ, dtype=jnp.int32)[None, None, :]
    first_tok = jnp.sum(jnp.where(onehot, starts[:, None, :], 0), axis=-1)
    tok_group = jnp.sum(jnp.where(onehot, groups[:, None, :], 0), axis=-1)
    return (request, position[None, :] - first_tok, tok_group)


def split_blocks(row_count):
    if row_count % 1024 == 0 and row_count > 1024:
        return row_count // 1024
    return 1


def pack_parts(parts):
    return jnp.concatenate([parts[0], parts[1], parts[2]], axis=1)


def unpack_parts(packed, head_count):
    columns = head_count * HEAD
    return (
        packed[:, :columns],
        packed[:, columns : columns + head_count],
        packed[:, columns + head_count :],
    )


def attend_prefix(query_rows, query_group, prefix_k, prefix_v):
    row_count, columns = query_rows.shape
    head_count = columns // HEAD
    span = prefix_k.shape[1]
    key_grid = prefix_k.reshape(G, span, head_count, HEAD)
    val_grid = prefix_v.reshape(G, span, head_count, HEAD)
    blocks = split_blocks(row_count)
    block_len = row_count // blocks
    scaling = 1.0 / math.sqrt(HEAD)

    def per_block(pieces):
        block_q, block_g = pieces
        query_grid = block_q.reshape(block_len, head_count, HEAD)
        scores = (
            jnp.einsum("qhd,gkhd->hqgk", query_grid, key_grid, preferred_element_type=jnp.float32)
            * scaling
        )
        member = block_g[:, None] == jnp.arange(G, dtype=jnp.int32)[None, :]
        scores = jnp.where(member[None, :, :, None], scores, NEG)
        maxima = jnp.max(scores, axis=(2, 3))
        exp_terms = jnp.exp(scores - maxima[:, :, None, None])
        totals = jnp.sum(exp_terms, axis=(2, 3))
        weighted = jnp.einsum(
            "hqgk,gkhd->qhd",
            exp_terms.astype(jnp.bfloat16),
            val_grid,
            preferred_element_type=jnp.float32,
        )
        return (weighted.reshape(block_len, columns), maxima.T, totals.T)

    weighted, maxima, totals = lax.map(
        per_block,
        (query_rows.reshape(blocks, block_len, columns), query_group.reshape(blocks, block_len)),
    )
    return (
        weighted.reshape(row_count, columns),
        maxima.reshape(row_count, head_count),
        totals.reshape(row_count, head_count),
    )


def attend_suffix(queries, keys, values, request, position):
    row_count, columns = queries.shape
    head_count = columns // HEAD
    blocks = split_blocks(row_count)
    block_len = row_count // blocks
    scaling = 1.0 / math.sqrt(HEAD)
    key_grid = keys.reshape(row_count, head_count, HEAD)
    val_grid = values.reshape(row_count, head_count, HEAD)

    def per_block(pieces):
        block_q, block_req, block_pos = pieces
        query_grid = block_q.reshape(block_len, head_count, HEAD)
        scores = (
            jnp.einsum("qhd,khd->hqk", query_grid, key_grid, preferred_element_type=jnp.float32)
            * scaling
        )
        allowed = (request[None, :] == block_req[:, None]) & (
            position[None, :] <= block_pos[:, None]
        )
        scores = jnp.where(allowed[None, :, :], scores, NEG)
        maxima = jnp.max(scores, axis=2)
        exp_terms = jnp.exp(scores - maxima[:, :, None])
        totals = jnp.sum(exp_terms, axis=2)
        weighted = jnp.einsum(
            "hqk,khd->qhd",
            exp_terms.astype(jnp.bfloat16),
            val_grid,
            preferred_element_type=jnp.float32,
        )
        return (weighted.reshape(block_len, columns), maxima.T, totals.T)

    weighted, maxima, totals = lax.map(
        per_block,
        (
            queries.reshape(blocks, block_len, columns),
            request.reshape(blocks, block_len),
            position.reshape(blocks, block_len),
        ),
    )
    return (
        weighted.reshape(row_count, columns),
        maxima.reshape(row_count, head_count),
        totals.reshape(row_count, head_count),
    )


def combine(former, latter):
    weighted_a, maxima_a, totals_a = former
    weighted_b, maxima_b, totals_b = latter
    row_count, head_count = maxima_a.shape
    maxima = jnp.maximum(maxima_a, maxima_b)
    factor_a = jnp.exp(maxima_a - maxima)
    factor_b = jnp.exp(maxima_b - maxima)
    weighted = (
        weighted_a.reshape(row_count, head_count, HEAD) * factor_a[:, :, None]
        + weighted_b.reshape(row_count, head_count, HEAD) * factor_b[:, :, None]
    )
    return (
        weighted.reshape(row_count, head_count * HEAD),
        maxima,
        totals_a * factor_a + totals_b * factor_b,
    )


def general_device(
    queries,
    keys,
    values,
    prefix_keys,
    prefix_values,
    lengths,
    groups,
    residual,
    out_proj,
    norm_gain,
    expert_ids,
    expert_gates,
    w_gate,
    w_up,
    w_down,
):
    row_tok, columns = queries.shape
    head_count = columns // HEAD
    tok_dev = residual.shape[0]
    request, position, tok_group = token_layout(lengths, groups)
    request, position, tok_group = (request[0], position[0], tok_group[0])
    all_groups = lax.all_gather(tok_group, "req", axis=0, tiled=True)
    partial_value = pack_parts(
        attend_prefix(
            lax.all_gather(queries, "req", axis=0, tiled=True),
            all_groups,
            prefix_keys,
            prefix_values,
        )
    )
    returned = lax.all_to_all(partial_value, "req", split_axis=0, concat_axis=0, tiled=True)
    owners = returned.shape[0] // row_tok
    back_w, back_m, back_t = unpack_parts(returned, head_count)
    all_weighted = back_w.reshape(owners, row_tok, head_count, HEAD)
    all_maxima = back_m.reshape(owners, row_tok, head_count)
    all_totals = back_t.reshape(owners, row_tok, head_count)
    maxima = jnp.max(all_maxima, axis=0)
    factor = jnp.exp(all_maxima - maxima[None])
    weighted = jnp.sum(all_weighted * factor[..., None], axis=0).reshape(row_tok, columns)
    prefix_part = (weighted, maxima, jnp.sum(all_totals * factor, axis=0))
    suffix_part = attend_suffix(queries, keys, values, request, position)
    weighted, maxima, totals = combine(prefix_part, suffix_part)
    attended = (
        (weighted.reshape(row_tok, head_count, HEAD) / totals[:, :, None])
        .reshape(row_tok, columns)
        .astype(jnp.bfloat16)
    )
    projected = lax.psum_scatter(
        jnp.dot(attended, out_proj, preferred_element_type=jnp.float32),
        "exp",
        scatter_dimension=0,
        tiled=True,
    )
    stream = residual.astype(jnp.float32) + projected
    meansq = jnp.mean(stream * stream, axis=-1, keepdims=True)
    normed = (stream * lax.rsqrt(meansq + 1e-06) * norm_gain.astype(jnp.float32)).astype(
        jnp.bfloat16
    )
    capacity = max(2, tok_dev // 4)
    flat_ids = expert_ids.reshape(-1)
    onehot = (flat_ids[:, None] == jnp.arange(EXPERTS, dtype=jnp.int32)[None, :]).astype(jnp.int32)
    slot_of = jnp.sum(onehot * (jnp.cumsum(onehot, axis=0) - 1), axis=1)
    source_rows = jnp.arange(tok_dev * TOPK, dtype=jnp.int32) // TOPK
    buffer = (
        jnp.zeros((EXPERTS, capacity, normed.shape[1]), jnp.bfloat16)
        .at[flat_ids, slot_of]
        .set(normed[source_rows])
    )
    exp_count = lax.axis_size("exp")
    exp_dev = w_gate.shape[0]
    received = lax.all_to_all(buffer, "exp", split_axis=0, concat_axis=0, tiled=True)
    slots = received.shape[1]
    grid_in = received.reshape(exp_count, exp_dev, slots, received.shape[2])
    gate_h = jnp.einsum("secd,edf->secf", grid_in, w_gate, preferred_element_type=jnp.float32)
    up_h = jnp.einsum("secd,edf->secf", grid_in, w_up, preferred_element_type=jnp.float32)
    hidden = (jax.nn.silu(gate_h) * up_h).astype(jnp.bfloat16)
    expert_out = jnp.einsum("secf,efd->secd", hidden, w_down, preferred_element_type=jnp.float32)
    returned = lax.all_to_all(
        expert_out.reshape(EXPERTS, slots, received.shape[2]),
        "exp",
        split_axis=0,
        concat_axis=0,
        tiled=True,
    )
    gathered = returned[flat_ids, slot_of] * expert_gates.reshape(-1).astype(jnp.float32)[:, None]
    mixture = jnp.sum(gathered.reshape(tok_dev, TOPK, gathered.shape[1]), axis=1)
    return (stream + mixture).astype(jnp.bfloat16)


BLK = 128
LOG2E = 1.4426950408889634
SCORE_SCALE = LOG2E / math.sqrt(HEAD)
VMEM_BIG = 28 * 1024 * 1024
VMEM_SMALL = 12 * 1024 * 1024


def core_swap(array):
    return lax.ppermute(array, "req", [(i, i ^ 1) for i in range(4)])


def x_swap(array):
    return lax.ppermute(array, "req", [(i, i ^ 2) for i in range(4)])


def y_swap(array):
    return lax.ppermute(array, "exp", [(i, i ^ 1) for i in range(8)])


def outer_swap(array):
    return lax.ppermute(array, "exp", [(i, i ^ 2) for i in range(8)])


def gather_z(array):
    return lax.all_gather(
        array, "exp", axis=0, axis_index_groups=[[0, 2, 4, 6], [1, 3, 5, 7]], tiled=True
    )


def middle_swap(array):
    return lax.ppermute(array, "exp", [(2, 4), (3, 5), (4, 2), (5, 3)])


def split_kernel(sc_ref, q, k, v, pk, pv, out_tokens, out_prefix):
    for i, part in enumerate((q, k, v)):
        out_tokens[i] = part[...]
    out_prefix[0] = pk[...]
    out_prefix[1] = pv[...]


def split_theirs(place, q, k, v, pk, pv):
    rows, span = q.shape[0], pk.shape[1]
    part = rows // G
    tokens = pl.BlockSpec((part, HEAD), lambda i, s: (i, 1 - s[0]))
    prefix = pl.BlockSpec((1, span, HEAD), lambda i, s: (i, 0, 1 - s[0]))
    return pl.pallas_call(
        split_kernel,
        grid_spec=pltpu.PrefetchScalarGridSpec(
            num_scalar_prefetch=1,
            grid=(G,),
            in_specs=[tokens] * 3 + [prefix] * 2,
            out_specs=[
                pl.BlockSpec((3, part, HEAD), lambda i, s: (0, i, 0)),
                pl.BlockSpec((2, 1, span, HEAD), lambda i, s: (0, i, 0, 0)),
            ],
        ),
        out_shape=(
            jax.ShapeDtypeStruct((3, rows, HEAD), q.dtype),
            jax.ShapeDtypeStruct((2, G, span, HEAD), q.dtype),
        ),
        name="split_theirs",
    )(place, q, k, v, pk, pv)


def as_row(column):
    return jnp.transpose(jnp.broadcast_to(column, (BLK, BLK)))[0:1, :]


SUF = 256
SUB = 32
PER_ITEM = 8
ITEMS = 16


def build_work(shapes, item_group, item_block):
    per_row = ROW_TOK // SUB
    spans = []
    for r, (shape, at) in enumerate(shapes):
        start = 0
        for j in range(RQ):
            end = start + shape[at, j]
            first, last = r * per_row + start // SUB, r * per_row + (end - 1) // SUB
            spans.append((first, last, shape[at, RQ + j]))
            start = end

    def of_group(g, begin):
        at, done = begin, jnp.int32(-1)
        for first, last, group in spans:
            first = jnp.maximum(first, done + 1)
            match = group == g
            count = jnp.where(match, last - first + 1, 0)

            def put(i, carry, at=at, first=first):
                item_block[at + i] = first + i
                return carry

            lax.fori_loop(0, count, put, 0)
            at = at + count
            done = jnp.where(match, last, done)
        stop = (at + PER_ITEM - 1) // PER_ITEM * PER_ITEM

        def fill(i, carry):
            item_block[i] = item_block[begin]
            return carry

        def name(i, carry):
            item_group[i] = g
            return carry

        lax.fori_loop(at, stop, fill, 0)
        lax.fori_loop(begin // PER_ITEM, stop // PER_ITEM, name, 0)
        return stop

    return lax.fori_loop(0, G, of_group, jnp.int32(0)) // PER_ITEM


def prefix_kernel(
    sc_ref, shape_a, shape_b, q0, q1, pk, pv, other, o_ref, lse_ref,
    q_ref, ka, kb, va, vb, grp, lse, sa, sb, ta, tb, item_group, item_block, sems,
):
    tokens = q_ref.shape[0]
    span = ka.shape[1]
    shapes = ((shape_a, 0), (shape_b, 0))
    mine = pl.ds(pl.multiple_of(sc_ref[0] * HEAD, HEAD), HEAD)
    copies = [
        pltpu.make_async_copy(q0.at[:, mine], q_ref.at[:ROW_TOK, :], sems.at[0]),
        pltpu.make_async_copy(q1.at[0], q_ref.at[ROW_TOK:, :], sems.at[1]),
        pltpu.make_async_copy(pk.at[:, :, mine], ka, sems.at[2]),
        pltpu.make_async_copy(other.at[0], kb, sems.at[3]),
        pltpu.make_async_copy(pv.at[:, :, mine], va, sems.at[4]),
        pltpu.make_async_copy(other.at[1], vb, sems.at[5]),
    ]
    for copy in copies:
        copy.start()
    for r, (shape, at) in enumerate(shapes):
        token = lax.broadcasted_iota(jnp.int32, (ROW_TOK, HEAD), 0)
        group = jnp.full((ROW_TOK, HEAD), shape[at, RQ], jnp.int32)
        start = 0
        for j in range(1, RQ):
            start = start + shape[at, j - 1]
            group = jnp.where(token >= start, shape[at, RQ + j], group)
        grp[r * ROW_TOK : (r + 1) * ROW_TOK, :] = group
    count = build_work(shapes, item_group, item_block)
    for copy in copies:
        copy.wait()
    step = 512

    def held(item):
        return jnp.where(item < count, item, 0)

    def places(item):
        at = held(item) * PER_ITEM
        return [
            pl.ds(pl.multiple_of(item_block[at + i] * SUB, SUB), SUB) for i in range(PER_ITEM)
        ]

    def group_of(item):
        return item_group[held(item)]

    def lanes(x, op):
        parts = [x[:, c : c + HEAD] for c in range(0, x.shape[1], HEAD)]
        while len(parts) > 1:
            parts = [op(a, b) for a, b in zip(parts[::2], parts[1::2])]
        return parts[0]

    def score(item, s, tops):
        g = group_of(item)
        q = jnp.concatenate([q_ref[place, :] for place in places(item)], axis=0)
        for half, k in enumerate((ka, kb)):
            for c in range(0, span, step):
                x = lax.dot_general(
                    q,
                    k[g, c : c + step, :],
                    (((1,), (1,)), ((), ())),
                    preferred_element_type=jnp.float32,
                )
                s[:, half * span + c : half * span + c + step] = x
                top = lanes(x, jnp.maximum)
                tops[...] = top if half == 0 and c == 0 else jnp.maximum(tops[...], top)

    def weigh(item, s, tops):
        g = group_of(item)
        where = places(item)
        for part in range(2):
            here = slice(part * BLK, (part + 1) * BLK)
            top = jnp.max(tops[here, :], axis=1, keepdims=True)
            out = jnp.zeros((BLK, HEAD), jnp.float32)
            total = jnp.zeros((BLK, HEAD), jnp.float32)
            for half, v in enumerate((va, vb)):
                for c in range(0, span, step):
                    x = s[here, half * span + c : half * span + c + step]
                    p = jnp.exp2((x - top) * SCORE_SCALE)
                    total = total + lanes(p, jnp.add)
                    out = out + jnp.dot(
                        p.astype(jnp.bfloat16),
                        v[g, c : c + step, :],
                        preferred_element_type=jnp.float32,
                    )
            total = jnp.sum(total, axis=1, keepdims=True)
            out = out * (1.0 / total)
            here_lse = jnp.broadcast_to(top * SCORE_SCALE + jnp.log2(total), (BLK, HEAD))
            for i in range(BLK // SUB):
                place = where[part * (BLK // SUB) + i]
                sub = slice(i * SUB, (i + 1) * SUB)
                mine = grp[place, :] == g
                o_ref[place, :] = jnp.where(
                    mine, out[sub], o_ref[place, :].astype(jnp.float32)
                ).astype(o_ref.dtype)
                lse[place, :] = jnp.where(mine, here_lse[sub], lse[place, :])

    score(0, sa, ta)

    def pair(i, carry):
        score(2 * i + 1, sb, tb)
        weigh(2 * i, sa, ta)

        @pl.when(2 * i + 1 < count)
        def second():
            score(2 * i + 2, sa, ta)
            weigh(2 * i + 1, sb, tb)

        return carry

    lax.fori_loop(0, (count + 1) // 2, pair, 0)
    for b in range(tokens // BLK):
        lse_ref[b // 8, b % 8 : b % 8 + 1, :] = jnp.transpose(lse[b * BLK : (b + 1) * BLK, :])[
            0:1, :
        ]


def prefix_attend(place, shape_a, shape_b, q0, q1, pk, pv, other, out_dtype):
    rows = 2
    tokens = rows * ROW_TOK
    span = pk.shape[1]
    blocks = ROW_TOK // BLK
    smem = pl.BlockSpec(memory_space=pltpu.SMEM)
    vmem = pl.BlockSpec(memory_space=pltpu.VMEM)
    anywhere = pl.BlockSpec(memory_space=pl.ANY)
    prefix_buffer = pltpu.VMEM((G, span, HEAD), pk.dtype)
    per_token = pltpu.VMEM((tokens, HEAD), jnp.float32)
    scores = pltpu.VMEM((PER_ITEM * SUB, 2 * span), jnp.float32)
    tops = pltpu.VMEM((PER_ITEM * SUB, HEAD), jnp.float32)
    return pl.pallas_call(
        prefix_kernel,
        in_specs=[smem] * 3 + [anywhere] * 5,
        out_specs=(vmem, vmem),
        out_shape=(
            jax.ShapeDtypeStruct((tokens, HEAD), out_dtype),
            jax.ShapeDtypeStruct((rows, blocks, BLK), jnp.float32),
        ),
        scratch_shapes=[
            pltpu.VMEM((tokens, HEAD), q0.dtype),
            prefix_buffer,
            prefix_buffer,
            prefix_buffer,
            prefix_buffer,
            pltpu.VMEM((tokens, HEAD), jnp.int32),
            per_token,
            scores,
            scores,
            tops,
            tops,
            pltpu.SMEM((ITEMS,), jnp.int32),
            pltpu.SMEM((ITEMS * PER_ITEM,), jnp.int32),
            pltpu.SemaphoreType.DMA((6,)),
        ],
        compiler_params=pltpu.CompilerParams(vmem_limit_bytes=VMEM_BIG),
        cost_estimate=pl.CostEstimate(
            flops=tokens * span * HEAD * 8 * 4,
            bytes_accessed=4 * G * span * HEAD * 2,
            transcendentals=0,
        ),
        name="prefix_attend",
    )(place, shape_a, shape_b, q0, q1, pk, pv, other)


def suffix_kernel(sc_ref, shape_a, shape_b, q, k, v, other_row, o_ref, lse_ref):
    count = ROW_TOK // SUF
    rows = ((shape_a, (q, k, v)), (shape_b, [other_row.at[i] for i in range(3)]))
    for row, (shape, qkv) in enumerate(rows):
        token = lax.broadcasted_iota(jnp.int32, (ROW_TOK, 1), 0)
        first = jnp.zeros((ROW_TOK, 1), jnp.int32)
        start = 0
        for j in range(1, RQ):
            start = start + shape[0, j - 1]
            first = jnp.where(token >= start, start, first)

        def bounds(i):
            low = max(0, i * SUF - ROW_TOK // 2)
            return low, slice(i * SUF, (i + 1) * SUF), slice(low, (i + 1) * SUF)

        def score(i, qkv=qkv, first=first, token=token):
            low, here, seen = bounds(i)
            s = lax.dot_general(
                qkv[0][here, :],
                qkv[1][seen, :],
                (((1,), (1,)), ((), ())),
                preferred_element_type=jnp.float32,
            )
            other = low + lax.broadcasted_iota(jnp.int32, s.shape, 1)
            return jnp.where((other >= first[here]) & (other <= token[here]), s, NEG)

        def weigh(i, s, row=row, qkv=qkv):
            unused, here, seen = bounds(i)
            top = jnp.max(s, axis=1, keepdims=True)
            p = jnp.exp2((s - top) * SCORE_SCALE)
            total = jnp.sum(p, axis=1, keepdims=True)
            out = jnp.dot(
                p.astype(jnp.bfloat16), qkv[2][seen, :], preferred_element_type=jnp.float32
            )
            o_ref[row * ROW_TOK + i * SUF : row * ROW_TOK + (i + 1) * SUF, :] = out * (1.0 / total)
            lse = top * SCORE_SCALE + jnp.log2(total)
            for part in range(SUF // BLK):
                at = i * (SUF // BLK) + part
                lse_ref[row, at : at + 1, :] = as_row(lse[part * BLK : (part + 1) * BLK])

        held = score(0)
        for i in range(count):
            later = score(i + 1) if i + 1 < count else None
            weigh(i, held)
            held = later


def suffix_attend(place, shape_a, shape_b, q, k, v, other):
    rows, tokens = 2, q.shape[0]
    blocks = tokens // BLK
    smem = pl.BlockSpec(memory_space=pltpu.SMEM)
    mine = pl.BlockSpec((tokens, HEAD), lambda i, s: (0, s[0]))
    return pl.pallas_call(
        suffix_kernel,
        grid_spec=pltpu.PrefetchScalarGridSpec(
            num_scalar_prefetch=1,
            grid=(1,),
            in_specs=[smem, smem]
            + [mine] * 3
            + [pl.BlockSpec((3, tokens, HEAD), lambda i, s: (0, 0, 0))],
            out_specs=[
                pl.BlockSpec((rows * tokens, HEAD), lambda i, s: (0, 0)),
                pl.BlockSpec((rows, blocks, BLK), lambda i, s: (0, 0, 0)),
            ],
        ),
        out_shape=(
            jax.ShapeDtypeStruct((rows * tokens, HEAD), jnp.float32),
            jax.ShapeDtypeStruct((rows, blocks, BLK), jnp.float32),
        ),
        compiler_params=pltpu.CompilerParams(vmem_limit_bytes=VMEM_BIG),
        cost_estimate=pl.CostEstimate(
            flops=rows * tokens * tokens * HEAD * 4 * 4, bytes_accessed=1 << 20, transcendentals=0
        ),
        name="suffix_attend",
    )(place, shape_a, shape_b, q, k, v, other)


def merge_kernel(sc_ref, *refs):
    parts, tab_ref, out_ref = refs[:-2], refs[-2], refs[-1]
    block = pl.program_id(0)
    out_ref[0, 2 * BLK :, :] = tab_ref[...]
    half = len(parts) // 2
    for row in range(2):
        sources = parts[row * half : (row + 1) * half]
        lses = [
            jnp.transpose(jnp.broadcast_to(lse[0, pl.ds(block, 1), :], (BLK, BLK)))
            for lse in sources[1::2]
        ]
        top = lses[0]
        for lse in lses[1:]:
            top = jnp.maximum(top, lse)
        total, summed = 0.0, 0.0
        for lse, o in zip(lses, sources[0::2]):
            weight = jnp.exp2(lse - top)
            total = total + weight
            summed = summed + weight * o[...].astype(jnp.float32)
        out_ref[0, row * BLK : (row + 1) * BLK, :] = (summed / total).astype(out_ref.dtype)


def merge_parts(place, parts, tab):
    extra = tab.shape[0]
    blocks = ROW_TOK // BLK
    specs, operands = [], []
    for row in range(2):
        for o, lse in parts:
            operands += [o, lse]
            specs += [
                pl.BlockSpec((BLK, HEAD), lambda b, s, row=row: (row * blocks + b, 0)),
                pl.BlockSpec((1, blocks, BLK), lambda b, s, row=row: (row, 0, 0)),
            ]
    return pl.pallas_call(
        merge_kernel,
        grid_spec=pltpu.PrefetchScalarGridSpec(
            num_scalar_prefetch=1,
            grid=(blocks,),
            in_specs=specs + [pl.BlockSpec((extra, BLK), lambda b, s: (0, 0))],
            out_specs=pl.BlockSpec((1, 2 * BLK + extra, HEAD), lambda b, s: (b ^ s[1], 0, 0)),
        ),
        out_shape=jax.ShapeDtypeStruct((blocks, 2 * BLK + extra, HEAD), jnp.bfloat16),
        compiler_params=pltpu.CompilerParams(vmem_limit_bytes=VMEM_SMALL),
        name="merge_parts",
    )(place, *operands, tab)


def exchange_heads(attended):
    heads = [attended[:2]]
    for d in range(1, attended.shape[0] // 2):
        heads.append(
            lax.ppermute(
                attended[2 * d : 2 * d + 2], "exp", [(i, i ^ (2 * d)) for i in range(8)]
            )
        )
    return heads


def project_kernel(sc_ref, *refs):
    heads, weights, outs, lhs = refs[:4], refs[4], refs[5:9], refs[9]
    z_here = sc_ref[1] // 2
    for d, part in enumerate(heads):
        columns = pl.ds(pl.multiple_of((z_here ^ d) * HEAD, HEAD), HEAD)
        for row in range(2):
            for chunk in range(2):
                to = (2 * row + chunk) * BLK
                lhs[to : to + BLK, columns] = part[chunk, row * BLK : (row + 1) * BLK, :]
    tile = 512
    for low in range(0, weights.shape[1], tile):
        here = slice(low, low + tile)
        out = jnp.dot(lhs[...], weights[:, here], preferred_element_type=jnp.float32)
        for i, out_ref in enumerate(outs):
            out_ref[:, here] = out[i * BLK : (i + 1) * BLK].astype(out_ref.dtype)


def project(place, heads, weights):
    depth, width = weights.shape
    smem = pl.BlockSpec(memory_space=pltpu.SMEM)
    vmem = pl.BlockSpec(memory_space=pltpu.VMEM)
    return pl.pallas_call(
        project_kernel,
        in_specs=[smem] + [vmem] * 5,
        out_specs=[vmem] * 4,
        out_shape=[
            jax.ShapeDtypeStruct((BLK, width), dtype)
            for dtype in (jnp.float32, jnp.bfloat16, jnp.bfloat16, jnp.bfloat16)
        ],
        scratch_shapes=[pltpu.VMEM((4 * BLK, depth), jnp.bfloat16)],
        compiler_params=pltpu.CompilerParams(vmem_limit_bytes=VMEM_SMALL),
        name="project",
    )(place, *heads, weights)


def norm_kernel(keep, got, late, residual, gain, stream_ref, normed_ref):
    stream = residual[...].astype(jnp.float32) + (
        keep[...] + got[...].astype(jnp.float32) + late[...].astype(jnp.float32)
    )
    meansq = jnp.mean(stream * stream, axis=-1, keepdims=True)
    stream_ref[...] = stream
    normed = stream * lax.rsqrt(meansq + 1e-06) * gain[...].astype(jnp.float32)
    normed_ref[...] = normed.astype(normed_ref.dtype)


def norm_rows(keep, got, late, residual, gain):
    return pl.pallas_call(
        norm_kernel,
        out_shape=(
            jax.ShapeDtypeStruct(keep.shape, jnp.float32),
            jax.ShapeDtypeStruct(keep.shape, jnp.bfloat16),
        ),
        compiler_params=pltpu.CompilerParams(vmem_limit_bytes=VMEM_SMALL),
        name="norm_rows",
    )(keep, got, late, residual, gain)


EXP_DEV = 4
VMEM_STAGE = 2 * 1024 * 1024
EXPERT_VMEM = 8 * 1024 * 1024
SLOTS = 32
SLOTS_XOR = (0, 2, 4, 6, 1, 3, 5, 7)


def route_kernel(sc_ref, *refs):
    own, other, pick_ref, give_ref = refs
    before = (
        lax.broadcasted_iota(jnp.int32, (BLK, BLK), 0)
        < lax.broadcasted_iota(jnp.int32, (BLK, BLK), 1)
    ).astype(jnp.bfloat16)
    place = lax.broadcasted_iota(jnp.int32, (SLOTS, BLK), 0).astype(jnp.float32)
    place_here = sc_ref[1]
    for slot, offset in enumerate(SLOTS_XOR):
        tab = (own if offset % 2 == 0 else other)[offset // 2].astype(jnp.float32)
        ids, gates = tab[:TOPK], tab[TOPK : 2 * TOPK]
        chosen, weights = [], []
        for j in range(EXP_DEV):
            match = ids == (place_here * EXP_DEV + j).astype(jnp.float32)
            chosen.append(jnp.sum(match.astype(jnp.float32), axis=0, keepdims=True))
            weights.append(jnp.sum(jnp.where(match, gates, 0.0), axis=0, keepdims=True))
        held = jnp.concatenate(chosen + chosen, axis=0)
        places = jnp.dot(held.astype(jnp.bfloat16), before, preferred_element_type=jnp.float32)
        places = jnp.where(held > 0.5, places, -1.0)
        hits = [place == places[j : j + 1] for j in range(EXP_DEV)]
        pick_ref[slot] = jnp.concatenate(
            [hit.astype(jnp.float32) for hit in hits], axis=0
        ).astype(jnp.bfloat16)
        spread = jnp.concatenate(
            [jnp.where(hit, weight, 0.0) for hit, weight in zip(hits, weights)], axis=0
        )
        give_ref[slot] = jnp.transpose(spread).astype(jnp.bfloat16)


def route(place, own, other):
    shape = jax.ShapeDtypeStruct((8, BLK, EXP_DEV * SLOTS), jnp.bfloat16)
    vmem = pl.BlockSpec(memory_space=pltpu.VMEM)
    return pl.pallas_call(
        route_kernel,
        in_specs=[pl.BlockSpec(memory_space=pltpu.SMEM), vmem, vmem],
        out_specs=[vmem, vmem],
        out_shape=(shape, shape),
        compiler_params=pltpu.CompilerParams(vmem_limit_bytes=VMEM_SMALL),
        name="route",
    )(place, own, other)


def stage_kernel(source, held, sems):
    copies = [pltpu.make_async_copy(source.at[i], held.at[i], sems.at[i]) for i in range(EXP_DEV)]
    for copy in copies:
        copy.start()
    for copy in copies:
        copy.wait()


def stage(weights):
    return pl.pallas_call(
        stage_kernel,
        in_specs=[pl.BlockSpec(memory_space=pltpu.HBM)],
        out_specs=pl.BlockSpec(memory_space=pltpu.VMEM),
        out_shape=jax.ShapeDtypeStruct(weights.shape, weights.dtype),
        scratch_shapes=[pltpu.SemaphoreType.DMA((EXP_DEV,))],
        compiler_params=pltpu.CompilerParams(vmem_limit_bytes=VMEM_STAGE),
        cost_estimate=pl.CostEstimate(flops=0, bytes_accessed=2 * weights.size, transcendentals=0),
        name="stage",
    )(weights)


def experts_kernel(*refs):
    picked = refs[:8]
    give_ref, wg, wu, wd = refs[8:12]
    outs, rows_out = refs[12:-1], refs[-1]
    contract = (((1,), (1,)), ((), ()))

    def run(expert, carry):
        here = pl.ds(pl.multiple_of(expert * SLOTS, SLOTS), SLOTS)
        rows = jnp.concatenate([part[here, :] for part in picked], axis=0)
        gate_h = lax.dot_general(wg[expert], rows, contract, preferred_element_type=jnp.float32)
        up_h = lax.dot_general(wu[expert], rows, contract, preferred_element_type=jnp.float32)
        hidden = jnp.transpose((gate_h / (1.0 + jnp.exp(-gate_h)) * up_h).astype(jnp.bfloat16))
        out = jnp.dot(hidden, wd[expert], preferred_element_type=jnp.float32).astype(jnp.bfloat16)
        for slot in range(8):
            rows_out[slot, here, :] = out[slot * SLOTS : (slot + 1) * SLOTS]
        return carry

    lax.fori_loop(0, EXP_DEV, run, 0)
    for slot in range(8):
        out = jnp.dot(give_ref[slot], rows_out[slot], preferred_element_type=jnp.float32)
        out = out.astype(jnp.bfloat16)
        if slot < 7:
            outs[slot][...] = out
        else:
            outs[7][...] = out[: BLK // 2]
            outs[8][...] = out[BLK // 2 :]


def run_experts(picked, give, w_gate, w_up, w_down):
    width = picked[0].shape[1]
    heights = [BLK] * 7 + [BLK // 2] * 2
    vmem = pl.BlockSpec(memory_space=pltpu.VMEM)
    return pl.pallas_call(
        experts_kernel,
        in_specs=[vmem] * 12,
        out_specs=[vmem] * 9,
        out_shape=[jax.ShapeDtypeStruct((n, width), jnp.bfloat16) for n in heights],
        scratch_shapes=[pltpu.VMEM((8, EXP_DEV * SLOTS, width), jnp.bfloat16)],
        compiler_params=pltpu.CompilerParams(vmem_limit_bytes=EXPERT_VMEM),
        name="experts",
    )(*picked, give, w_gate, w_up, w_down)


def together(*arrays):
    return lax.optimization_barrier(arrays)


def gather_rows(middle, own, weights):
    half = own.shape[0] // 2
    own, *weights = together(own, *weights)
    outer0, middle0, there0, gate = together(
        outer_swap(own), middle_swap(own), y_swap(own), stage(weights[0])
    )
    outer1, middle1, there1, down = together(
        outer_swap(middle0), middle_swap(outer0), y_swap(outer0), stage(weights[2])
    )
    second = jnp.where(middle, middle1, outer1)
    outer2, there2 = together(outer_swap(middle1), y_swap(second))
    third = jnp.where(middle, middle0, outer2)
    there3, late_outer, late_middle = together(
        y_swap(third[:half]), outer_swap(there2[half:]), middle_swap(there0[half:])
    )
    late = jnp.where(middle, late_middle, late_outer)
    return [own, outer0, second, third], [there0, there1, there2, there3, late], (gate, weights[1], down)


def pick_rows(pick, parts):
    picked = [
        jnp.dot(matrix, part, preferred_element_type=jnp.float32)
        for matrix, part in zip(pick, parts[:4])
        if part.shape[0] == matrix.shape[1]
    ]
    if len(parts) == 5:
        half = parts[3].shape[0]
        picked.append(
            jnp.dot(pick[3][:, :half], parts[3], preferred_element_type=jnp.float32)
            + jnp.dot(pick[3][:, half:], parts[4], preferred_element_type=jnp.float32)
        )
    return [part.astype(jnp.bfloat16) for part in picked]


def scatter_sums(middle, stream, own, there):
    half = there[3].shape[0]

    def plus(*parts):
        total = parts[0].astype(jnp.float32)
        for part in parts[1:]:
            total = total + part.astype(jnp.float32)
        return total

    def plus16(*parts):
        return plus(*parts).astype(jnp.bfloat16)

    def in_middle(array):
        return jnp.where(middle, array.astype(jnp.float32), 0.0)

    got, late_outer, late_middle = together(
        y_swap(there[3]), outer_swap(there[4]), middle_swap(there[4])
    )
    sum3 = jnp.concatenate([plus16(own[3][:half], got), own[3][half:]], axis=0)
    there2 = jnp.concatenate(
        [there[2][:half], plus16(there[2][half:], in_middle(late_outer))], axis=0
    )
    there0 = jnp.concatenate(
        [there[0][:half], plus16(there[0][half:], in_middle(late_middle))], axis=0
    )
    got, outer = together(y_swap(there2), outer_swap(sum3))
    sum2 = plus16(own[2], got, in_middle(outer))
    got, outer, across = together(y_swap(there[1]), outer_swap(sum2), middle_swap(sum2))
    sum1 = plus16(own[1], got, in_middle(across))
    sum3 = plus16(sum3, in_middle(outer))
    got, outer, across = together(y_swap(there0), outer_swap(sum1), middle_swap(sum3))
    return plus(stream, own[0], got, outer, in_middle(across))


def block_device(
    queries,
    keys,
    values,
    prefix_keys,
    prefix_values,
    lengths,
    groups,
    residual,
    out_proj,
    norm_gain,
    expert_ids,
    expert_gates,
    w_gate,
    w_up,
    w_down,
):
    core = lax.rem(lax.axis_index("req"), 2)
    z = lax.axis_index("exp") // 2
    middle = (z == 1) | (z == 2)
    place = jnp.stack([core, lax.axis_index("exp")]).astype(jnp.int32)

    shape = jnp.concatenate([lengths, groups], axis=1)
    other_shape = core_swap(shape)
    far_shape = x_swap(shape)
    far_queries = x_swap(queries)

    proj_rows = gather_z(lax.dynamic_slice_in_dim(out_proj, core * HEAD, HEAD, 0))

    theirs, prefix_theirs = split_theirs(place, queries, keys, values, prefix_keys, prefix_values)
    other, prefix_other = core_swap(theirs), core_swap(prefix_theirs)

    def prefix(shape_a, shape_b, q0, q1, dtype):
        return prefix_attend(
            place, shape_a, shape_b, q0, q1, prefix_keys, prefix_values, prefix_other, dtype
        )

    tab = jnp.concatenate([expert_ids.T.astype(jnp.bfloat16), expert_gates.T], axis=0)
    tab = jnp.pad(tab, ((0, 16 - tab.shape[0]), (0, 0)))
    suffix = suffix_attend(place, shape, other_shape, queries, keys, values, other)
    unused, far_queries, far_shape = together(suffix[1], far_queries, far_shape)
    far_send = jnp.where(core == 0, far_queries[:, HEAD:], far_queries[:, :HEAD])[None]
    far_other, far_other_shape = core_swap(far_send), core_swap(far_shape)
    far = prefix(far_shape, far_other_shape, far_queries, far_other, jnp.bfloat16)
    back = (x_swap(far[0]), x_swap(far[1]))
    near = prefix(shape, other_shape, queries, other, jnp.float32)
    near_o, gain = together(near[0], norm_gain.reshape(1, -1))
    attended = merge_parts(place, [suffix, (near_o, near[1]), back], tab)
    heads = exchange_heads(attended)
    tabs = jnp.stack([part[0, 2 * BLK :, :] for part in heads])
    keep, pair, send, send_pair = project(place, heads, proj_rows)
    send_pair, tabs, other_tabs = together(send_pair, tabs, y_swap(tabs))
    pair = pair.astype(jnp.float32) + core_swap(send_pair).astype(jnp.float32)
    late = y_swap(pair.astype(jnp.bfloat16))
    stream, normed = norm_rows(keep, core_swap(send), late, residual, gain)
    pick, give = route(place, tabs, other_tabs)
    weights = (w_gate.transpose(0, 2, 1), w_up.transpose(0, 2, 1), w_down)
    here, there, weights = gather_rows(middle, normed, weights)
    picked = pick_rows(pick[:4], here) + pick_rows(pick[4:], there)
    sums = run_experts(picked, give, *weights)
    return scatter_sums(middle, stream, sums[:4], sums[4:]).astype(jnp.bfloat16)


def solution(mesh):
    in_specs = (
        P("req", "exp"),
        P("req", "exp"),
        P("req", "exp"),
        P(None, "req", "exp"),
        P(None, "req", "exp"),
        P("req", None),
        P("req", None),
        P(("req", "exp"), None),
        P("exp", None),
        P(),
        P(("req", "exp"), None),
        P(("req", "exp"), None),
        P("exp", None, None),
        P("exp", None, None),
        P("exp", None, None),
    )
    out_specs = P(("req", "exp"), None)
    blocked = mesh.shape["req"] == 4 and mesh.shape["exp"] == 8
    return jax.shard_map(
        block_device if blocked else general_device,
        mesh=mesh,
        in_specs=in_specs,
        out_specs=out_specs,
        check_vma=False,
    )
```

```python
import math

import jax
import jax.numpy as jnp
from jax import lax
from jax.experimental import pallas as pl
from jax.experimental.pallas import tpu as pltpu
from jax.sharding import PartitionSpec as P

HEAD = 128
TOPK = 4
EXPERTS = 32
G = 4
RQ = 8
ROW_TOK = 1024


NEG = -1e30


def token_layout(lengths, groups):
    req_ends = jnp.cumsum(lengths, axis=-1)
    starts = req_ends - lengths
    position = jnp.arange(ROW_TOK, dtype=jnp.int32)
    request = jnp.sum((position[None, :, None] >= req_ends[:, None, :]).astype(jnp.int32), axis=-1)
    onehot = request[:, :, None] == jnp.arange(RQ, dtype=jnp.int32)[None, None, :]
    first_tok = jnp.sum(jnp.where(onehot, starts[:, None, :], 0), axis=-1)
    tok_group = jnp.sum(jnp.where(onehot, groups[:, None, :], 0), axis=-1)
    return (request, position[None, :] - first_tok, tok_group)


def split_blocks(row_count):
    if row_count % 1024 == 0 and row_count > 1024:
        return row_count // 1024
    return 1


def pack_parts(parts):
    return jnp.concatenate([parts[0], parts[1], parts[2]], axis=1)


def unpack_parts(packed, head_count):
    columns = head_count * HEAD
    return (
        packed[:, :columns],
        packed[:, columns : columns + head_count],
        packed[:, columns + head_count :],
    )


def attend_prefix(query_rows, query_group, prefix_k, prefix_v):
    row_count, columns = query_rows.shape
    head_count = columns // HEAD
    span = prefix_k.shape[1]
    key_grid = prefix_k.reshape(G, span, head_count, HEAD)
    val_grid = prefix_v.reshape(G, span, head_count, HEAD)
    blocks = split_blocks(row_count)
    block_len = row_count // blocks
    scaling = 1.0 / math.sqrt(HEAD)

    def per_block(pieces):
        block_q, block_g = pieces
        query_grid = block_q.reshape(block_len, head_count, HEAD)
        scores = (
            jnp.einsum("qhd,gkhd->hqgk", query_grid, key_grid, preferred_element_type=jnp.float32)
            * scaling
        )
        member = block_g[:, None] == jnp.arange(G, dtype=jnp.int32)[None, :]
        scores = jnp.where(member[None, :, :, None], scores, NEG)
        maxima = jnp.max(scores, axis=(2, 3))
        exp_terms = jnp.exp(scores - maxima[:, :, None, None])
        totals = jnp.sum(exp_terms, axis=(2, 3))
        weighted = jnp.einsum(
            "hqgk,gkhd->qhd",
            exp_terms.astype(jnp.bfloat16),
            val_grid,
            preferred_element_type=jnp.float32,
        )
        return (weighted.reshape(block_len, columns), maxima.T, totals.T)

    weighted, maxima, totals = lax.map(
        per_block,
        (query_rows.reshape(blocks, block_len, columns), query_group.reshape(blocks, block_len)),
    )
    return (
        weighted.reshape(row_count, columns),
        maxima.reshape(row_count, head_count),
        totals.reshape(row_count, head_count),
    )


def attend_suffix(queries, keys, values, request, position):
    row_count, columns = queries.shape
    head_count = columns // HEAD
    blocks = split_blocks(row_count)
    block_len = row_count // blocks
    scaling = 1.0 / math.sqrt(HEAD)
    key_grid = keys.reshape(row_count, head_count, HEAD)
    val_grid = values.reshape(row_count, head_count, HEAD)

    def per_block(pieces):
        block_q, block_req, block_pos = pieces
        query_grid = block_q.reshape(block_len, head_count, HEAD)
        scores = (
            jnp.einsum("qhd,khd->hqk", query_grid, key_grid, preferred_element_type=jnp.float32)
            * scaling
        )
        allowed = (request[None, :] == block_req[:, None]) & (
            position[None, :] <= block_pos[:, None]
        )
        scores = jnp.where(allowed[None, :, :], scores, NEG)
        maxima = jnp.max(scores, axis=2)
        exp_terms = jnp.exp(scores - maxima[:, :, None])
        totals = jnp.sum(exp_terms, axis=2)
        weighted = jnp.einsum(
            "hqk,khd->qhd",
            exp_terms.astype(jnp.bfloat16),
            val_grid,
            preferred_element_type=jnp.float32,
        )
        return (weighted.reshape(block_len, columns), maxima.T, totals.T)

    weighted, maxima, totals = lax.map(
        per_block,
        (
            queries.reshape(blocks, block_len, columns),
            request.reshape(blocks, block_len),
            position.reshape(blocks, block_len),
        ),
    )
    return (
        weighted.reshape(row_count, columns),
        maxima.reshape(row_count, head_count),
        totals.reshape(row_count, head_count),
    )


def combine(former, latter):
    weighted_a, maxima_a, totals_a = former
    weighted_b, maxima_b, totals_b = latter
    row_count, head_count = maxima_a.shape
    maxima = jnp.maximum(maxima_a, maxima_b)
    factor_a = jnp.exp(maxima_a - maxima)
    factor_b = jnp.exp(maxima_b - maxima)
    weighted = (
        weighted_a.reshape(row_count, head_count, HEAD) * factor_a[:, :, None]
        + weighted_b.reshape(row_count, head_count, HEAD) * factor_b[:, :, None]
    )
    return (
        weighted.reshape(row_count, head_count * HEAD),
        maxima,
        totals_a * factor_a + totals_b * factor_b,
    )


def general_device(
    queries,
    keys,
    values,
    prefix_keys,
    prefix_values,
    lengths,
    groups,
    residual,
    out_proj,
    norm_gain,
    expert_ids,
    expert_gates,
    w_gate,
    w_up,
    w_down,
):
    row_tok, columns = queries.shape
    head_count = columns // HEAD
    tok_dev = residual.shape[0]
    request, position, tok_group = token_layout(lengths, groups)
    request, position, tok_group = (request[0], position[0], tok_group[0])
    all_groups = lax.all_gather(tok_group, "req", axis=0, tiled=True)
    partial_value = pack_parts(
        attend_prefix(
            lax.all_gather(queries, "req", axis=0, tiled=True),
            all_groups,
            prefix_keys,
            prefix_values,
        )
    )
    returned = lax.all_to_all(partial_value, "req", split_axis=0, concat_axis=0, tiled=True)
    owners = returned.shape[0] // row_tok
    back_w, back_m, back_t = unpack_parts(returned, head_count)
    all_weighted = back_w.reshape(owners, row_tok, head_count, HEAD)
    all_maxima = back_m.reshape(owners, row_tok, head_count)
    all_totals = back_t.reshape(owners, row_tok, head_count)
    maxima = jnp.max(all_maxima, axis=0)
    factor = jnp.exp(all_maxima - maxima[None])
    weighted = jnp.sum(all_weighted * factor[..., None], axis=0).reshape(row_tok, columns)
    prefix_part = (weighted, maxima, jnp.sum(all_totals * factor, axis=0))
    suffix_part = attend_suffix(queries, keys, values, request, position)
    weighted, maxima, totals = combine(prefix_part, suffix_part)
    attended = (
        (weighted.reshape(row_tok, head_count, HEAD) / totals[:, :, None])
        .reshape(row_tok, columns)
        .astype(jnp.bfloat16)
    )
    projected = lax.psum_scatter(
        jnp.dot(attended, out_proj, preferred_element_type=jnp.float32),
        "exp",
        scatter_dimension=0,
        tiled=True,
    )
    stream = residual.astype(jnp.float32) + projected
    meansq = jnp.mean(stream * stream, axis=-1, keepdims=True)
    normed = (stream * lax.rsqrt(meansq + 1e-06) * norm_gain.astype(jnp.float32)).astype(
        jnp.bfloat16
    )
    capacity = max(2, tok_dev // 4)
    flat_ids = expert_ids.reshape(-1)
    onehot = (flat_ids[:, None] == jnp.arange(EXPERTS, dtype=jnp.int32)[None, :]).astype(jnp.int32)
    slot_of = jnp.sum(onehot * (jnp.cumsum(onehot, axis=0) - 1), axis=1)
    source_rows = jnp.arange(tok_dev * TOPK, dtype=jnp.int32) // TOPK
    buffer = (
        jnp.zeros((EXPERTS, capacity, normed.shape[1]), jnp.bfloat16)
        .at[flat_ids, slot_of]
        .set(normed[source_rows])
    )
    exp_count = lax.axis_size("exp")
    exp_dev = w_gate.shape[0]
    received = lax.all_to_all(buffer, "exp", split_axis=0, concat_axis=0, tiled=True)
    slots = received.shape[1]
    grid_in = received.reshape(exp_count, exp_dev, slots, received.shape[2])
    gate_h = jnp.einsum("secd,edf->secf", grid_in, w_gate, preferred_element_type=jnp.float32)
    up_h = jnp.einsum("secd,edf->secf", grid_in, w_up, preferred_element_type=jnp.float32)
    hidden = (jax.nn.silu(gate_h) * up_h).astype(jnp.bfloat16)
    expert_out = jnp.einsum("secf,efd->secd", hidden, w_down, preferred_element_type=jnp.float32)
    returned = lax.all_to_all(
        expert_out.reshape(EXPERTS, slots, received.shape[2]),
        "exp",
        split_axis=0,
        concat_axis=0,
        tiled=True,
    )
    gathered = returned[flat_ids, slot_of] * expert_gates.reshape(-1).astype(jnp.float32)[:, None]
    mixture = jnp.sum(gathered.reshape(tok_dev, TOPK, gathered.shape[1]), axis=1)
    return (stream + mixture).astype(jnp.bfloat16)


BLK = 128
LOG2E = 1.4426950408889634
SCORE_SCALE = LOG2E / math.sqrt(HEAD)
VMEM_BIG = 28 * 1024 * 1024
VMEM_MOST = 56 * 1024 * 1024
VMEM_SMALL = 12 * 1024 * 1024


def core_swap(array):
    return lax.ppermute(array, "req", [(i, i ^ 1) for i in range(4)])


def x_swap(array):
    return lax.ppermute(array, "req", [(i, i ^ 2) for i in range(4)])


def y_swap(array):
    return lax.ppermute(array, "exp", [(i, i ^ 1) for i in range(8)])


def outer_swap(array):
    return lax.ppermute(array, "exp", [(i, i ^ 2) for i in range(8)])


def gather_z(array):
    return lax.all_gather(
        array, "exp", axis=0, axis_index_groups=[[0, 2, 4, 6], [1, 3, 5, 7]], tiled=True
    )


def middle_swap(array):
    return lax.ppermute(array, "exp", [(2, 4), (3, 5), (4, 2), (5, 3)])


def split_kernel(sc_ref, q, k, v, pk, pv, out_tokens, out_prefix, sems):
    theirs = pl.ds(pl.multiple_of((1 - sc_ref[0]) * HEAD, HEAD), HEAD)
    copies = [
        pltpu.make_async_copy(part.at[:, theirs], out_tokens.at[i], sems.at[i])
        for i, part in enumerate((q, k, v))
    ]
    for i, part in enumerate((pk, pv)):
        for g in range(G):
            copies.append(
                pltpu.make_async_copy(
                    part.at[g, :, theirs], out_prefix.at[i, g], sems.at[3 + i * G + g]
                )
            )
    for copy in copies:
        copy.start()
    for copy in copies:
        copy.wait()


def split_theirs(place, q, k, v, pk, pv):
    rows, span = q.shape[0], pk.shape[1]
    vmem = pl.BlockSpec(memory_space=pltpu.VMEM)
    return pl.pallas_call(
        split_kernel,
        in_specs=[pl.BlockSpec(memory_space=pltpu.SMEM)]
        + [pl.BlockSpec(memory_space=pl.ANY)] * 5,
        out_specs=[vmem, vmem],
        out_shape=(
            jax.ShapeDtypeStruct((3, rows, HEAD), q.dtype),
            jax.ShapeDtypeStruct((2, G, span, HEAD), q.dtype),
        ),
        scratch_shapes=[pltpu.SemaphoreType.DMA((3 + 2 * G,))],
        compiler_params=pltpu.CompilerParams(vmem_limit_bytes=VMEM_MOST),
        name="split_theirs",
    )(place, q, k, v, pk, pv)


def as_row(column):
    return jnp.transpose(jnp.broadcast_to(column, (BLK, BLK)))[0:1, :]


SUF = 256
SUB = 32
PER_ITEM = 8
ITEMS = 16


def build_work(shapes, item_group, item_block):
    per_row = ROW_TOK // SUB
    spans = []
    for r, (shape, at) in enumerate(shapes):
        start = 0
        for j in range(RQ):
            end = start + shape[at, j]
            first, last = r * per_row + start // SUB, r * per_row + (end - 1) // SUB
            spans.append((first, last, shape[at, RQ + j]))
            start = end

    def of_group(g, begin):
        at, done = begin, jnp.int32(-1)
        for first, last, group in spans:
            first = jnp.maximum(first, done + 1)
            match = group == g
            count = jnp.where(match, last - first + 1, 0)

            def put(i, carry, at=at, first=first):
                item_block[at + i] = first + i
                return carry

            lax.fori_loop(0, count, put, 0)
            at = at + count
            done = jnp.where(match, last, done)
        stop = (at + PER_ITEM - 1) // PER_ITEM * PER_ITEM

        def fill(i, carry):
            item_block[i] = item_block[begin]
            return carry

        def name(i, carry):
            item_group[i] = g
            return carry

        lax.fori_loop(at, stop, fill, 0)
        lax.fori_loop(begin // PER_ITEM, stop // PER_ITEM, name, 0)
        return stop

    return lax.fori_loop(0, G, of_group, jnp.int32(0)) // PER_ITEM


def prefix_kernel(
    sc_ref, shape_a, shape_b, q0, q1, pk, pv, other, o_ref, lse_ref,
    q_ref, ka, kb, va, vb, grp, lse, sa, sb, ta, tb, item_group, item_block, sems,
):
    tokens = q_ref.shape[0]
    span = ka.shape[1]
    shapes = ((shape_a, 0), (shape_b, 0))
    mine = pl.ds(pl.multiple_of(sc_ref[0] * HEAD, HEAD), HEAD)
    copies = [
        pltpu.make_async_copy(q0.at[:, mine], q_ref.at[:ROW_TOK, :], sems.at[0]),
        pltpu.make_async_copy(q1.at[0], q_ref.at[ROW_TOK:, :], sems.at[1]),
        pltpu.make_async_copy(pk.at[:, :, mine], ka, sems.at[2]),
        pltpu.make_async_copy(other.at[0], kb, sems.at[3]),
        pltpu.make_async_copy(pv.at[:, :, mine], va, sems.at[4]),
        pltpu.make_async_copy(other.at[1], vb, sems.at[5]),
    ]
    for copy in copies:
        copy.start()
    for r, (shape, at) in enumerate(shapes):
        token = lax.broadcasted_iota(jnp.int32, (ROW_TOK, HEAD), 0)
        group = jnp.full((ROW_TOK, HEAD), shape[at, RQ], jnp.int32)
        start = 0
        for j in range(1, RQ):
            start = start + shape[at, j - 1]
            group = jnp.where(token >= start, shape[at, RQ + j], group)
        grp[r * ROW_TOK : (r + 1) * ROW_TOK, :] = group
    count = build_work(shapes, item_group, item_block)
    for copy in copies:
        copy.wait()
    step = 512

    def held(item):
        return jnp.where(item < count, item, 0)

    def places(item):
        at = held(item) * PER_ITEM
        return [
            pl.ds(pl.multiple_of(item_block[at + i] * SUB, SUB), SUB) for i in range(PER_ITEM)
        ]

    def group_of(item):
        return item_group[held(item)]

    def lanes(x, op):
        parts = [x[:, c : c + HEAD] for c in range(0, x.shape[1], HEAD)]
        while len(parts) > 1:
            parts = [op(a, b) for a, b in zip(parts[::2], parts[1::2])]
        return parts[0]

    def score(item, s, tops):
        g = group_of(item)
        q = jnp.concatenate([q_ref[place, :] for place in places(item)], axis=0)
        for half, k in enumerate((ka, kb)):
            for c in range(0, span, step):
                x = lax.dot_general(
                    q,
                    k[g, c : c + step, :],
                    (((1,), (1,)), ((), ())),
                    preferred_element_type=jnp.float32,
                )
                s[:, half * span + c : half * span + c + step] = x
                top = lanes(x, jnp.maximum)
                tops[...] = top if half == 0 and c == 0 else jnp.maximum(tops[...], top)

    def weigh(item, s, tops):
        g = group_of(item)
        where = places(item)
        for part in range(2):
            here = slice(part * BLK, (part + 1) * BLK)
            top = jnp.max(tops[here, :], axis=1, keepdims=True)
            out = jnp.zeros((BLK, HEAD), jnp.float32)
            total = jnp.zeros((BLK, HEAD), jnp.float32)
            for half, v in enumerate((va, vb)):
                for c in range(0, span, step):
                    x = s[here, half * span + c : half * span + c + step]
                    p = jnp.exp2((x - top) * SCORE_SCALE)
                    total = total + lanes(p, jnp.add)
                    out = out + jnp.dot(
                        p.astype(jnp.bfloat16),
                        v[g, c : c + step, :],
                        preferred_element_type=jnp.float32,
                    )
            total = jnp.sum(total, axis=1, keepdims=True)
            out = out * (1.0 / total)
            here_lse = jnp.broadcast_to(top * SCORE_SCALE + jnp.log2(total), (BLK, HEAD))
            for i in range(BLK // SUB):
                place = where[part * (BLK // SUB) + i]
                sub = slice(i * SUB, (i + 1) * SUB)
                mine = grp[place, :] == g
                o_ref[place, :] = jnp.where(
                    mine, out[sub], o_ref[place, :].astype(jnp.float32)
                ).astype(o_ref.dtype)
                lse[place, :] = jnp.where(mine, here_lse[sub], lse[place, :])

    score(0, sa, ta)

    def pair(i, carry):
        score(2 * i + 1, sb, tb)
        weigh(2 * i, sa, ta)

        @pl.when(2 * i + 1 < count)
        def second():
            score(2 * i + 2, sa, ta)
            weigh(2 * i + 1, sb, tb)

        return carry

    lax.fori_loop(0, (count + 1) // 2, pair, 0)
    for b in range(tokens // BLK):
        lse_ref[b // 8, b % 8 : b % 8 + 1, :] = jnp.transpose(lse[b * BLK : (b + 1) * BLK, :])[
            0:1, :
        ]


def prefix_attend(place, shape_a, shape_b, q0, q1, pk, pv, other, out_dtype):
    rows = 2
    tokens = rows * ROW_TOK
    span = pk.shape[1]
    blocks = ROW_TOK // BLK
    smem = pl.BlockSpec(memory_space=pltpu.SMEM)
    vmem = pl.BlockSpec(memory_space=pltpu.VMEM)
    anywhere = pl.BlockSpec(memory_space=pl.ANY)
    prefix_buffer = pltpu.VMEM((G, span, HEAD), pk.dtype)
    per_token = pltpu.VMEM((tokens, HEAD), jnp.float32)
    scores = pltpu.VMEM((PER_ITEM * SUB, 2 * span), jnp.float32)
    tops = pltpu.VMEM((PER_ITEM * SUB, HEAD), jnp.float32)
    return pl.pallas_call(
        prefix_kernel,
        in_specs=[smem] * 3 + [anywhere] * 5,
        out_specs=(vmem, vmem),
        out_shape=(
            jax.ShapeDtypeStruct((tokens, HEAD), out_dtype),
            jax.ShapeDtypeStruct((rows, blocks, BLK), jnp.float32),
        ),
        scratch_shapes=[
            pltpu.VMEM((tokens, HEAD), q0.dtype),
            prefix_buffer,
            prefix_buffer,
            prefix_buffer,
            prefix_buffer,
            pltpu.VMEM((tokens, HEAD), jnp.int32),
            per_token,
            scores,
            scores,
            tops,
            tops,
            pltpu.SMEM((ITEMS,), jnp.int32),
            pltpu.SMEM((ITEMS * PER_ITEM,), jnp.int32),
            pltpu.SemaphoreType.DMA((6,)),
        ],
        compiler_params=pltpu.CompilerParams(vmem_limit_bytes=VMEM_BIG),
        cost_estimate=pl.CostEstimate(
            flops=tokens * span * HEAD * 8 * 4,
            bytes_accessed=4 * G * span * HEAD * 2,
            transcendentals=0,
        ),
        name="prefix_attend",
    )(place, shape_a, shape_b, q0, q1, pk, pv, other)


def suffix_kernel(sc_ref, shape_a, shape_b, q, k, v, other_row, o_ref, lse_ref):
    count = ROW_TOK // SUF
    rows = ((shape_a, (q, k, v)), (shape_b, [other_row.at[i] for i in range(3)]))
    for row, (shape, qkv) in enumerate(rows):
        token = lax.broadcasted_iota(jnp.int32, (ROW_TOK, 1), 0)
        first = jnp.zeros((ROW_TOK, 1), jnp.int32)
        start = 0
        for j in range(1, RQ):
            start = start + shape[0, j - 1]
            first = jnp.where(token >= start, start, first)

        def bounds(i):
            low = max(0, i * SUF - ROW_TOK // 2)
            return low, slice(i * SUF, (i + 1) * SUF), slice(low, (i + 1) * SUF)

        def score(i, qkv=qkv, first=first, token=token):
            low, here, seen = bounds(i)
            s = lax.dot_general(
                qkv[0][here, :],
                qkv[1][seen, :],
                (((1,), (1,)), ((), ())),
                preferred_element_type=jnp.float32,
            )
            other = low + lax.broadcasted_iota(jnp.int32, s.shape, 1)
            return jnp.where((other >= first[here]) & (other <= token[here]), s, NEG)

        def weigh(i, s, row=row, qkv=qkv):
            unused, here, seen = bounds(i)
            top = jnp.max(s, axis=1, keepdims=True)
            p = jnp.exp2((s - top) * SCORE_SCALE)
            total = jnp.sum(p, axis=1, keepdims=True)
            out = jnp.dot(
                p.astype(jnp.bfloat16), qkv[2][seen, :], preferred_element_type=jnp.float32
            )
            o_ref[row * ROW_TOK + i * SUF : row * ROW_TOK + (i + 1) * SUF, :] = out * (1.0 / total)
            lse = top * SCORE_SCALE + jnp.log2(total)
            for part in range(SUF // BLK):
                at = i * (SUF // BLK) + part
                lse_ref[row, at : at + 1, :] = as_row(lse[part * BLK : (part + 1) * BLK])

        held = score(0)
        for i in range(count):
            later = score(i + 1) if i + 1 < count else None
            weigh(i, held)
            held = later


def suffix_attend(place, shape_a, shape_b, q, k, v, other):
    rows, tokens = 2, q.shape[0]
    blocks = tokens // BLK
    smem = pl.BlockSpec(memory_space=pltpu.SMEM)
    mine = pl.BlockSpec((tokens, HEAD), lambda i, s: (0, s[0]))
    return pl.pallas_call(
        suffix_kernel,
        grid_spec=pltpu.PrefetchScalarGridSpec(
            num_scalar_prefetch=1,
            grid=(1,),
            in_specs=[smem, smem]
            + [mine] * 3
            + [pl.BlockSpec((3, tokens, HEAD), lambda i, s: (0, 0, 0))],
            out_specs=[
                pl.BlockSpec((rows * tokens, HEAD), lambda i, s: (0, 0)),
                pl.BlockSpec((rows, blocks, BLK), lambda i, s: (0, 0, 0)),
            ],
        ),
        out_shape=(
            jax.ShapeDtypeStruct((rows * tokens, HEAD), jnp.float32),
            jax.ShapeDtypeStruct((rows, blocks, BLK), jnp.float32),
        ),
        compiler_params=pltpu.CompilerParams(vmem_limit_bytes=VMEM_MOST),
        cost_estimate=pl.CostEstimate(
            flops=rows * tokens * tokens * HEAD * 4 * 4, bytes_accessed=1 << 20, transcendentals=0
        ),
        name="suffix_attend",
    )(place, shape_a, shape_b, q, k, v, other)


def merge_kernel(sc_ref, *refs):
    parts, tab_ref, out_ref = refs[:-2], refs[-2], refs[-1]
    block = pl.program_id(0)
    out_ref[0, 2 * BLK :, :] = tab_ref[...]
    half = len(parts) // 2
    for row in range(2):
        sources = parts[row * half : (row + 1) * half]
        lses = [
            jnp.transpose(jnp.broadcast_to(lse[0, pl.ds(block, 1), :], (BLK, BLK)))
            for lse in sources[1::2]
        ]
        top = lses[0]
        for lse in lses[1:]:
            top = jnp.maximum(top, lse)
        total, summed = 0.0, 0.0
        for lse, o in zip(lses, sources[0::2]):
            weight = jnp.exp2(lse - top)
            total = total + weight
            summed = summed + weight * o[...].astype(jnp.float32)
        out_ref[0, row * BLK : (row + 1) * BLK, :] = (summed / total).astype(out_ref.dtype)


def merge_parts(place, parts, tab):
    extra = tab.shape[0]
    blocks = ROW_TOK // BLK
    specs, operands = [], []
    for row in range(2):
        for o, lse in parts:
            operands += [o, lse]
            specs += [
                pl.BlockSpec((BLK, HEAD), lambda b, s, row=row: (row * blocks + b, 0)),
                pl.BlockSpec((1, blocks, BLK), lambda b, s, row=row: (row, 0, 0)),
            ]
    return pl.pallas_call(
        merge_kernel,
        grid_spec=pltpu.PrefetchScalarGridSpec(
            num_scalar_prefetch=1,
            grid=(blocks,),
            in_specs=specs + [pl.BlockSpec((extra, BLK), lambda b, s: (0, 0))],
            out_specs=pl.BlockSpec((1, 2 * BLK + extra, HEAD), lambda b, s: (b ^ s[1], 0, 0)),
        ),
        out_shape=jax.ShapeDtypeStruct((blocks, 2 * BLK + extra, HEAD), jnp.bfloat16),
        compiler_params=pltpu.CompilerParams(vmem_limit_bytes=VMEM_SMALL),
        name="merge_parts",
    )(place, *operands, tab)


def exchange_heads(attended):
    heads = [attended[:2]]
    for d in range(1, attended.shape[0] // 2):
        heads.append(
            lax.ppermute(
                attended[2 * d : 2 * d + 2], "exp", [(i, i ^ (2 * d)) for i in range(8)]
            )
        )
    return heads


def project_kernel(sc_ref, *refs):
    heads, weights, outs, lhs = refs[:4], refs[4], refs[5:9], refs[9]
    z_here = sc_ref[1] // 2
    for d, part in enumerate(heads):
        columns = pl.ds(pl.multiple_of((z_here ^ d) * HEAD, HEAD), HEAD)
        for row in range(2):
            for chunk in range(2):
                to = (2 * row + chunk) * BLK
                lhs[to : to + BLK, columns] = part[chunk, row * BLK : (row + 1) * BLK, :]
    tile = 512
    for low in range(0, weights.shape[1], tile):
        here = slice(low, low + tile)
        out = jnp.dot(lhs[...], weights[:, here], preferred_element_type=jnp.float32)
        for i, out_ref in enumerate(outs):
            out_ref[:, here] = out[i * BLK : (i + 1) * BLK].astype(out_ref.dtype)


def project(place, heads, weights):
    depth, width = weights.shape
    smem = pl.BlockSpec(memory_space=pltpu.SMEM)
    vmem = pl.BlockSpec(memory_space=pltpu.VMEM)
    return pl.pallas_call(
        project_kernel,
        in_specs=[smem] + [vmem] * 5,
        out_specs=[vmem] * 4,
        out_shape=[
            jax.ShapeDtypeStruct((BLK, width), dtype)
            for dtype in (jnp.float32, jnp.bfloat16, jnp.bfloat16, jnp.bfloat16)
        ],
        scratch_shapes=[pltpu.VMEM((4 * BLK, depth), jnp.bfloat16)],
        compiler_params=pltpu.CompilerParams(vmem_limit_bytes=VMEM_SMALL),
        name="project",
    )(place, *heads, weights)


def norm_kernel(keep, got, late, residual, gain, stream_ref, normed_ref):
    stream = residual[...].astype(jnp.float32) + (
        keep[...] + got[...].astype(jnp.float32) + late[...].astype(jnp.float32)
    )
    meansq = jnp.mean(stream * stream, axis=-1, keepdims=True)
    stream_ref[...] = stream
    normed = stream * lax.rsqrt(meansq + 1e-06) * gain[...].astype(jnp.float32)
    normed_ref[...] = normed.astype(normed_ref.dtype)


def norm_rows(keep, got, late, residual, gain):
    return pl.pallas_call(
        norm_kernel,
        out_shape=(
            jax.ShapeDtypeStruct(keep.shape, jnp.float32),
            jax.ShapeDtypeStruct(keep.shape, jnp.bfloat16),
        ),
        compiler_params=pltpu.CompilerParams(vmem_limit_bytes=VMEM_SMALL),
        name="norm_rows",
    )(keep, got, late, residual, gain)


EXP_DEV = 4
VMEM_STAGE = 2 * 1024 * 1024
EXPERT_VMEM = 8 * 1024 * 1024
SLOTS = 32
SLOTS_XOR = (0, 2, 4, 6, 1, 3, 5, 7)


def route_kernel(sc_ref, *refs):
    own, other, pick_ref, give_ref = refs
    before = (
        lax.broadcasted_iota(jnp.int32, (BLK, BLK), 0)
        < lax.broadcasted_iota(jnp.int32, (BLK, BLK), 1)
    ).astype(jnp.bfloat16)
    place = lax.broadcasted_iota(jnp.int32, (SLOTS, BLK), 0).astype(jnp.float32)
    place_here = sc_ref[1]
    for slot, offset in enumerate(SLOTS_XOR):
        tab = (own if offset % 2 == 0 else other)[offset // 2].astype(jnp.float32)
        ids, gates = tab[:TOPK], tab[TOPK : 2 * TOPK]
        chosen, weights = [], []
        for j in range(EXP_DEV):
            match = ids == (place_here * EXP_DEV + j).astype(jnp.float32)
            chosen.append(jnp.sum(match.astype(jnp.float32), axis=0, keepdims=True))
            weights.append(jnp.sum(jnp.where(match, gates, 0.0), axis=0, keepdims=True))
        held = jnp.concatenate(chosen + chosen, axis=0)
        places = jnp.dot(held.astype(jnp.bfloat16), before, preferred_element_type=jnp.float32)
        places = jnp.where(held > 0.5, places, -1.0)
        hits = [place == places[j : j + 1] for j in range(EXP_DEV)]
        pick_ref[slot] = jnp.concatenate(
            [hit.astype(jnp.float32) for hit in hits], axis=0
        ).astype(jnp.bfloat16)
        spread = jnp.concatenate(
            [jnp.where(hit, weight, 0.0) for hit, weight in zip(hits, weights)], axis=0
        )
        give_ref[slot] = jnp.transpose(spread).astype(jnp.bfloat16)


def route(place, own, other):
    shape = jax.ShapeDtypeStruct((8, BLK, EXP_DEV * SLOTS), jnp.bfloat16)
    vmem = pl.BlockSpec(memory_space=pltpu.VMEM)
    return pl.pallas_call(
        route_kernel,
        in_specs=[pl.BlockSpec(memory_space=pltpu.SMEM), vmem, vmem],
        out_specs=[vmem, vmem],
        out_shape=(shape, shape),
        compiler_params=pltpu.CompilerParams(vmem_limit_bytes=VMEM_SMALL),
        name="route",
    )(place, own, other)


def stage_kernel(source, held, sems):
    copies = [pltpu.make_async_copy(source.at[i], held.at[i], sems.at[i]) for i in range(EXP_DEV)]
    for copy in copies:
        copy.start()
    for copy in copies:
        copy.wait()


def stage(weights):
    return pl.pallas_call(
        stage_kernel,
        in_specs=[pl.BlockSpec(memory_space=pltpu.HBM)],
        out_specs=pl.BlockSpec(memory_space=pltpu.VMEM),
        out_shape=jax.ShapeDtypeStruct(weights.shape, weights.dtype),
        scratch_shapes=[pltpu.SemaphoreType.DMA((EXP_DEV,))],
        compiler_params=pltpu.CompilerParams(vmem_limit_bytes=VMEM_STAGE),
        cost_estimate=pl.CostEstimate(flops=0, bytes_accessed=2 * weights.size, transcendentals=0),
        name="stage",
    )(weights)


def experts_kernel(*refs):
    picked = refs[:8]
    give_ref, wg, wu, wd = refs[8:12]
    outs, rows_out = refs[12:-1], refs[-1]
    contract = (((1,), (1,)), ((), ()))

    def run(expert, carry):
        here = pl.ds(pl.multiple_of(expert * SLOTS, SLOTS), SLOTS)
        rows = jnp.concatenate([part[here, :] for part in picked], axis=0)
        gate_h = lax.dot_general(wg[expert], rows, contract, preferred_element_type=jnp.float32)
        up_h = lax.dot_general(wu[expert], rows, contract, preferred_element_type=jnp.float32)
        hidden = jnp.transpose((gate_h / (1.0 + jnp.exp(-gate_h)) * up_h).astype(jnp.bfloat16))
        out = jnp.dot(hidden, wd[expert], preferred_element_type=jnp.float32).astype(jnp.bfloat16)
        for slot in range(8):
            rows_out[slot, here, :] = out[slot * SLOTS : (slot + 1) * SLOTS]
        return carry

    lax.fori_loop(0, EXP_DEV, run, 0)
    for slot in range(8):
        out = jnp.dot(give_ref[slot], rows_out[slot], preferred_element_type=jnp.float32)
        out = out.astype(jnp.bfloat16)
        if slot < 7:
            outs[slot][...] = out
        else:
            outs[7][...] = out[: BLK // 2]
            outs[8][...] = out[BLK // 2 :]


def run_experts(picked, give, w_gate, w_up, w_down):
    width = picked[0].shape[1]
    heights = [BLK] * 7 + [BLK // 2] * 2
    vmem = pl.BlockSpec(memory_space=pltpu.VMEM)
    return pl.pallas_call(
        experts_kernel,
        in_specs=[vmem] * 12,
        out_specs=[vmem] * 9,
        out_shape=[jax.ShapeDtypeStruct((n, width), jnp.bfloat16) for n in heights],
        scratch_shapes=[pltpu.VMEM((8, EXP_DEV * SLOTS, width), jnp.bfloat16)],
        compiler_params=pltpu.CompilerParams(vmem_limit_bytes=EXPERT_VMEM),
        name="experts",
    )(*picked, give, w_gate, w_up, w_down)


def together(*arrays):
    return lax.optimization_barrier(arrays)


def gather_rows(middle, own, weights):
    half = own.shape[0] // 2
    own, *weights = together(own, *weights)
    outer0, middle0, there0, gate = together(
        outer_swap(own), middle_swap(own), y_swap(own), stage(weights[0])
    )
    outer1, middle1, there1, down = together(
        outer_swap(middle0), middle_swap(outer0), y_swap(outer0), stage(weights[2])
    )
    second = jnp.where(middle, middle1, outer1)
    outer2, there2 = together(outer_swap(middle1), y_swap(second))
    third = jnp.where(middle, middle0, outer2)
    there3, late_outer, late_middle = together(
        y_swap(third[:half]), outer_swap(there2[half:]), middle_swap(there0[half:])
    )
    late = jnp.where(middle, late_middle, late_outer)
    return [own, outer0, second, third], [there0, there1, there2, there3, late], (gate, weights[1], down)


def pick_rows(pick, parts):
    picked = [
        jnp.dot(matrix, part, preferred_element_type=jnp.float32)
        for matrix, part in zip(pick, parts[:4])
        if part.shape[0] == matrix.shape[1]
    ]
    if len(parts) == 5:
        half = parts[3].shape[0]
        picked.append(
            jnp.dot(pick[3][:, :half], parts[3], preferred_element_type=jnp.float32)
            + jnp.dot(pick[3][:, half:], parts[4], preferred_element_type=jnp.float32)
        )
    return [part.astype(jnp.bfloat16) for part in picked]


def scatter_sums(middle, stream, own, there):
    half = there[3].shape[0]

    def plus(*parts):
        total = parts[0].astype(jnp.float32)
        for part in parts[1:]:
            total = total + part.astype(jnp.float32)
        return total

    def plus16(*parts):
        return plus(*parts).astype(jnp.bfloat16)

    def in_middle(array):
        return jnp.where(middle, array.astype(jnp.float32), 0.0)

    got, late_outer, late_middle = together(
        y_swap(there[3]), outer_swap(there[4]), middle_swap(there[4])
    )
    sum3 = jnp.concatenate([plus16(own[3][:half], got), own[3][half:]], axis=0)
    there2 = jnp.concatenate(
        [there[2][:half], plus16(there[2][half:], in_middle(late_outer))], axis=0
    )
    there0 = jnp.concatenate(
        [there[0][:half], plus16(there[0][half:], in_middle(late_middle))], axis=0
    )
    got, outer = together(y_swap(there2), outer_swap(sum3))
    sum2 = plus16(own[2], got, in_middle(outer))
    got, outer, across = together(y_swap(there[1]), outer_swap(sum2), middle_swap(sum2))
    sum1 = plus16(own[1], got, in_middle(across))
    sum3 = plus16(sum3, in_middle(outer))
    got, outer, across = together(y_swap(there0), outer_swap(sum1), middle_swap(sum3))
    return plus(stream, own[0], got, outer, in_middle(across))


def block_device(
    queries,
    keys,
    values,
    prefix_keys,
    prefix_values,
    lengths,
    groups,
    residual,
    out_proj,
    norm_gain,
    expert_ids,
    expert_gates,
    w_gate,
    w_up,
    w_down,
):
    core = lax.rem(lax.axis_index("req"), 2)
    z = lax.axis_index("exp") // 2
    middle = (z == 1) | (z == 2)
    place = jnp.stack([core, lax.axis_index("exp")]).astype(jnp.int32)

    shape = jnp.concatenate([lengths, groups], axis=1)
    other_shape = core_swap(shape)
    far_shape = x_swap(shape)
    far_queries = x_swap(queries)

    proj_rows = gather_z(lax.dynamic_slice_in_dim(out_proj, core * HEAD, HEAD, 0))

    theirs, prefix_theirs = split_theirs(place, queries, keys, values, prefix_keys, prefix_values)
    other, prefix_other = core_swap(theirs), core_swap(prefix_theirs)

    def prefix(shape_a, shape_b, q0, q1, dtype):
        return prefix_attend(
            place, shape_a, shape_b, q0, q1, prefix_keys, prefix_values, prefix_other, dtype
        )

    tab = jnp.concatenate([expert_ids.T.astype(jnp.bfloat16), expert_gates.T], axis=0)
    tab = jnp.pad(tab, ((0, 16 - tab.shape[0]), (0, 0)))
    suffix = suffix_attend(place, shape, other_shape, queries, keys, values, other)
    unused, far_queries, far_shape = together(suffix[1], far_queries, far_shape)
    far_send = jnp.where(core == 0, far_queries[:, HEAD:], far_queries[:, :HEAD])[None]
    far_other, far_other_shape = core_swap(far_send), core_swap(far_shape)
    far = prefix(far_shape, far_other_shape, far_queries, far_other, jnp.bfloat16)
    back = (x_swap(far[0]), x_swap(far[1]))
    near = prefix(shape, other_shape, queries, other, jnp.float32)
    near_o, gain = together(near[0], norm_gain.reshape(1, -1))
    attended = merge_parts(place, [suffix, (near_o, near[1]), back], tab)
    heads = exchange_heads(attended)
    tabs = jnp.stack([part[0, 2 * BLK :, :] for part in heads])
    keep, pair, send, send_pair = project(place, heads, proj_rows)
    send_pair, tabs, other_tabs = together(send_pair, tabs, y_swap(tabs))
    pair = pair.astype(jnp.float32) + core_swap(send_pair).astype(jnp.float32)
    late = y_swap(pair.astype(jnp.bfloat16))
    stream, normed = norm_rows(keep, core_swap(send), late, residual, gain)
    pick, give = route(place, tabs, other_tabs)
    weights = (w_gate.transpose(0, 2, 1), w_up.transpose(0, 2, 1), w_down)
    here, there, weights = gather_rows(middle, normed, weights)
    picked = pick_rows(pick[:4], here) + pick_rows(pick[4:], there)
    sums = run_experts(picked, give, *weights)
    return scatter_sums(middle, stream, sums[:4], sums[4:]).astype(jnp.bfloat16)


def solution(mesh):
    in_specs = (
        P("req", "exp"),
        P("req", "exp"),
        P("req", "exp"),
        P(None, "req", "exp"),
        P(None, "req", "exp"),
        P("req", None),
        P("req", None),
        P(("req", "exp"), None),
        P("exp", None),
        P(),
        P(("req", "exp"), None),
        P(("req", "exp"), None),
        P("exp", None, None),
        P("exp", None, None),
        P("exp", None, None),
    )
    out_specs = P(("req", "exp"), None)
    blocked = mesh.shape["req"] == 4 and mesh.shape["exp"] == 8
    return jax.shard_map(
        block_device if blocked else general_device,
        mesh=mesh,
        in_specs=in_specs,
        out_specs=out_specs,
        check_vma=False,
    )
```

```python
import math

import jax
import jax.numpy as jnp
from jax import lax
from jax.experimental import pallas as pl
from jax.experimental.pallas import tpu as pltpu
from jax.sharding import PartitionSpec as P

HEAD = 128
TOPK = 4
EXPERTS = 32
G = 4
RQ = 8
ROW_TOK = 1024


NEG = -1e30


def token_layout(lengths, groups):
    req_ends = jnp.cumsum(lengths, axis=-1)
    starts = req_ends - lengths
    position = jnp.arange(ROW_TOK, dtype=jnp.int32)
    request = jnp.sum((position[None, :, None] >= req_ends[:, None, :]).astype(jnp.int32), axis=-1)
    onehot = request[:, :, None] == jnp.arange(RQ, dtype=jnp.int32)[None, None, :]
    first_tok = jnp.sum(jnp.where(onehot, starts[:, None, :], 0), axis=-1)
    tok_group = jnp.sum(jnp.where(onehot, groups[:, None, :], 0), axis=-1)
    return (request, position[None, :] - first_tok, tok_group)


def split_blocks(row_count):
    if row_count % 1024 == 0 and row_count > 1024:
        return row_count // 1024
    return 1


def pack_parts(parts):
    return jnp.concatenate([parts[0], parts[1], parts[2]], axis=1)


def unpack_parts(packed, head_count):
    columns = head_count * HEAD
    return (
        packed[:, :columns],
        packed[:, columns : columns + head_count],
        packed[:, columns + head_count :],
    )


def attend_prefix(query_rows, query_group, prefix_k, prefix_v):
    row_count, columns = query_rows.shape
    head_count = columns // HEAD
    span = prefix_k.shape[1]
    key_grid = prefix_k.reshape(G, span, head_count, HEAD)
    val_grid = prefix_v.reshape(G, span, head_count, HEAD)
    blocks = split_blocks(row_count)
    block_len = row_count // blocks
    scaling = 1.0 / math.sqrt(HEAD)

    def per_block(pieces):
        block_q, block_g = pieces
        query_grid = block_q.reshape(block_len, head_count, HEAD)
        scores = (
            jnp.einsum("qhd,gkhd->hqgk", query_grid, key_grid, preferred_element_type=jnp.float32)
            * scaling
        )
        member = block_g[:, None] == jnp.arange(G, dtype=jnp.int32)[None, :]
        scores = jnp.where(member[None, :, :, None], scores, NEG)
        maxima = jnp.max(scores, axis=(2, 3))
        exp_terms = jnp.exp(scores - maxima[:, :, None, None])
        totals = jnp.sum(exp_terms, axis=(2, 3))
        weighted = jnp.einsum(
            "hqgk,gkhd->qhd",
            exp_terms.astype(jnp.bfloat16),
            val_grid,
            preferred_element_type=jnp.float32,
        )
        return (weighted.reshape(block_len, columns), maxima.T, totals.T)

    weighted, maxima, totals = lax.map(
        per_block,
        (query_rows.reshape(blocks, block_len, columns), query_group.reshape(blocks, block_len)),
    )
    return (
        weighted.reshape(row_count, columns),
        maxima.reshape(row_count, head_count),
        totals.reshape(row_count, head_count),
    )


def attend_suffix(queries, keys, values, request, position):
    row_count, columns = queries.shape
    head_count = columns // HEAD
    blocks = split_blocks(row_count)
    block_len = row_count // blocks
    scaling = 1.0 / math.sqrt(HEAD)
    key_grid = keys.reshape(row_count, head_count, HEAD)
    val_grid = values.reshape(row_count, head_count, HEAD)

    def per_block(pieces):
        block_q, block_req, block_pos = pieces
        query_grid = block_q.reshape(block_len, head_count, HEAD)
        scores = (
            jnp.einsum("qhd,khd->hqk", query_grid, key_grid, preferred_element_type=jnp.float32)
            * scaling
        )
        allowed = (request[None, :] == block_req[:, None]) & (
            position[None, :] <= block_pos[:, None]
        )
        scores = jnp.where(allowed[None, :, :], scores, NEG)
        maxima = jnp.max(scores, axis=2)
        exp_terms = jnp.exp(scores - maxima[:, :, None])
        totals = jnp.sum(exp_terms, axis=2)
        weighted = jnp.einsum(
            "hqk,khd->qhd",
            exp_terms.astype(jnp.bfloat16),
            val_grid,
            preferred_element_type=jnp.float32,
        )
        return (weighted.reshape(block_len, columns), maxima.T, totals.T)

    weighted, maxima, totals = lax.map(
        per_block,
        (
            queries.reshape(blocks, block_len, columns),
            request.reshape(blocks, block_len),
            position.reshape(blocks, block_len),
        ),
    )
    return (
        weighted.reshape(row_count, columns),
        maxima.reshape(row_count, head_count),
        totals.reshape(row_count, head_count),
    )


def combine(former, latter):
    weighted_a, maxima_a, totals_a = former
    weighted_b, maxima_b, totals_b = latter
    row_count, head_count = maxima_a.shape
    maxima = jnp.maximum(maxima_a, maxima_b)
    factor_a = jnp.exp(maxima_a - maxima)
    factor_b = jnp.exp(maxima_b - maxima)
    weighted = (
        weighted_a.reshape(row_count, head_count, HEAD) * factor_a[:, :, None]
        + weighted_b.reshape(row_count, head_count, HEAD) * factor_b[:, :, None]
    )
    return (
        weighted.reshape(row_count, head_count * HEAD),
        maxima,
        totals_a * factor_a + totals_b * factor_b,
    )


def general_device(
    queries,
    keys,
    values,
    prefix_keys,
    prefix_values,
    lengths,
    groups,
    residual,
    out_proj,
    norm_gain,
    expert_ids,
    expert_gates,
    w_gate,
    w_up,
    w_down,
):
    row_tok, columns = queries.shape
    head_count = columns // HEAD
    tok_dev = residual.shape[0]
    request, position, tok_group = token_layout(lengths, groups)
    request, position, tok_group = (request[0], position[0], tok_group[0])
    all_groups = lax.all_gather(tok_group, "req", axis=0, tiled=True)
    partial_value = pack_parts(
        attend_prefix(
            lax.all_gather(queries, "req", axis=0, tiled=True),
            all_groups,
            prefix_keys,
            prefix_values,
        )
    )
    returned = lax.all_to_all(partial_value, "req", split_axis=0, concat_axis=0, tiled=True)
    owners = returned.shape[0] // row_tok
    back_w, back_m, back_t = unpack_parts(returned, head_count)
    all_weighted = back_w.reshape(owners, row_tok, head_count, HEAD)
    all_maxima = back_m.reshape(owners, row_tok, head_count)
    all_totals = back_t.reshape(owners, row_tok, head_count)
    maxima = jnp.max(all_maxima, axis=0)
    factor = jnp.exp(all_maxima - maxima[None])
    weighted = jnp.sum(all_weighted * factor[..., None], axis=0).reshape(row_tok, columns)
    prefix_part = (weighted, maxima, jnp.sum(all_totals * factor, axis=0))
    suffix_part = attend_suffix(queries, keys, values, request, position)
    weighted, maxima, totals = combine(prefix_part, suffix_part)
    attended = (
        (weighted.reshape(row_tok, head_count, HEAD) / totals[:, :, None])
        .reshape(row_tok, columns)
        .astype(jnp.bfloat16)
    )
    projected = lax.psum_scatter(
        jnp.dot(attended, out_proj, preferred_element_type=jnp.float32),
        "exp",
        scatter_dimension=0,
        tiled=True,
    )
    stream = residual.astype(jnp.float32) + projected
    meansq = jnp.mean(stream * stream, axis=-1, keepdims=True)
    normed = (stream * lax.rsqrt(meansq + 1e-06) * norm_gain.astype(jnp.float32)).astype(
        jnp.bfloat16
    )
    capacity = max(2, tok_dev // 4)
    flat_ids = expert_ids.reshape(-1)
    onehot = (flat_ids[:, None] == jnp.arange(EXPERTS, dtype=jnp.int32)[None, :]).astype(jnp.int32)
    slot_of = jnp.sum(onehot * (jnp.cumsum(onehot, axis=0) - 1), axis=1)
    source_rows = jnp.arange(tok_dev * TOPK, dtype=jnp.int32) // TOPK
    buffer = (
        jnp.zeros((EXPERTS, capacity, normed.shape[1]), jnp.bfloat16)
        .at[flat_ids, slot_of]
        .set(normed[source_rows])
    )
    exp_count = lax.axis_size("exp")
    exp_dev = w_gate.shape[0]
    received = lax.all_to_all(buffer, "exp", split_axis=0, concat_axis=0, tiled=True)
    slots = received.shape[1]
    grid_in = received.reshape(exp_count, exp_dev, slots, received.shape[2])
    gate_h = jnp.einsum("secd,edf->secf", grid_in, w_gate, preferred_element_type=jnp.float32)
    up_h = jnp.einsum("secd,edf->secf", grid_in, w_up, preferred_element_type=jnp.float32)
    hidden = (jax.nn.silu(gate_h) * up_h).astype(jnp.bfloat16)
    expert_out = jnp.einsum("secf,efd->secd", hidden, w_down, preferred_element_type=jnp.float32)
    returned = lax.all_to_all(
        expert_out.reshape(EXPERTS, slots, received.shape[2]),
        "exp",
        split_axis=0,
        concat_axis=0,
        tiled=True,
    )
    gathered = returned[flat_ids, slot_of] * expert_gates.reshape(-1).astype(jnp.float32)[:, None]
    mixture = jnp.sum(gathered.reshape(tok_dev, TOPK, gathered.shape[1]), axis=1)
    return (stream + mixture).astype(jnp.bfloat16)


BLK = 128
LOG2E = 1.4426950408889634
SCORE_SCALE = LOG2E / math.sqrt(HEAD)
VMEM_BIG = 28 * 1024 * 1024
VMEM_MOST = 56 * 1024 * 1024
VMEM_SMALL = 12 * 1024 * 1024


def core_swap(array):
    return lax.ppermute(array, "req", [(i, i ^ 1) for i in range(4)])


def x_swap(array):
    return lax.ppermute(array, "req", [(i, i ^ 2) for i in range(4)])


def y_swap(array):
    return lax.ppermute(array, "exp", [(i, i ^ 1) for i in range(8)])


def outer_swap(array):
    return lax.ppermute(array, "exp", [(i, i ^ 2) for i in range(8)])


def gather_z(array):
    return lax.all_gather(
        array, "exp", axis=0, axis_index_groups=[[0, 2, 4, 6], [1, 3, 5, 7]], tiled=True
    )


def middle_swap(array):
    return lax.ppermute(array, "exp", [(2, 4), (3, 5), (4, 2), (5, 3)])


def split_kernel(sc_ref, q, k, v, pk, pv, out_tokens, out_prefix, sems):
    theirs = pl.ds(pl.multiple_of((1 - sc_ref[0]) * HEAD, HEAD), HEAD)
    copies = [
        pltpu.make_async_copy(part.at[:, theirs], out_tokens.at[i], sems.at[i])
        for i, part in enumerate((q, k, v))
    ]
    for i, part in enumerate((pk, pv)):
        for g in range(G):
            copies.append(
                pltpu.make_async_copy(
                    part.at[g, :, theirs], out_prefix.at[i, g], sems.at[3 + i * G + g]
                )
            )
    for copy in copies:
        copy.start()
    for copy in copies:
        copy.wait()


def split_theirs(place, q, k, v, pk, pv):
    rows, span = q.shape[0], pk.shape[1]
    vmem = pl.BlockSpec(memory_space=pltpu.VMEM)
    return pl.pallas_call(
        split_kernel,
        in_specs=[pl.BlockSpec(memory_space=pltpu.SMEM)]
        + [pl.BlockSpec(memory_space=pl.ANY)] * 5,
        out_specs=[vmem, vmem],
        out_shape=(
            jax.ShapeDtypeStruct((3, rows, HEAD), q.dtype),
            jax.ShapeDtypeStruct((2, G, span, HEAD), q.dtype),
        ),
        scratch_shapes=[pltpu.SemaphoreType.DMA((3 + 2 * G,))],
        compiler_params=pltpu.CompilerParams(vmem_limit_bytes=VMEM_MOST),
        name="split_theirs",
    )(place, q, k, v, pk, pv)


def as_row(column):
    return jnp.transpose(jnp.broadcast_to(column, (BLK, BLK)))[0:1, :]


SUF = 256
SUB = 32
PER_ITEM = 8
ITEMS = 16


def build_work(shapes, item_group, item_block):
    per_row = ROW_TOK // SUB
    spans = []
    for r, (shape, at) in enumerate(shapes):
        start = 0
        for j in range(RQ):
            end = start + shape[at, j]
            first, last = r * per_row + start // SUB, r * per_row + (end - 1) // SUB
            spans.append((first, last, shape[at, RQ + j]))
            start = end

    def of_group(g, begin):
        at, done = begin, jnp.int32(-1)
        for first, last, group in spans:
            first = jnp.maximum(first, done + 1)
            match = group == g
            count = jnp.where(match, last - first + 1, 0)

            def put(i, carry, at=at, first=first):
                item_block[at + i] = first + i
                return carry

            lax.fori_loop(0, count, put, 0)
            at = at + count
            done = jnp.where(match, last, done)
        stop = (at + PER_ITEM - 1) // PER_ITEM * PER_ITEM

        def fill(i, carry):
            item_block[i] = item_block[begin]
            return carry

        def name(i, carry):
            item_group[i] = g
            return carry

        lax.fori_loop(at, stop, fill, 0)
        lax.fori_loop(begin // PER_ITEM, stop // PER_ITEM, name, 0)
        return stop

    return lax.fori_loop(0, G, of_group, jnp.int32(0)) // PER_ITEM


def prefix_kernel(
    sc_ref, shape_a, shape_b, q0, q1, pk, pv, other, o_ref, lse_ref,
    q_ref, ka, kb, va, vb, grp, lse, sa, sb, ta, tb, item_group, item_block, sems,
):
    tokens = q_ref.shape[0]
    span = ka.shape[1]
    shapes = ((shape_a, 0), (shape_b, 0))
    mine = pl.ds(pl.multiple_of(sc_ref[0] * HEAD, HEAD), HEAD)
    copies = [
        pltpu.make_async_copy(q0.at[:, mine], q_ref.at[:ROW_TOK, :], sems.at[0]),
        pltpu.make_async_copy(q1.at[0], q_ref.at[ROW_TOK:, :], sems.at[1]),
        pltpu.make_async_copy(pk.at[:, :, mine], ka, sems.at[2]),
        pltpu.make_async_copy(other.at[0], kb, sems.at[3]),
        pltpu.make_async_copy(pv.at[:, :, mine], va, sems.at[4]),
        pltpu.make_async_copy(other.at[1], vb, sems.at[5]),
    ]
    for copy in copies:
        copy.start()
    for r, (shape, at) in enumerate(shapes):
        token = lax.broadcasted_iota(jnp.int32, (ROW_TOK, HEAD), 0)
        group = jnp.full((ROW_TOK, HEAD), shape[at, RQ], jnp.int32)
        start = 0
        for j in range(1, RQ):
            start = start + shape[at, j - 1]
            group = jnp.where(token >= start, shape[at, RQ + j], group)
        grp[r * ROW_TOK : (r + 1) * ROW_TOK, :] = group
    count = build_work(shapes, item_group, item_block)
    for copy in copies:
        copy.wait()
    step = 512

    def held(item):
        return jnp.where(item < count, item, 0)

    def places(item):
        at = held(item) * PER_ITEM
        return [
            pl.ds(pl.multiple_of(item_block[at + i] * SUB, SUB), SUB) for i in range(PER_ITEM)
        ]

    def group_of(item):
        return item_group[held(item)]

    def lanes(x, op):
        parts = [x[:, c : c + HEAD] for c in range(0, x.shape[1], HEAD)]
        while len(parts) > 1:
            parts = [op(a, b) for a, b in zip(parts[::2], parts[1::2])]
        return parts[0]

    def score(item, s, tops):
        g = group_of(item)
        q = jnp.concatenate([q_ref[place, :] for place in places(item)], axis=0)
        for half, k in enumerate((ka, kb)):
            for c in range(0, span, step):
                x = lax.dot_general(
                    q,
                    k[g, c : c + step, :],
                    (((1,), (1,)), ((), ())),
                    preferred_element_type=jnp.float32,
                )
                s[:, half * span + c : half * span + c + step] = x
                top = lanes(x, jnp.maximum)
                tops[...] = top if half == 0 and c == 0 else jnp.maximum(tops[...], top)

    def weigh(item, s, tops):
        g = group_of(item)
        where = places(item)
        for part in range(2):
            here = slice(part * BLK, (part + 1) * BLK)
            top = jnp.max(tops[here, :], axis=1, keepdims=True)
            out = jnp.zeros((BLK, HEAD), jnp.float32)
            total = jnp.zeros((BLK, HEAD), jnp.float32)
            for half, v in enumerate((va, vb)):
                for c in range(0, span, step):
                    x = s[here, half * span + c : half * span + c + step]
                    p = jnp.exp2((x - top) * SCORE_SCALE)
                    total = total + lanes(p, jnp.add)
                    out = out + jnp.dot(
                        p.astype(jnp.bfloat16),
                        v[g, c : c + step, :],
                        preferred_element_type=jnp.float32,
                    )
            total = jnp.sum(total, axis=1, keepdims=True)
            out = out * (1.0 / total)
            here_lse = jnp.broadcast_to(top * SCORE_SCALE + jnp.log2(total), (BLK, HEAD))
            for i in range(BLK // SUB):
                place = where[part * (BLK // SUB) + i]
                sub = slice(i * SUB, (i + 1) * SUB)
                mine = grp[place, :] == g
                o_ref[place, :] = jnp.where(
                    mine, out[sub], o_ref[place, :].astype(jnp.float32)
                ).astype(o_ref.dtype)
                lse[place, :] = jnp.where(mine, here_lse[sub], lse[place, :])

    score(0, sa, ta)

    def pair(i, carry):
        score(2 * i + 1, sb, tb)
        weigh(2 * i, sa, ta)

        @pl.when(2 * i + 1 < count)
        def second():
            score(2 * i + 2, sa, ta)
            weigh(2 * i + 1, sb, tb)

        return carry

    lax.fori_loop(0, (count + 1) // 2, pair, 0)
    for b in range(tokens // BLK):
        lse_ref[b // 8, b % 8 : b % 8 + 1, :] = jnp.transpose(lse[b * BLK : (b + 1) * BLK, :])[
            0:1, :
        ]


def prefix_attend(place, shape_a, shape_b, q0, q1, pk, pv, other, out_dtype):
    rows = 2
    tokens = rows * ROW_TOK
    span = pk.shape[1]
    blocks = ROW_TOK // BLK
    smem = pl.BlockSpec(memory_space=pltpu.SMEM)
    vmem = pl.BlockSpec(memory_space=pltpu.VMEM)
    anywhere = pl.BlockSpec(memory_space=pl.ANY)
    prefix_buffer = pltpu.VMEM((G, span, HEAD), pk.dtype)
    per_token = pltpu.VMEM((tokens, HEAD), jnp.float32)
    scores = pltpu.VMEM((PER_ITEM * SUB, 2 * span), jnp.float32)
    tops = pltpu.VMEM((PER_ITEM * SUB, HEAD), jnp.float32)
    return pl.pallas_call(
        prefix_kernel,
        in_specs=[smem] * 3 + [anywhere] * 5,
        out_specs=(vmem, vmem),
        out_shape=(
            jax.ShapeDtypeStruct((tokens, HEAD), out_dtype),
            jax.ShapeDtypeStruct((rows, blocks, BLK), jnp.float32),
        ),
        scratch_shapes=[
            pltpu.VMEM((tokens, HEAD), q0.dtype),
            prefix_buffer,
            prefix_buffer,
            prefix_buffer,
            prefix_buffer,
            pltpu.VMEM((tokens, HEAD), jnp.int32),
            per_token,
            scores,
            scores,
            tops,
            tops,
            pltpu.SMEM((ITEMS,), jnp.int32),
            pltpu.SMEM((ITEMS * PER_ITEM,), jnp.int32),
            pltpu.SemaphoreType.DMA((6,)),
        ],
        compiler_params=pltpu.CompilerParams(vmem_limit_bytes=VMEM_BIG),
        cost_estimate=pl.CostEstimate(
            flops=tokens * span * HEAD * 8 * 4,
            bytes_accessed=4 * G * span * HEAD * 2,
            transcendentals=0,
        ),
        name="prefix_attend",
    )(place, shape_a, shape_b, q0, q1, pk, pv, other)


def suffix_kernel(sc_ref, shape_a, shape_b, q, k, v, other_row, o_ref, lse_ref):
    count = ROW_TOK // SUF
    rows = ((shape_a, (q, k, v)), (shape_b, [other_row.at[i] for i in range(3)]))
    for row, (shape, qkv) in enumerate(rows):
        token = lax.broadcasted_iota(jnp.int32, (ROW_TOK, 1), 0)
        first = jnp.zeros((ROW_TOK, 1), jnp.int32)
        start = 0
        for j in range(1, RQ):
            start = start + shape[0, j - 1]
            first = jnp.where(token >= start, start, first)

        def bounds(i):
            low = max(0, i * SUF - ROW_TOK // 2)
            return low, slice(i * SUF, (i + 1) * SUF), slice(low, (i + 1) * SUF)

        def score(i, qkv=qkv, first=first, token=token):
            low, here, seen = bounds(i)
            s = lax.dot_general(
                qkv[0][here, :],
                qkv[1][seen, :],
                (((1,), (1,)), ((), ())),
                preferred_element_type=jnp.float32,
            )
            other = low + lax.broadcasted_iota(jnp.int32, s.shape, 1)
            return jnp.where((other >= first[here]) & (other <= token[here]), s, NEG)

        def weigh(i, s, row=row, qkv=qkv):
            unused, here, seen = bounds(i)
            top = jnp.max(s, axis=1, keepdims=True)
            p = jnp.exp2((s - top) * SCORE_SCALE)
            total = jnp.sum(p, axis=1, keepdims=True)
            out = jnp.dot(
                p.astype(jnp.bfloat16), qkv[2][seen, :], preferred_element_type=jnp.float32
            )
            o_ref[row * ROW_TOK + i * SUF : row * ROW_TOK + (i + 1) * SUF, :] = out * (1.0 / total)
            lse = top * SCORE_SCALE + jnp.log2(total)
            for part in range(SUF // BLK):
                at = i * (SUF // BLK) + part
                lse_ref[row, at : at + 1, :] = as_row(lse[part * BLK : (part + 1) * BLK])

        held = score(0)
        for i in range(count):
            later = score(i + 1) if i + 1 < count else None
            weigh(i, held)
            held = later


def suffix_attend(place, shape_a, shape_b, q, k, v, other):
    rows, tokens = 2, q.shape[0]
    blocks = tokens // BLK
    smem = pl.BlockSpec(memory_space=pltpu.SMEM)
    mine = pl.BlockSpec((tokens, HEAD), lambda i, s: (0, s[0]))
    return pl.pallas_call(
        suffix_kernel,
        grid_spec=pltpu.PrefetchScalarGridSpec(
            num_scalar_prefetch=1,
            grid=(1,),
            in_specs=[smem, smem]
            + [mine] * 3
            + [pl.BlockSpec((3, tokens, HEAD), lambda i, s: (0, 0, 0))],
            out_specs=[
                pl.BlockSpec((rows * tokens, HEAD), lambda i, s: (0, 0)),
                pl.BlockSpec((rows, blocks, BLK), lambda i, s: (0, 0, 0)),
            ],
        ),
        out_shape=(
            jax.ShapeDtypeStruct((rows * tokens, HEAD), jnp.float32),
            jax.ShapeDtypeStruct((rows, blocks, BLK), jnp.float32),
        ),
        compiler_params=pltpu.CompilerParams(vmem_limit_bytes=VMEM_MOST),
        cost_estimate=pl.CostEstimate(
            flops=rows * tokens * tokens * HEAD * 4 * 4, bytes_accessed=1 << 20, transcendentals=0
        ),
        name="suffix_attend",
    )(place, shape_a, shape_b, q, k, v, other)


def merge_kernel(sc_ref, *refs):
    parts, tab_ref, out_ref = refs[:-2], refs[-2], refs[-1]
    block = pl.program_id(0)
    out_ref[0, 2 * BLK :, :] = tab_ref[...]
    half = len(parts) // 2
    for row in range(2):
        sources = parts[row * half : (row + 1) * half]
        lses = [
            jnp.transpose(jnp.broadcast_to(lse[0, pl.ds(block, 1), :], (BLK, BLK)))
            for lse in sources[1::2]
        ]
        top = lses[0]
        for lse in lses[1:]:
            top = jnp.maximum(top, lse)
        total, summed = 0.0, 0.0
        for lse, o in zip(lses, sources[0::2]):
            weight = jnp.exp2(lse - top)
            total = total + weight
            summed = summed + weight * o[...].astype(jnp.float32)
        out_ref[0, row * BLK : (row + 1) * BLK, :] = (summed / total).astype(out_ref.dtype)


def merge_parts(place, parts, tab):
    extra = tab.shape[0]
    blocks = ROW_TOK // BLK
    specs, operands = [], []
    for row in range(2):
        for o, lse in parts:
            operands += [o, lse]
            specs += [
                pl.BlockSpec((BLK, HEAD), lambda b, s, row=row: (row * blocks + b, 0)),
                pl.BlockSpec((1, blocks, BLK), lambda b, s, row=row: (row, 0, 0)),
            ]
    return pl.pallas_call(
        merge_kernel,
        grid_spec=pltpu.PrefetchScalarGridSpec(
            num_scalar_prefetch=1,
            grid=(blocks,),
            in_specs=specs + [pl.BlockSpec((extra, BLK), lambda b, s: (0, 0))],
            out_specs=pl.BlockSpec((1, 2 * BLK + extra, HEAD), lambda b, s: (b ^ s[1], 0, 0)),
        ),
        out_shape=jax.ShapeDtypeStruct((blocks, 2 * BLK + extra, HEAD), jnp.bfloat16),
        compiler_params=pltpu.CompilerParams(vmem_limit_bytes=VMEM_SMALL),
        name="merge_parts",
    )(place, *operands, tab)


def exchange_heads(attended):
    heads = [attended[:2]]
    for d in range(1, attended.shape[0] // 2):
        heads.append(
            lax.ppermute(
                attended[2 * d : 2 * d + 2], "exp", [(i, i ^ (2 * d)) for i in range(8)]
            )
        )
    return heads


def project_kernel(sc_ref, *refs):
    heads, source, outs, (lhs, weights, sems) = refs[:4], refs[4], refs[5:9], refs[9:]
    z_here = sc_ref[1] // 2
    tile = 512
    slices = [slice(low, low + tile) for low in range(0, weights.shape[1], tile)]
    copies = [
        pltpu.make_async_copy(source.at[:, here], weights.at[:, here], sems.at[i])
        for i, here in enumerate(slices)
    ]
    for copy in copies:
        copy.start()
    for d, part in enumerate(heads):
        columns = pl.ds(pl.multiple_of((z_here ^ d) * HEAD, HEAD), HEAD)
        for row in range(2):
            for chunk in range(2):
                to = (2 * row + chunk) * BLK
                lhs[to : to + BLK, columns] = part[chunk, row * BLK : (row + 1) * BLK, :]
    for here, copy in zip(slices, copies):
        copy.wait()
        out = jnp.dot(lhs[...], weights[:, here], preferred_element_type=jnp.float32)
        for i, out_ref in enumerate(outs):
            out_ref[:, here] = out[i * BLK : (i + 1) * BLK].astype(out_ref.dtype)


def project(place, heads, weights):
    depth, width = weights.shape
    smem = pl.BlockSpec(memory_space=pltpu.SMEM)
    vmem = pl.BlockSpec(memory_space=pltpu.VMEM)
    return pl.pallas_call(
        project_kernel,
        in_specs=[smem] + [vmem] * 4 + [pl.BlockSpec(memory_space=pl.ANY)],
        out_specs=[vmem] * 4,
        out_shape=[
            jax.ShapeDtypeStruct((BLK, width), dtype)
            for dtype in (jnp.float32, jnp.bfloat16, jnp.bfloat16, jnp.bfloat16)
        ],
        scratch_shapes=[
            pltpu.VMEM((4 * BLK, depth), jnp.bfloat16),
            pltpu.VMEM((depth, width), weights.dtype),
            pltpu.SemaphoreType.DMA((width // 512,)),
        ],
        compiler_params=pltpu.CompilerParams(vmem_limit_bytes=VMEM_MOST),
        name="project",
    )(place, *heads, weights)


def norm_kernel(keep, got, late, residual, gain, stream_ref, normed_ref):
    stream = residual[...].astype(jnp.float32) + (
        keep[...] + got[...].astype(jnp.float32) + late[...].astype(jnp.float32)
    )
    meansq = jnp.mean(stream * stream, axis=-1, keepdims=True)
    stream_ref[...] = stream
    normed = stream * lax.rsqrt(meansq + 1e-06) * gain[...].astype(jnp.float32)
    normed_ref[...] = normed.astype(normed_ref.dtype)


def norm_rows(keep, got, late, residual, gain):
    return pl.pallas_call(
        norm_kernel,
        out_shape=(
            jax.ShapeDtypeStruct(keep.shape, jnp.float32),
            jax.ShapeDtypeStruct(keep.shape, jnp.bfloat16),
        ),
        compiler_params=pltpu.CompilerParams(vmem_limit_bytes=VMEM_SMALL),
        name="norm_rows",
    )(keep, got, late, residual, gain)


EXP_DEV = 4
VMEM_STAGE = 2 * 1024 * 1024
EXPERT_VMEM = 8 * 1024 * 1024
SLOTS = 32
SLOTS_XOR = (0, 2, 4, 6, 1, 3, 5, 7)


def route_kernel(sc_ref, *refs):
    own, other, pick_ref, give_ref = refs
    before = (
        lax.broadcasted_iota(jnp.int32, (BLK, BLK), 0)
        < lax.broadcasted_iota(jnp.int32, (BLK, BLK), 1)
    ).astype(jnp.bfloat16)
    place = lax.broadcasted_iota(jnp.int32, (SLOTS, BLK), 0).astype(jnp.float32)
    place_here = sc_ref[1]
    for slot, offset in enumerate(SLOTS_XOR):
        tab = (own if offset % 2 == 0 else other)[offset // 2].astype(jnp.float32)
        ids, gates = tab[:TOPK], tab[TOPK : 2 * TOPK]
        chosen, weights = [], []
        for j in range(EXP_DEV):
            match = ids == (place_here * EXP_DEV + j).astype(jnp.float32)
            chosen.append(jnp.sum(match.astype(jnp.float32), axis=0, keepdims=True))
            weights.append(jnp.sum(jnp.where(match, gates, 0.0), axis=0, keepdims=True))
        held = jnp.concatenate(chosen + chosen, axis=0)
        places = jnp.dot(held.astype(jnp.bfloat16), before, preferred_element_type=jnp.float32)
        places = jnp.where(held > 0.5, places, -1.0)
        hits = [place == places[j : j + 1] for j in range(EXP_DEV)]
        pick_ref[slot] = jnp.concatenate(
            [hit.astype(jnp.float32) for hit in hits], axis=0
        ).astype(jnp.bfloat16)
        spread = jnp.concatenate(
            [jnp.where(hit, weight, 0.0) for hit, weight in zip(hits, weights)], axis=0
        )
        give_ref[slot] = jnp.transpose(spread).astype(jnp.bfloat16)


def route(place, own, other):
    shape = jax.ShapeDtypeStruct((8, BLK, EXP_DEV * SLOTS), jnp.bfloat16)
    vmem = pl.BlockSpec(memory_space=pltpu.VMEM)
    return pl.pallas_call(
        route_kernel,
        in_specs=[pl.BlockSpec(memory_space=pltpu.SMEM), vmem, vmem],
        out_specs=[vmem, vmem],
        out_shape=(shape, shape),
        compiler_params=pltpu.CompilerParams(vmem_limit_bytes=VMEM_SMALL),
        name="route",
    )(place, own, other)


def stage_kernel(source, held, sems):
    copies = [pltpu.make_async_copy(source.at[i], held.at[i], sems.at[i]) for i in range(EXP_DEV)]
    for copy in copies:
        copy.start()
    for copy in copies:
        copy.wait()


def stage(weights):
    return pl.pallas_call(
        stage_kernel,
        in_specs=[pl.BlockSpec(memory_space=pltpu.HBM)],
        out_specs=pl.BlockSpec(memory_space=pltpu.VMEM),
        out_shape=jax.ShapeDtypeStruct(weights.shape, weights.dtype),
        scratch_shapes=[pltpu.SemaphoreType.DMA((EXP_DEV,))],
        compiler_params=pltpu.CompilerParams(vmem_limit_bytes=VMEM_STAGE),
        cost_estimate=pl.CostEstimate(flops=0, bytes_accessed=2 * weights.size, transcendentals=0),
        name="stage",
    )(weights)


def experts_kernel(*refs):
    picked = refs[:8]
    give_ref, wg, wu, wd = refs[8:12]
    outs, rows_out = refs[12:-1], refs[-1]
    contract = (((1,), (1,)), ((), ()))

    def run(expert, carry):
        here = pl.ds(pl.multiple_of(expert * SLOTS, SLOTS), SLOTS)
        rows = jnp.concatenate([part[here, :] for part in picked], axis=0)
        gate_h = lax.dot_general(wg[expert], rows, contract, preferred_element_type=jnp.float32)
        up_h = lax.dot_general(wu[expert], rows, contract, preferred_element_type=jnp.float32)
        hidden = jnp.transpose((gate_h / (1.0 + jnp.exp(-gate_h)) * up_h).astype(jnp.bfloat16))
        out = jnp.dot(hidden, wd[expert], preferred_element_type=jnp.float32).astype(jnp.bfloat16)
        for slot in range(8):
            rows_out[slot, here, :] = out[slot * SLOTS : (slot + 1) * SLOTS]
        return carry

    lax.fori_loop(0, EXP_DEV, run, 0)
    for slot in range(8):
        out = jnp.dot(give_ref[slot], rows_out[slot], preferred_element_type=jnp.float32)
        out = out.astype(jnp.bfloat16)
        if slot < 7:
            outs[slot][...] = out
        else:
            outs[7][...] = out[: BLK // 2]
            outs[8][...] = out[BLK // 2 :]


def run_experts(picked, give, w_gate, w_up, w_down):
    width = picked[0].shape[1]
    heights = [BLK] * 7 + [BLK // 2] * 2
    vmem = pl.BlockSpec(memory_space=pltpu.VMEM)
    return pl.pallas_call(
        experts_kernel,
        in_specs=[vmem] * 12,
        out_specs=[vmem] * 9,
        out_shape=[jax.ShapeDtypeStruct((n, width), jnp.bfloat16) for n in heights],
        scratch_shapes=[pltpu.VMEM((8, EXP_DEV * SLOTS, width), jnp.bfloat16)],
        compiler_params=pltpu.CompilerParams(vmem_limit_bytes=EXPERT_VMEM),
        name="experts",
    )(*picked, give, w_gate, w_up, w_down)


def together(*arrays):
    return lax.optimization_barrier(arrays)


def gather_rows(middle, own, weights):
    half = own.shape[0] // 2
    own, *weights = together(own, *weights)
    outer0, middle0, there0, gate = together(
        outer_swap(own), middle_swap(own), y_swap(own), stage(weights[0])
    )
    outer1, middle1, there1, down = together(
        outer_swap(middle0), middle_swap(outer0), y_swap(outer0), stage(weights[2])
    )
    second = jnp.where(middle, middle1, outer1)
    outer2, there2 = together(outer_swap(middle1), y_swap(second))
    third = jnp.where(middle, middle0, outer2)
    there3, late_outer, late_middle = together(
        y_swap(third[:half]), outer_swap(there2[half:]), middle_swap(there0[half:])
    )
    late = jnp.where(middle, late_middle, late_outer)
    return [own, outer0, second, third], [there0, there1, there2, there3, late], (gate, weights[1], down)


def pick_rows(pick, parts):
    picked = [
        jnp.dot(matrix, part, preferred_element_type=jnp.float32)
        for matrix, part in zip(pick, parts[:4])
        if part.shape[0] == matrix.shape[1]
    ]
    if len(parts) == 5:
        half = parts[3].shape[0]
        picked.append(
            jnp.dot(pick[3][:, :half], parts[3], preferred_element_type=jnp.float32)
            + jnp.dot(pick[3][:, half:], parts[4], preferred_element_type=jnp.float32)
        )
    return [part.astype(jnp.bfloat16) for part in picked]


def scatter_sums(middle, stream, own, there):
    half = there[3].shape[0]

    def plus(*parts):
        total = parts[0].astype(jnp.float32)
        for part in parts[1:]:
            total = total + part.astype(jnp.float32)
        return total

    def plus16(*parts):
        return plus(*parts).astype(jnp.bfloat16)

    def in_middle(array):
        return jnp.where(middle, array.astype(jnp.float32), 0.0)

    got, late_outer, late_middle = together(
        y_swap(there[3]), outer_swap(there[4]), middle_swap(there[4])
    )
    sum3 = jnp.concatenate([plus16(own[3][:half], got), own[3][half:]], axis=0)
    there2 = jnp.concatenate(
        [there[2][:half], plus16(there[2][half:], in_middle(late_outer))], axis=0
    )
    there0 = jnp.concatenate(
        [there[0][:half], plus16(there[0][half:], in_middle(late_middle))], axis=0
    )
    got, outer = together(y_swap(there2), outer_swap(sum3))
    sum2 = plus16(own[2], got, in_middle(outer))
    got, outer, across = together(y_swap(there[1]), outer_swap(sum2), middle_swap(sum2))
    sum1 = plus16(own[1], got, in_middle(across))
    sum3 = plus16(sum3, in_middle(outer))
    got, outer, across = together(y_swap(there0), outer_swap(sum1), middle_swap(sum3))
    return plus(stream, own[0], got, outer, in_middle(across))


def block_device(
    queries,
    keys,
    values,
    prefix_keys,
    prefix_values,
    lengths,
    groups,
    residual,
    out_proj,
    norm_gain,
    expert_ids,
    expert_gates,
    w_gate,
    w_up,
    w_down,
):
    core = lax.rem(lax.axis_index("req"), 2)
    z = lax.axis_index("exp") // 2
    middle = (z == 1) | (z == 2)
    place = jnp.stack([core, lax.axis_index("exp")]).astype(jnp.int32)

    shape = jnp.concatenate([lengths, groups], axis=1)
    other_shape = core_swap(shape)
    far_shape = x_swap(shape)
    far_queries = x_swap(queries)

    proj_rows = gather_z(lax.dynamic_slice_in_dim(out_proj, core * HEAD, HEAD, 0))

    theirs, prefix_theirs = split_theirs(place, queries, keys, values, prefix_keys, prefix_values)
    other, prefix_other = core_swap(theirs), core_swap(prefix_theirs)

    def prefix(shape_a, shape_b, q0, q1, dtype):
        return prefix_attend(
            place, shape_a, shape_b, q0, q1, prefix_keys, prefix_values, prefix_other, dtype
        )

    tab = jnp.concatenate([expert_ids.T.astype(jnp.bfloat16), expert_gates.T], axis=0)
    tab = jnp.pad(tab, ((0, 16 - tab.shape[0]), (0, 0)))
    suffix = suffix_attend(place, shape, other_shape, queries, keys, values, other)
    unused, far_queries, far_shape = together(suffix[1], far_queries, far_shape)
    far_send = jnp.where(core == 0, far_queries[:, HEAD:], far_queries[:, :HEAD])[None]
    far_other, far_other_shape = core_swap(far_send), core_swap(far_shape)
    far = prefix(far_shape, far_other_shape, far_queries, far_other, jnp.bfloat16)
    back = (x_swap(far[0]), x_swap(far[1]))
    near = prefix(shape, other_shape, queries, other, jnp.float32)
    near_o, gain = together(near[0], norm_gain.reshape(1, -1))
    attended = merge_parts(place, [suffix, (near_o, near[1]), back], tab)
    heads = exchange_heads(attended)
    tabs = jnp.stack([part[0, 2 * BLK :, :] for part in heads])
    keep, pair, send, send_pair = project(place, heads, proj_rows)
    send_pair, tabs, other_tabs = together(send_pair, tabs, y_swap(tabs))
    pair = pair.astype(jnp.float32) + core_swap(send_pair).astype(jnp.float32)
    late = y_swap(pair.astype(jnp.bfloat16))
    stream, normed = norm_rows(keep, core_swap(send), late, residual, gain)
    pick, give = route(place, tabs, other_tabs)
    weights = (w_gate.transpose(0, 2, 1), w_up.transpose(0, 2, 1), w_down)
    here, there, weights = gather_rows(middle, normed, weights)
    picked = pick_rows(pick[:4], here) + pick_rows(pick[4:], there)
    sums = run_experts(picked, give, *weights)
    return scatter_sums(middle, stream, sums[:4], sums[4:]).astype(jnp.bfloat16)


def solution(mesh):
    in_specs = (
        P("req", "exp"),
        P("req", "exp"),
        P("req", "exp"),
        P(None, "req", "exp"),
        P(None, "req", "exp"),
        P("req", None),
        P("req", None),
        P(("req", "exp"), None),
        P("exp", None),
        P(),
        P(("req", "exp"), None),
        P(("req", "exp"), None),
        P("exp", None, None),
        P("exp", None, None),
        P("exp", None, None),
    )
    out_specs = P(("req", "exp"), None)
    blocked = mesh.shape["req"] == 4 and mesh.shape["exp"] == 8
    return jax.shard_map(
        block_device if blocked else general_device,
        mesh=mesh,
        in_specs=in_specs,
        out_specs=out_specs,
        check_vma=False,
    )
```
